32 devices in a mesh: fsdp: 16 (over z, y, core), sp: 2 (over x).
Axes of the slice: x: 2, y: 2, z: 4, core: 2. Of those that a mesh axis runs over, the one named last changes fastest.
Arguments:
- hidden_in: bfloat16 [32, 2048, 512], P('fsdp', 'sp'), may hold values from -6 to 6
- token_stream: bfloat16 [32, 2048, 512], P('fsdp', 'sp'), may hold values from -6 to 6
- encoder_out: bfloat16 [32, 1024, 512], P('fsdp', 'sp'), may hold values from -6 to 6
- out_grad: bfloat16 [32, 2048, 512], P('fsdp', 'sp'), may hold values from -6 to 6
- doc_ids: int32 [32, 8], P('fsdp'), may hold values from 0 to 3, never falling along the last dimension, each value on 1 to 4 neighbouring positions
- key_order: int32 [32, 8, 256], P('fsdp'), may hold values from 0 to 255, each once within a row
- context_size: int32 [32, 8, 256], P('fsdp'), may hold values from 2 to 256
- self_query: bfloat16 [512, 512], P('fsdp'), may hold values from -0.375 to 0.375
- self_key: bfloat16 [512, 512], P('fsdp'), may hold values from -0.25 to 0.25
- self_value: bfloat16 [512, 512], P('fsdp'), may hold values from -0.25 to 0.25
- self_output: bfloat16 [512, 512], P('fsdp'), may hold values from -1.5 to 1.5
- cross_query: bfloat16 [512, 512], P('fsdp'), may hold values from -0.375 to 0.375
- cross_key: bfloat16 [512, 512], P('fsdp'), may hold values from -0.25 to 0.25
- cross_value: bfloat16 [512, 512], P('fsdp'), may hold values from -0.25 to 0.25
- cross_output: bfloat16 [512, 512], P('fsdp'), may hold values from -3 to 3
- inner_weight: bfloat16 [512, 2048], P('fsdp'), may hold values from -0.25 to 0.25
- inner_bias: bfloat16 [2048], P('fsdp'), may hold values from -3 to 3
- outer_weight: bfloat16 [2048, 512], P('fsdp'), may hold values from -0.1875 to 0.1875
- outer_bias: bfloat16 [512], P('fsdp'), may hold values from -3 to 3
- first_gain: bfloat16 [512], P('fsdp'), may hold values from 0.25 to 1.75
- first_shift: bfloat16 [512], P('fsdp'), may hold values from -2 to 2
- second_gain: bfloat16 [512], P('fsdp'), may hold values from 0.25 to 1.75
- second_shift: bfloat16 [512], P('fsdp'), may hold values from -2 to 2
- third_gain: bfloat16 [512], P('fsdp'), may hold values from 0.25 to 1.75
- third_shift: bfloat16 [512], P('fsdp'), may hold values from -2 to 2
Outputs:
- layer_out: float32 [32, 2048, 512], P('fsdp', 'sp')
- hidden_grad: float32 [32, 2048, 512], P('fsdp', 'sp')
- token_grad: float32 [32, 2048, 512], P('fsdp', 'sp')
- encoder_grad: float32 [32, 1024, 512], P('fsdp', 'sp')
- self_query_grad: float32 [512, 512], P('fsdp')
- self_key_grad: float32 [512, 512], P('fsdp')
- self_value_grad: float32 [512, 512], P('fsdp')
- self_output_grad: float32 [512, 512], P('fsdp')
- cross_query_grad: float32 [512, 512], P('fsdp')
- cross_key_grad: float32 [512, 512], P('fsdp')
- cross_value_grad: float32 [512, 512], P('fsdp')
- cross_output_grad: float32 [512, 512], P('fsdp')
- inner_weight_grad: float32 [512, 2048], P('fsdp')
- inner_bias_grad: float32 [2048], P('fsdp')
- outer_weight_grad: float32 [2048, 512], P('fsdp')
- outer_bias_grad: float32 [512], P('fsdp')
- first_gain_grad: float32 [512], P('fsdp')
- first_shift_grad: float32 [512], P('fsdp')
- second_gain_grad: float32 [512], P('fsdp')
- second_shift_grad: float32 [512], P('fsdp')
- third_gain_grad: float32 [512], P('fsdp')
- third_shift_grad: float32 [512], P('fsdp')
The draws below stay inside these ranges and needn't reach their ends.
Inputs may be any that keep to these rules, and one draw needn't show every extreme that they name: `doc_ids`: block ids never fall along a sequence's 8 blocks; tokens may attend only within blocks of equal id. `key_order`: the 256 entries of each block are a permutation.
All inputs are finite; a program needn't handle non-finite values.
Results may differ from the reference program's by a relative error of at most 0.03.
Values may be sent and summed in bfloat16 or wider, within the bound.
No kernel may reach another device: no remote copies, remote signals or barrier semaphores. Data moves between devices by JAX's collectives and lax.ppermute only.
A program may use at most 256 MiB of HBM per device.

```python
import math
import jax
import jax.numpy as jnp
import numpy as np
from jax import lax

D = 512
H = 8
HD = 64
FF = 2048
BLK = 256
LEN = 2048
ENC = 1024
SEQS = 32
NBLK = 8


def plant(drawn, rng, low, high):
    place = [jax.random.randint(jax.random.fold_in(rng, axis), (), 0, length) for axis, length in enumerate(drawn.shape)]
    widest = drawn.shape.index(max(drawn.shape))
    next_to = place[:widest] + [(place[widest] + 1) % drawn.shape[widest]] + place[widest + 1:]
    return drawn.at[tuple(place)].set(low).at[tuple(next_to)].set(high)


def steps_of(own_key, extent, cuts, low, top_value):
    def one(position, blocks):
        draws = jax.random.uniform(jax.random.fold_in(jax.random.fold_in(own_key, 6), position), (blocks,), jnp.float32, low / len(cuts), top_value / len(cuts))
        return jnp.repeat(jnp.exp(draws), extent[position] // blocks).reshape((-1,) + (1,) * (len(extent) - position - 1))

    level = one(*cuts[0])
    for cut in cuts[1:]:
        level = level * one(*cut)
    return level


def profile(number_of, total, most, slope):
    loads = [(1 << 20) // math.isqrt(standing ** slope) + 1 for standing in range(2, number_of + 1)]
    spare, counts = total - most - (number_of - 1), [1] * (number_of - 1)
    while spare > 0:
        free = [i for i in range(number_of - 1) if counts[i] < most]
        mass, remaining = sum([loads[i] for i in free]), spare
        for i in free:
            more = min(most - counts[i], max(1, remaining * loads[i] // mass), spare)
            counts[i] = counts[i] + more
            spare = spare - more
    return np.array([most] + counts)


def ragged(own_key, count, total, most, skew):
    if count == 2:
        one = jax.random.randint(own_key, (), max(1, total - most), min(most, total - 1) + 1)
        return jnp.stack([one, total - one])
    tallies = jnp.asarray(profile(count, total, most, skew), jnp.int32)
    couples = (count - 1) // 2
    giver, receiver = tallies[1:1 + 2 * couples:2], tallies[2:2 + 2 * couples:2]
    margin = jnp.minimum(giver - 1, most - receiver)
    moved = jax.random.randint(jax.random.fold_in(own_key, 1), (couples,), 0, 1 << 20) % (margin + 1)
    tallies = tallies.at[1:1 + 2 * couples:2].set(giver - moved).at[2:2 + 2 * couples:2].set(receiver + moved)
    return tallies[jax.random.permutation(jax.random.fold_in(own_key, 2), count)]


def normal_values(stream_key, extent, deviation, most, cuts=(), held_as=jnp.bfloat16):
    values = jax.random.normal(stream_key, extent, jnp.float32) * deviation
    if len(cuts) > 0:
        values = steps_of(stream_key, extent, cuts, -0.22, 0.18) * values
    return jnp.clip(values, min=-most, max=most).astype(held_as)


def setup_inputs(seed: int = 0) -> dict:
    key_of = jax.random.split(jax.random.key(seed), 26)
    hidden_in = normal_values(key_of[0], (SEQS, LEN, D), 1.0, 6.0, ((0, 16), (1, 2)))
    token_stream = normal_values(key_of[1], (SEQS, LEN, D), 1.0, 6.0, ((0, 16), (1, 2)))
    encoder_out = normal_values(key_of[2], (SEQS, ENC, D), 1.0, 6.0, ((0, 16), (1, 2)))
    out_grad = normal_values(key_of[3], (SEQS, LEN, D), 1.0, 6.0, ((0, 16), (1, 2)))
    doc_ids = jax.vmap(lambda own: jnp.searchsorted(jnp.cumsum(ragged(own, max(1, LEN // BLK // 2), NBLK, max(2, LEN // BLK // 2), 0)), jnp.arange(NBLK), side="right"))(jax.random.split(key_of[4], SEQS)).reshape((SEQS, NBLK)).astype(jnp.int32)
    key_order = jax.vmap(lambda own: jax.random.permutation(own, BLK))(jax.random.split(key_of[5], SEQS * NBLK)).reshape((SEQS, NBLK, BLK)).astype(jnp.int32)
    context_size = plant(jax.random.randint(key_of[6], (SEQS, NBLK, BLK), 2, BLK + 1), jax.random.fold_in(key_of[6], 1), 2, BLK).astype(jnp.int32)
    self_query = normal_values(key_of[7], (D, D), (D // 2) ** -0.5, 0.375, ((0, 16),))
    self_key = normal_values(key_of[8], (D, D), D ** -0.5, 0.25, ((0, 16),))
    self_value = normal_values(key_of[9], (D, D), D ** -0.5, 0.25, ((0, 16),))
    self_output = normal_values(key_of[10], (D, D), (8 * D // BLK) ** -0.5, 1.5, ((0, 16),))
    cross_query = normal_values(key_of[11], (D, D), (D // 2) ** -0.5, 0.375, ((0, 16),))
    cross_key = normal_values(key_of[12], (D, D), D ** -0.5, 0.25, ((0, 16),))
    cross_value = normal_values(key_of[13], (D, D), D ** -0.5, 0.25, ((0, 16),))
    cross_output = normal_values(key_of[14], (D, D), (8 * D // ENC) ** -0.5, 3.0, ((0, 16),))
    inner_weight = normal_values(key_of[15], (D, FF), D ** -0.5, 0.25, ((0, 16),))
    inner_bias = normal_values(key_of[16], (FF,), 0.5, 3.0, ((0, 16),))
    outer_weight = normal_values(key_of[17], (FF, D), (FF // 2) ** -0.5, 0.1875, ((0, 16),))
    outer_bias = normal_values(key_of[18], (D,), 0.5, 3.0, ((0, 16),))
    first_gain = jnp.clip(1.0 + 0.15 * jax.random.normal(key_of[19], (D,), jnp.float32), 0.25, 1.75).astype(jnp.bfloat16)
    first_shift = normal_values(key_of[20], (D,), 0.3, 2.0, ((0, 16),))
    second_gain = jnp.clip(1.0 + 0.15 * jax.random.normal(key_of[21], (D,), jnp.float32), 0.25, 1.75).astype(jnp.bfloat16)
    second_shift = normal_values(key_of[22], (D,), 0.3, 2.0, ((0, 16),))
    third_gain = jnp.clip(1.0 + 0.15 * jax.random.normal(key_of[23], (D,), jnp.float32), 0.25, 1.75).astype(jnp.bfloat16)
    third_shift = normal_values(key_of[24], (D,), 0.3, 2.0, ((0, 16),))
    return {"hidden_in": hidden_in, "token_stream": token_stream, "encoder_out": encoder_out, "out_grad": out_grad, "doc_ids": doc_ids, "key_order": key_order, "context_size": context_size, "self_query": self_query, "self_key": self_key, "self_value": self_value, "self_output": self_output, "cross_query": cross_query, "cross_key": cross_key, "cross_value": cross_value, "cross_output": cross_output, "inner_weight": inner_weight, "inner_bias": inner_bias, "outer_weight": outer_weight, "outer_bias": outer_bias, "first_gain": first_gain, "first_shift": first_shift, "second_gain": second_gain, "second_shift": second_shift, "third_gain": third_gain, "third_shift": third_shift}


epsilon = 1e-05
mask_fill = -1000000000.0

@jax.custom_vjp
def low(v):
    return lax.optimization_barrier(v.astype(jnp.bfloat16)).astype(jnp.float32)

@jax.custom_vjp
def low_back(v):
    return v

def low_keep(v):
    return (low(v), None)

def low_pass(kept, grad):
    return (grad,)

def back_keep(v):
    return (v, None)

def back_low(kept, grad):
    return (low(grad),)
low.defvjp(low_keep, low_pass)
low_back.defvjp(back_keep, back_low)

def matmul_high(left, right):
    return jnp.dot(left, right, precision=lax.Precision.HIGHEST, preferred_element_type=jnp.float32)

def smooth_gate(values):
    return jax.nn.gelu(values, approximate=False)

def normalize(rows, gain, shift):
    center = rows - lax.optimization_barrier(jnp.mean(rows, axis=-1, keepdims=True))
    scaled = center * lax.rsqrt(lax.optimization_barrier(jnp.mean(center * center, axis=-1, keepdims=True)) + epsilon)
    return scaled * gain + shift

def attend(queries, key_rows, value_rows, key_doc, key_order, query_doc, query_reach, positions, masked):
    key_count = key_rows.shape[0]
    block_rows = min(512, LEN)
    block_count = LEN // block_rows
    query_parts = queries.reshape(block_count, block_rows, H, HD)
    key_heads = key_rows.reshape(key_count, H, HD)
    value_heads = value_rows.reshape(key_count, H, HD)
    key_places = jnp.arange(key_count, dtype=jnp.int32)
    score_scale = 1.0 / math.sqrt(HD)

    def one_block(pieces):
        query_part, doc_part, reach_part, place_part = pieces
        scores = low_back(jnp.einsum('qhd,khd->hqk', query_part, key_heads, precision=lax.Precision.HIGHEST, preferred_element_type=jnp.float32) * score_scale)
        if masked:
            allowed = (doc_part[:, None] == key_doc[None, :]) & (key_order[None, :] < reach_part[:, None]) & (place_part[:, None] != key_places[None, :])
            scores = jnp.where(allowed[None], scores, mask_fill)
        row_max = lax.optimization_barrier(jnp.max(scores, axis=-1, keepdims=True))
        exp_terms = jnp.exp(scores - row_max)
        if masked:
            exp_terms = jnp.where(allowed[None], exp_terms, 0.0)
        prob_rows = exp_terms / lax.optimization_barrier(jnp.sum(exp_terms, axis=-1, keepdims=True))
        mixed_rows = jnp.einsum('hqk,khd->qhd', low(prob_rows), value_heads, precision=lax.Precision.HIGHEST, preferred_element_type=jnp.float32)
        return mixed_rows.reshape(block_rows, D)
    mixed_blocks = lax.map(jax.checkpoint(one_block), (query_parts, query_doc.reshape(block_count, block_rows), query_reach.reshape(block_count, block_rows), positions.reshape(block_count, block_rows)))
    return mixed_blocks.reshape(LEN, D)

def layer(stream, tokens, encoded, params, token_doc, token_order, token_reach, positions):
    w_query, w_key, w_value, w_output, c_query, c_key, c_value, c_output, w_inner, b_inner, w_outer, b_outer, g_first, s_first, g_second, s_second, g_third, s_third = params
    queries = low(low_back(matmul_high(stream, w_query)))
    key_rows = low(low_back(matmul_high(tokens, w_key)))
    value_rows = low(low_back(matmul_high(tokens, w_value)))
    mixed_rows = low(low_back(attend(queries, key_rows, value_rows, token_doc, token_order, token_doc, token_reach, positions, True)))
    first_sum = stream + low_back(matmul_high(mixed_rows, w_output))
    normed = normalize(first_sum, g_first, s_first)
    cross_queries = low(low_back(matmul_high(low(normed), c_query)))
    cross_keys = low(low_back(matmul_high(encoded, c_key)))
    cross_values = low(low_back(matmul_high(encoded, c_value)))
    cross_rows = low(low_back(attend(cross_queries, cross_keys, cross_values, token_doc, token_order, token_doc, token_reach, positions, False)))
    second_sum = normed + low_back(matmul_high(cross_rows, c_output))
    middle = normalize(second_sum, g_second, s_second)
    inner_pre = low_back(matmul_high(low(middle), w_inner) + b_inner)
    active = low(smooth_gate(inner_pre))
    third_sum = middle + low_back(matmul_high(active, w_outer) + b_outer)
    return normalize(third_sum, g_third, s_third)

def reference(hidden_in, token_stream, encoder_out, out_grad, doc_ids, key_order, context_size, self_query, self_key, self_value, self_output, cross_query, cross_key, cross_value, cross_output, inner_weight, inner_bias, outer_weight, outer_bias, first_gain, first_shift, second_gain, second_shift, third_gain, third_shift):
    weights = tuple((array_item.astype(jnp.float32) for array_item in (self_query, self_key, self_value, self_output, cross_query, cross_key, cross_value, cross_output, inner_weight, inner_bias, outer_weight, outer_bias, first_gain, first_shift, second_gain, second_shift, third_gain, third_shift)))
    positions = jnp.arange(LEN, dtype=jnp.int32)

    def one_sequence(running, pieces):
        stream, tokens, encoded, cotangent, doc_row, order_row, reach_row = pieces
        token_doc = jnp.repeat(doc_row, BLK)
        token_order = order_row.reshape(LEN)
        token_reach = reach_row.reshape(LEN)

        def forward(stream_full, tokens_full, encoded_full, params):
            return layer(stream_full, tokens_full, encoded_full, params, token_doc, token_order, token_reach, positions)
        result, pullback = jax.vjp(forward, stream.astype(jnp.float32), tokens.astype(jnp.float32), encoded.astype(jnp.float32), weights)
        stream_grad, tokens_grad, encoded_grad, param_grads = pullback(cotangent.astype(jnp.float32))
        running = jax.tree.map(jnp.add, running, param_grads)
        return (running, (result, stream_grad, tokens_grad, encoded_grad))
    zero_grads = tuple((jnp.zeros(array_item.shape, jnp.float32) for array_item in weights))
    totals, (out_rows, hidden_grad, token_grad, encoder_grad) = lax.scan(one_sequence, zero_grads, (hidden_in, token_stream, encoder_out, out_grad, doc_ids, key_order, context_size))
    return (out_rows, hidden_grad, token_grad, encoder_grad, totals[0], totals[1], totals[2], totals[3], totals[4], totals[5], totals[6], totals[7], totals[8], totals[9], totals[10], totals[11], totals[12], totals[13], totals[14], totals[15], totals[16], totals[17])
```

```python
import functools
import math

import jax
import jax.numpy as jnp
from jax import lax
from jax.experimental import pallas as pl
from jax.experimental.pallas import tpu as pltpu
from jax.sharding import PartitionSpec as P

HD = 64
BLK = 256
WINDOW = 4
EPS = 1e-05
MASKED = -1e30
LOG2E = 1.4426950408889634
LN2 = 0.6931471805599453
SAFE = 60.0
F32 = jnp.float32
BF16 = jnp.bfloat16
NN = (((1,), (0,)), ((), ()))
NT = (((1,), (1,)), ((), ()))
TN = (((0,), (0,)), ((), ()))
VMEM_LIMIT = 62 * 2**20


def dot(left, right, form=NN):
    return lax.dot_general(left, right, form, preferred_element_type=F32)


def norm(rows):
    center = rows - jnp.mean(rows, axis=0, keepdims=True)
    inverse = lax.rsqrt(jnp.mean(center * center, axis=0, keepdims=True) + EPS)
    return center * inverse, inverse


def norm_back(scaled, inverse, gain, upstream):
    through = upstream * gain
    return inverse * (
        through
        - jnp.mean(through, axis=0, keepdims=True)
        - scaled * jnp.mean(through * scaled, axis=0, keepdims=True)
    )


def fold(values):
    total = values[:, :128]
    for start in range(128, values.shape[1], 128):
        total = total + values[:, start : start + 128]
    return total


def gelu_pair(x):
    size = jnp.abs(x)
    t = 1.0 / (1.0 + (0.3275911 / math.sqrt(2.0)) * size)
    bell = jnp.exp2((-0.5 * LOG2E) * (x * x))
    series = t * (
        0.127414796 + t * (-0.142248368 + t * (0.7107068705 + t * (-0.7265760135 + t * 0.5307027145)))
    )
    tail = series * bell
    phi = jnp.where(x >= 0.0, 1.0 - tail, tail)
    return x * phi, phi + x * bell * (1.0 / math.sqrt(2.0 * math.pi))


def weight(pack, first, rows):
    return jnp.concatenate([pack[f, first : first + rows, :] for f in range(pack.shape[0])], axis=0)


def unpack_weight(pack, first, rows, plain=None, turned=None):
    whole = weight(pack, first, rows)
    if plain is not None:
        plain[...] = whole
    if turned is not None:
        turned[...] = whole.T


def attend(count, exact, keys, values, off, query, probs, mixed, inverse, bias):
    head_count = query.shape[0] // HD

    def scores(hs, j):
        part = dot(keys[hs, pl.ds(off + j * BLK, BLK)], query[hs, :], TN)
        if bias is not None:
            part = part + bias[j * BLK : (j + 1) * BLK, :]
        return part

    def first(h, hs):
        total = None
        if exact:
            parts = [scores(hs, j) for j in range(count)]
            top = jnp.max(parts[0], axis=0, keepdims=True)
            for part in parts[1:]:
                top = jnp.maximum(top, jnp.max(part, axis=0, keepdims=True))
        for j in range(count):
            terms = jnp.exp2(parts[j] - top if exact else scores(hs, j))
            partial = jnp.sum(terms.reshape(BLK // 8, 8, BLK), axis=0)
            total = partial if total is None else total + partial
            probs[h, j * BLK : (j + 1) * BLK, :] = terms.astype(BF16)
        return total

    def second(h, hs, total):
        sums = dot(values[hs, pl.ds(off, count * BLK)], probs[h, : count * BLK, :])
        scale = 1.0 / jnp.sum(total, axis=0, keepdims=True)
        mixed[hs, :] = (sums * scale).astype(BF16)
        inverse[pl.ds(h, 1), :] = scale

    if exact:

        def one(h, carry):
            hs = pl.ds(pl.multiple_of(h * HD, HD), HD)
            second(h, hs, first(h, hs))
            return carry

        lax.fori_loop(0, head_count, one, 0)
        return
    waiting = None
    for h in range(head_count):
        total = first(h, slice(h * HD, (h + 1) * HD))
        if h > 0:
            second(h - 1, slice((h - 1) * HD, h * HD), waiting)
        waiting = total
    second(head_count - 1, slice((head_count - 1) * HD, head_count * HD), waiting)


def attend_back(
    count, keys, values, off, query, grad, inner, probs, kept, query_grad, key_grad, value_grad
):
    head_count = query.shape[0] // HD

    def first(h):
        hs = slice(h * HD, (h + 1) * HD)
        for j in range(count):
            us = slice(j * BLK, (j + 1) * BLK)
            prob_grad = dot(values[hs, pl.ds(off + j * BLK, BLK)], grad[hs, :], TN)
            kept[h, us, :] = (probs[h, us, :].astype(F32) * (prob_grad - inner[h : h + 1, :])).astype(BF16)

    def second(h):
        hs = slice(h * HD, (h + 1) * HD)
        us = slice(0, count * BLK)
        window = pl.ds(off, count * BLK)
        query_grad[hs, :] = (dot(keys[hs, window], kept[h, us, :]) * (1.0 / math.sqrt(HD))).astype(BF16)
        key_grad[hs, window] += dot(query[hs, :], kept[h, us, :], NT)
        value_grad[hs, window] += dot(grad[hs, :], probs[h, us, :], NT)

    first(0)
    for h in range(1, head_count):
        first(h)
        second(h - 1)
    second(head_count - 1)


def scale_grad(mixed_grad, mixed, inverse, grad, inner):
    for h in range(mixed.shape[0] // HD):
        hs = slice(h * HD, (h + 1) * HD)
        scaled = mixed_grad[hs, :] * inverse[h : h + 1, :]
        grad[hs, :] = scaled.astype(BF16)
        inner[h : h + 1, :] = jnp.sum(scaled * mixed[hs, :].astype(F32), axis=0, keepdims=True)


def head_norms(rows, head_count):
    found = []
    for h in range(head_count):
        part = rows[h * HD : (h + 1) * HD, :].astype(F32)
        found.append(jnp.max(jnp.sum(part * part, axis=0, keepdims=True), axis=1, keepdims=True))
    return found


def safe_scores(query, key_norms):
    head_count = query.shape[0] // HD
    worst = None
    for h, found in enumerate(head_norms(query[...], head_count)):
        product = found * key_norms[h : h + 1, 0:1]
        worst = product if worst is None else jnp.maximum(worst, product)
    return jnp.max(worst) < SAFE * SAFE


def store_key_norms(key_norms, keys):
    head_count = keys.shape[0] // HD
    for h, found in enumerate(head_norms(keys[...], head_count)):
        key_norms[h : h + 1, :] = jnp.broadcast_to(found, (1, key_norms.shape[1]))


def doc_span(docs, seq, block, block_count):
    mine = docs[seq, block]
    low = jnp.int32(0)
    count = jnp.int32(0)
    for b in range(block_count):
        low = low + jnp.where(docs[seq, b] < mine, 1, 0).astype(jnp.int32)
        count = count + jnp.where(docs[seq, b] == mine, 1, 0).astype(jnp.int32)
    return low, count


def self_forward_kernel(
    shard, docs, place, hidden, own_tokens, far_tokens, order, reach, pack, cols,
    keys, values, query, mixed, probs, inverse, scaled1, inverse1,
    q_turned, k_turned, v_turned, o_turned, bias, key_norms,
):
    seq, step = pl.program_id(0), pl.program_id(1)
    steps = pl.num_programs(1)
    rows = shard
    local = own_tokens.shape[1]
    parts = far_tokens.shape[0] + 1
    block_count = order.shape[1]
    me = place[0]

    @pl.when((seq == 0) & (step == 0))
    def _():
        for which, turned in enumerate((q_turned, k_turned, v_turned, o_turned)):
            unpack_weight(pack, which * rows, rows, None, turned)

    @pl.when(step == 0)
    def _():
        for part in range(parts):
            tokens = own_tokens[0] if part == 0 else far_tokens[part - 1, 0]
            owner = lax.rem(me + part, parts)
            at = pl.ds(pl.multiple_of(owner * local, BLK), local)
            turned = tokens.T
            keys[0, :, at] = dot(k_turned[...], turned).astype(BF16)
            values[0, :, at] = dot(v_turned[...], turned).astype(BF16)
        store_key_norms(key_norms, keys.at[0])

    block = me * steps + step
    low, count = doc_span(docs, seq, block, block_count)
    turned = hidden[0].T
    query[0] = (dot(q_turned[...], turned) * (LOG2E / math.sqrt(HD))).astype(BF16)

    order_turned = order[0].astype(F32).T
    lanes = lax.broadcasted_iota(jnp.int32, order_turned.shape, 1)
    reach_row = reach[0, pl.ds(block, 1), :].astype(F32)
    differ = lax.broadcasted_iota(jnp.int32, (BLK, BLK), 0) != lax.broadcasted_iota(
        jnp.int32, (BLK, BLK), 1
    )
    for j in range(WINDOW):
        at = low + j
        column = jnp.sum(jnp.where(lanes == at, order_turned, 0.0), axis=1, keepdims=True)
        seen = (column < reach_row) & (differ | (at != block))
        bias[j * BLK : (j + 1) * BLK, :] = jnp.where(seen, 0.0, MASKED)

    safe = safe_scores(query.at[0], key_norms)
    off = pl.multiple_of(low * BLK, BLK)
    for size in range(1, WINDOW + 1):
        for exact in (False, True):

            @pl.when((count == size) & (safe != exact))
            def _(size=size, exact=exact):
                attend(
                    size, exact, keys.at[0], values.at[0], off, query.at[0], probs.at[0, 0],
                    mixed.at[0], inverse.at[0, 0], bias,
                )

    first_sum = turned.astype(F32) + dot(o_turned[...], mixed[0])
    center, inv = norm(first_sum)
    scaled1[0] = center
    inverse1[0, 0] = jnp.broadcast_to(inv, inverse1.shape[2:])


def cross_ffn_kernel(
    shard, inner_shard, scaled1, own_enc, far_enc, out_grad, pack, big_pack, cols, inner_bias,
    keys, values, query, mixed, probs, inverse, second_grad, layer_out, inner_out, outer_out, col_grads,
    bias_grad,
    q_turned, k_turned, v_turned, o_turned, inner, inner_turned, outer, outer_turned, inner_acc, outer_acc,
    sums, bias_sum, key_norms, slope,
):
    seq, step = pl.program_id(0), pl.program_id(1)
    rows = shard
    first_step = (seq == 0) & (step == 0)
    last_step = (seq == pl.num_programs(0) - 1) & (step == pl.num_programs(1) - 1)
    local = own_enc.shape[1]
    parts = far_enc.shape[0] + 1
    width = inner.shape[0]
    owners = pack.shape[0]
    chunks = inner.shape[1] // width
    outer_rows = outer.shape[0] // owners

    @pl.when(first_step)
    def _():
        for which, turned in enumerate((q_turned, k_turned, v_turned, o_turned)):
            unpack_weight(pack, which * rows, rows, None, turned)
        for c in range(chunks):
            cs = slice(c * width, (c + 1) * width)
            whole = weight(big_pack, c * rows, rows)
            inner[:, cs] = whole
            inner_turned[cs, :] = whole.T
        for f in range(owners):
            fs = slice(f * outer_rows, (f + 1) * outer_rows)
            outer[fs, :] = big_pack[f, chunks * rows : chunks * rows + outer_rows, :]
        for c in range(chunks):
            cs = slice(c * width, (c + 1) * width)
            outer_turned[:, cs] = outer[cs, :].T
        inner_acc[...] = jnp.zeros_like(inner_acc)
        outer_acc[...] = jnp.zeros_like(outer_acc)
        sums[...] = jnp.zeros_like(sums)
        bias_sum[...] = jnp.zeros_like(bias_sum)

    @pl.when(step == 0)
    def _():
        for part in range(parts):
            turned = (own_enc[0] if part == 0 else far_enc[part - 1, 0]).T
            at = slice(part * local, (part + 1) * local)
            keys[0, :, at] = dot(k_turned[...], turned).astype(BF16)
            values[0, :, at] = dot(v_turned[...], turned).astype(BF16)
        store_key_norms(key_norms, keys.at[0])

    normed = scaled1[0] * cols[:, 0:1] + cols[:, 1:2]
    query[0] = (dot(q_turned[...], normed.astype(BF16)) * (LOG2E / math.sqrt(HD))).astype(BF16)
    safe = safe_scores(query.at[0], key_norms)
    for exact in (False, True):

        @pl.when(safe != exact)
        def _(exact=exact):
            attend(
                parts * local // BLK, exact, keys.at[0], values.at[0], 0, query.at[0], probs.at[0, 0],
                mixed.at[0], inverse.at[0, 0], None,
            )

    second_sum = normed + dot(o_turned[...], mixed[0])
    scaled2, inverse2 = norm(second_sum)
    gain2 = cols[:, 2:3]
    middle = scaled2 * gain2 + cols[:, 3:4]
    middle_low = middle.astype(BF16)
    pre = dot(inner_turned[...], middle_low) + inner_bias[...]
    active, pull = gelu_pair(pre)
    active = active.astype(BF16)
    slope[...] = pull.astype(BF16)
    third_sum = middle + dot(outer_turned[...], active) + cols[:, 6:7]
    scaled3, inverse3 = norm(third_sum)
    gain3 = cols[:, 4:5]
    layer_out[0] = (scaled3 * gain3 + cols[:, 5:6]).T
    upstream = out_grad[0].T.astype(F32)
    third_grad = norm_back(scaled3, inverse3, gain3, upstream)
    sums[2] += fold(upstream * scaled3)
    sums[3] += fold(upstream)
    outer_low = third_grad.astype(BF16)
    sums[4] += fold(outer_low.astype(F32))
    outer_acc[...] += dot(active, outer_low, NT)
    inner_low = (dot(outer[...], outer_low) * slope[...].astype(F32)).astype(BF16)
    bias_sum[...] += fold(inner_low.astype(F32))
    inner_acc[...] += dot(middle_low, inner_low, NT)
    middle_grad = third_grad + dot(inner[...], inner_low)
    sums[0] += fold(middle_grad * scaled2)
    sums[1] += fold(middle_grad)
    second_grad[0] = norm_back(scaled2, inverse2, gain2, middle_grad)

    @pl.when(last_step)
    def _():
        for f in range(owners):
            for c in range(chunks):
                inner_out[f, c * rows : (c + 1) * rows, :] = inner_acc[
                    f * rows : (f + 1) * rows, c * width : (c + 1) * width
                ].astype(BF16)
            outer_out[f] = outer_acc[f * outer_rows : (f + 1) * outer_rows, :].astype(BF16)
        for which in range(5):
            col_grads[:, which : which + 1] = jnp.sum(sums[which], axis=1, keepdims=True)
        bias_grad[...] = jnp.sum(bias_sum[...], axis=1, keepdims=True)


def pack_grad(out, first, rows, acc):
    for f in range(out.shape[0]):
        out[f, first : first + rows, :] = acc[f * rows : (f + 1) * rows, :].astype(BF16)


def cross_back_kernel(
    shard, second_grad, scaled1, inverse1, own_enc, far_enc, keys, values, query, mixed, probs, inverse,
    self_mixed, pack, self_pack, cols,
    first_grad, self_mixed_grad, own_part, far_part, grads, col_grads,
    q_plain, k_plain, v_plain, o_plain, so_plain, accs, sums, key_acc, value_acc, kept, grad, inner, query_grad,
):
    seq, step = pl.program_id(0), pl.program_id(1)
    rows = shard
    first_step = (seq == 0) & (step == 0)
    last_step = (seq == pl.num_programs(0) - 1) & (step == pl.num_programs(1) - 1)
    local = own_enc.shape[1]
    parts = far_enc.shape[0] + 1

    @pl.when(first_step)
    def _():
        for which, plain in enumerate((q_plain, k_plain, v_plain, o_plain)):
            unpack_weight(pack, which * rows, rows, plain, None)
        unpack_weight(self_pack, 3 * rows, rows, so_plain, None)
        accs[...] = jnp.zeros_like(accs)
        sums[...] = jnp.zeros_like(sums)

    @pl.when(step == 0)
    def _():
        key_acc[...] = jnp.zeros_like(key_acc)
        value_acc[...] = jnp.zeros_like(value_acc)

    cross_low = second_grad[0].astype(BF16)
    scale_grad(dot(o_plain[...], cross_low), mixed.at[0], inverse.at[0, 0], grad, inner)
    accs[3] += dot(mixed[0], cross_low, NT)
    attend_back(
        parts * local // BLK, keys.at[0], values.at[0], 0, query.at[0], grad, inner, probs.at[0, 0],
        kept, query_grad, key_acc, value_acc,
    )
    scaled = scaled1[0]
    gain = cols[:, 0:1]
    normed_low = (scaled * gain + cols[:, 1:2]).astype(BF16)
    accs[0] += dot(normed_low, query_grad[...], NT)
    normed_grad = second_grad[0] + dot(q_plain[...], query_grad[...])
    sums[0] += fold(normed_grad * scaled)
    sums[1] += fold(normed_grad)
    through = norm_back(scaled, inverse1[0, 0, 0:1, :], gain, normed_grad)
    first_grad[0] = through
    self_low = through.astype(BF16)
    accs[4] += dot(self_mixed[0], self_low, NT)
    self_mixed_grad[0] = dot(so_plain[...], self_low).astype(BF16)

    @pl.when(step == pl.num_programs(1) - 1)
    def _():
        for part in range(parts):
            at = slice(part * local, (part + 1) * local)
            key_low = (key_acc[:, at] * LN2).astype(BF16)
            value_low = value_acc[:, at].astype(BF16)
            turned = (own_enc[0] if part == 0 else far_enc[part - 1, 0]).T
            accs[1] += dot(turned, key_low, NT)
            accs[2] += dot(turned, value_low, NT)
            whole = (dot(k_plain[...], key_low) + dot(v_plain[...], value_low)).T
            if part == 0:
                own_part[0] = whole
            else:
                far_part[part - 1, 0] = whole.astype(BF16)

    @pl.when(last_step)
    def _():
        for which in range(5):
            pack_grad(grads, which * rows, rows, accs.at[which])
        for which in range(2):
            col_grads[:, which : which + 1] = jnp.sum(sums[which], axis=1, keepdims=True)


def self_back_kernel(
    shard, docs, place, hidden, first_grad, own_tokens, far_tokens, keys, values, query, mixed, probs, inverse,
    mixed_grad, pack,
    hidden_grad, own_part, far_part, grads,
    q_plain, k_plain, v_plain, accs, key_acc, value_acc, kept, grad, inner, query_grad,
):
    seq, step = pl.program_id(0), pl.program_id(1)
    steps = pl.num_programs(1)
    rows = shard
    first_step = (seq == 0) & (step == 0)
    last_step = (seq == pl.num_programs(0) - 1) & (step == steps - 1)
    local = own_tokens.shape[1]
    parts = far_tokens.shape[0] + 1
    me = place[0]
    block_count = parts * steps

    @pl.when(first_step)
    def _():
        for which, plain in enumerate((q_plain, k_plain, v_plain)):
            unpack_weight(pack, which * rows, rows, plain, None)
        accs[...] = jnp.zeros_like(accs)

    @pl.when(step == 0)
    def _():
        key_acc[...] = jnp.zeros_like(key_acc)
        value_acc[...] = jnp.zeros_like(value_acc)

    low, count = doc_span(docs, seq, me * steps + step, block_count)
    off = pl.multiple_of(low * BLK, BLK)
    scale_grad(mixed_grad[0].astype(F32), mixed.at[0], inverse.at[0, 0], grad, inner)
    for size in range(1, WINDOW + 1):

        @pl.when(count == size)
        def _(size=size):
            attend_back(
                size, keys.at[0], values.at[0], off, query.at[0], grad, inner, probs.at[0, 0],
                kept, query_grad, key_acc, value_acc,
            )

    accs[0] += dot(hidden[0].T, query_grad[...], NT)
    hidden_grad[0] = (first_grad[0] + dot(q_plain[...], query_grad[...])).T

    @pl.when(step == steps - 1)
    def _():
        for part in range(parts):
            owner = lax.rem(me + part, parts)
            at = pl.ds(pl.multiple_of(owner * local, BLK), local)
            key_low = (key_acc[:, at] * LN2).astype(BF16)
            value_low = value_acc[:, at].astype(BF16)
            turned = (own_tokens[0] if part == 0 else far_tokens[part - 1, 0]).T
            accs[1] += dot(turned, key_low, NT)
            accs[2] += dot(turned, value_low, NT)
            whole = (dot(k_plain[...], key_low) + dot(v_plain[...], value_low)).T
            if part == 0:
                own_part[0] = whole
            else:
                far_part[part - 1, 0] = whole.astype(BF16)

    @pl.when(last_step)
    def _():
        for which in range(3):
            pack_grad(grads, which * rows, rows, accs.at[which])


def whole_spec():
    return pl.BlockSpec(memory_space=pltpu.VMEM)


def call(body, grid, scalars, in_specs, out_specs, out_shape, scratch, flops, args):
    return pl.pallas_call(
        body,
        grid_spec=pltpu.PrefetchScalarGridSpec(
            num_scalar_prefetch=scalars,
            grid=grid,
            in_specs=in_specs,
            out_specs=out_specs,
            scratch_shapes=scratch,
        ),
        out_shape=[jax.ShapeDtypeStruct(shape, kind) for shape, kind in out_shape],
        compiler_params=pltpu.CompilerParams(vmem_limit_bytes=VMEM_LIMIT),
        cost_estimate=pl.CostEstimate(flops=flops, bytes_accessed=2**25, transcendentals=0),
    )(*args)


def shift(array, axis, by, size):
    return lax.ppermute(array, axis, [((i + by) % size, i) for i in range(size)])


def others(array, size):
    return jnp.stack([shift(array, "sp", r, size) for r in range(1, size)])


def gather(parts):
    packed = jnp.concatenate(parts, axis=0)
    return lax.all_gather(packed, "fsdp", axis=0, tiled=False)


def on_device(sp, fsdp, *arrays):
    (
        hidden_in, token_stream, encoder_out, out_grad, doc_ids, key_order, context_size,
        self_query, self_key, self_value, self_output, cross_query, cross_key, cross_value, cross_output,
        inner_weight, inner_bias, outer_weight, outer_bias, first_gain, first_shift, second_gain,
        second_shift, third_gain, third_shift,
    ) = arrays
    seqs, local, width = hidden_in.shape
    enc_local = encoder_out.shape[1]
    shard, hidden_width = inner_weight.shape
    outer_rows = outer_weight.shape[0]
    chunks = hidden_width // width
    steps = local // BLK
    heads = width // HD
    length = local * sp
    enc_len = enc_local * sp
    block_count = key_order.shape[1]

    vectors = (inner_bias, first_gain, first_shift, second_gain, second_shift, third_gain, third_shift, outer_bias)
    flat = jnp.concatenate(vectors)
    tray = 16
    flat = jnp.pad(flat, (0, tray * width - flat.shape[0])).reshape(tray, width)
    self_pack = gather((self_query, self_key, self_value, self_output, flat))
    cross_pack = gather((cross_query, cross_key, cross_value, cross_output))
    big_pack = gather(tuple(jnp.split(inner_weight, chunks, axis=1)) + (outer_weight,))
    spread = self_pack[:, 4 * shard, :].astype(F32)
    bias_rows = inner_bias.shape[0]
    inner_bias_col = spread[:, :bias_rows].reshape(-1, 1)
    cols = (
        spread[:, bias_rows : bias_rows + 7 * shard]
        .reshape(fsdp, 7, shard)
        .transpose(0, 2, 1)
        .reshape(width, 7)
    )
    cols = jnp.pad(cols, ((0, 0), (0, 1)))

    far_tokens = others(token_stream, sp)
    far_enc = others(encoder_out, sp)
    place = lax.axis_index("sp").astype(jnp.int32).reshape(1)

    grid = (seqs, steps)
    whole = whole_spec()
    turned_spec = pl.BlockSpec((1, width, BLK), lambda s, i, *_: (s, 0, i))
    plain_spec = pl.BlockSpec((1, BLK, width), lambda s, i, *_: (s, i, 0))
    per_seq = lambda shape: pl.BlockSpec((1,) + shape, lambda s, i, *_: (s, 0, 0))
    far_seq = lambda rows: pl.BlockSpec((sp - 1, 1, rows, width), lambda s, i, *_: (0, s, 0, 0))
    rows_spec = pl.BlockSpec((1, 1, 8, BLK), lambda s, i, *_: (s, i, 0, 0))
    probs_spec = lambda keys: pl.BlockSpec((1, 1, heads, keys, BLK), lambda s, i, *_: (s, i, 0, 0, 0))
    turned_shape = (seqs, width, local)
    rows_shape = (seqs, steps, 8, BLK)
    square = pltpu.VMEM((width, width), BF16)
    rows_count = seqs * local
    window = WINDOW * BLK

    keys, values, query, mixed, probs, inverse, scaled1, inverse1 = call(
        functools.partial(self_forward_kernel, shard),
        grid, 2,
        [
            plain_spec, per_seq((local, width)), far_seq(local), per_seq((block_count, BLK)),
            per_seq((block_count, BLK)), whole, whole,
        ],
        [
            per_seq((width, length)), per_seq((width, length)), turned_spec, turned_spec, probs_spec(window),
            rows_spec, turned_spec, rows_spec,
        ],
        [
            ((seqs, width, length), BF16), ((seqs, width, length), BF16), (turned_shape, BF16),
            (turned_shape, BF16), ((seqs, steps, heads, window, BLK), BF16), (rows_shape, F32),
            (turned_shape, F32), (rows_shape, F32),
        ],
        [square] * 4 + [pltpu.VMEM((window, BLK), F32), pltpu.VMEM((heads, 128), F32)],
        rows_count * width * width * 12,
        (doc_ids, place, hidden_in, token_stream, far_tokens, key_order, context_size, self_pack, cols),
    )

    big = lambda a, b, kind: pltpu.VMEM((a, b), kind)
    (
        cross_keys, cross_values, cross_q, cross_mixed, cross_probs, cross_inverse, second_grad, layer_out,
        inner_grad, outer_grad, late_cols, bias_grad,
    ) = call(
        functools.partial(cross_ffn_kernel, shard, 0),
        grid, 0,
        [
            turned_spec, per_seq((enc_local, width)), far_seq(enc_local), plain_spec, whole, whole, whole, whole,
        ],
        [
            per_seq((width, enc_len)), per_seq((width, enc_len)), turned_spec, turned_spec, probs_spec(enc_len),
            rows_spec, turned_spec, plain_spec, whole, whole, whole, whole,
        ],
        [
            ((seqs, width, enc_len), BF16), ((seqs, width, enc_len), BF16), (turned_shape, BF16),
            (turned_shape, BF16), ((seqs, steps, heads, enc_len, BLK), BF16), (rows_shape, F32),
            (turned_shape, F32), ((seqs, local, width), F32), ((fsdp, chunks * shard, width), BF16),
            ((fsdp, outer_rows, width), BF16), ((width, 8), F32), ((hidden_width, 1), F32),
        ],
        [square] * 4
        + [
            big(width, hidden_width, BF16), big(hidden_width, width, BF16), big(hidden_width, width, BF16),
            big(width, hidden_width, BF16), big(width, hidden_width, F32), big(hidden_width, width, F32),
            pltpu.VMEM((5, width, 128), F32), big(hidden_width, 128, F32), big(heads, 128, F32),
            big(hidden_width, BLK, BF16),
        ],
        rows_count * width * width * 60,
        (scaled1, encoder_out, far_enc, out_grad, cross_pack, big_pack, cols, inner_bias_col),
    )

    attention_scratch = lambda keys_len, kept_len: [
        big(width, keys_len, F32), big(width, keys_len, F32), pltpu.VMEM((heads, kept_len, BLK), BF16),
        big(width, BLK, BF16), big(heads, BLK, F32), big(width, BLK, BF16),
    ]
    first_grad, mixed_grad, own_enc_part, far_enc_part, cross_grads, early_cols = call(
        functools.partial(cross_back_kernel, shard),
        grid, 0,
        [
            turned_spec, turned_spec, rows_spec, per_seq((enc_local, width)), far_seq(enc_local),
            per_seq((width, enc_len)), per_seq((width, enc_len)), turned_spec, turned_spec, probs_spec(enc_len),
            rows_spec, turned_spec, whole, whole, whole,
        ],
        [
            turned_spec, turned_spec, per_seq((enc_local, width)), far_seq(enc_local), whole, whole,
        ],
        [
            (turned_shape, F32), (turned_shape, BF16), ((seqs, enc_local, width), F32),
            ((sp - 1, seqs, enc_local, width), BF16), ((fsdp, 5 * shard, width), BF16), ((width, 8), F32),
        ],
        [square] * 5
        + [pltpu.VMEM((5, width, width), F32), pltpu.VMEM((2, width, 128), F32)]
        + attention_scratch(enc_len, enc_len),
        rows_count * width * width * 30,
        (
            second_grad, scaled1, inverse1, encoder_out, far_enc, cross_keys, cross_values, cross_q, cross_mixed,
            cross_probs, cross_inverse, mixed, cross_pack, self_pack, cols,
        ),
    )

    hidden_grad, own_part, far_part, self_grads = call(
        functools.partial(self_back_kernel, shard),
        grid, 2,
        [
            plain_spec, turned_spec, per_seq((local, width)), far_seq(local), per_seq((width, length)),
            per_seq((width, length)), turned_spec, turned_spec, probs_spec(window), rows_spec, turned_spec, whole,
        ],
        [plain_spec, per_seq((local, width)), far_seq(local), whole],
        [
            ((seqs, local, width), F32), ((seqs, local, width), F32), ((sp - 1, seqs, local, width), BF16),
            ((fsdp, 3 * shard, width), BF16),
        ],
        [square] * 3 + [pltpu.VMEM((3, width, width), F32)] + attention_scratch(length, window),
        rows_count * width * width * 30,
        (
            doc_ids, place, hidden_in, first_grad, token_stream, far_tokens, keys, values, query, mixed, probs,
            inverse, mixed_grad, self_pack,
        ),
    )

    def settle(own, far):
        for r in range(1, sp):
            own = own + shift(far[r - 1], "sp", -r, sp).astype(F32)
        return own

    token_grad = settle(own_part, far_part)
    encoder_grad = settle(own_enc_part, far_enc_part)

    def reduce(grads):
        mine = lax.psum_scatter(grads, "fsdp", scatter_dimension=0, tiled=True)[0]
        total = mine.astype(F32)
        for r in range(1, sp):
            total = total + shift(mine, "sp", r, sp).astype(F32)
        return total

    inner_total = reduce(inner_grad)
    inner_total = jnp.concatenate([inner_total[c * shard : (c + 1) * shard] for c in range(chunks)], axis=1)
    outer_total = reduce(outer_grad)
    cross_total = reduce(cross_grads)
    col_grads = jnp.concatenate([early_cols[:, :2], late_cols[:, :5]], axis=1)
    small = jnp.concatenate(
        [
            bias_grad.reshape(fsdp, bias_rows),
            col_grads.reshape(fsdp, shard, 7).transpose(0, 2, 1).reshape(fsdp, 7 * shard),
        ],
        axis=1,
    ).astype(BF16)
    small = jnp.pad(small, ((0, 0), (0, tray * width - small.shape[1]))).reshape(fsdp, tray, width)
    self_total = reduce(jnp.concatenate([self_grads, small], axis=1))
    flat = self_total[3 * shard :].reshape(-1)
    cut = lambda total, k: total[k * shard : (k + 1) * shard]
    vec = lambda k: flat[bias_rows + k * shard : bias_rows + (k + 1) * shard]
    return (
        layer_out, hidden_grad, token_grad, encoder_grad,
        cut(self_total, 0), cut(self_total, 1), cut(self_total, 2), cut(cross_total, 4),
        cut(cross_total, 0), cut(cross_total, 1), cut(cross_total, 2), cut(cross_total, 3),
        inner_total, flat[:bias_rows], outer_total, vec(6), vec(0), vec(1), vec(2), vec(3), vec(4), vec(5),
    )


def solution(mesh):
    tokens, table, vector = P("fsdp", "sp", None), P("fsdp", None), P("fsdp")
    order = P("fsdp", None, None)
    return jax.shard_map(
        functools.partial(on_device, mesh.shape["sp"], mesh.shape["fsdp"]),
        mesh=mesh,
        in_specs=(tokens,) * 4
        + (table, order, order)
        + (table,) * 9
        + (vector, table)
        + (vector,) * 7,
        out_specs=(tokens,) * 4 + (table,) * 9 + (vector, table) + (vector,) * 7,
        check_vma=False,
    )
```

```python
import functools
import math

import jax
import jax.numpy as jnp
from jax import lax
from jax.experimental import pallas as pl
from jax.experimental.pallas import tpu as pltpu
from jax.sharding import PartitionSpec as P

HD = 64
BLK = 256
WINDOW = 4
EPS = 1e-05
MASKED = -1e30
LOG2E = 1.4426950408889634
LN2 = 0.6931471805599453
SAFE = 60.0
F32 = jnp.float32
BF16 = jnp.bfloat16
NN = (((1,), (0,)), ((), ()))
NT = (((1,), (1,)), ((), ()))
TN = (((0,), (0,)), ((), ()))
VMEM_LIMIT = 62 * 2**20


def dot(left, right, form=NN):
    return lax.dot_general(left, right, form, preferred_element_type=F32)


def norm(rows):
    center = rows - jnp.mean(rows, axis=0, keepdims=True)
    inverse = lax.rsqrt(jnp.mean(center * center, axis=0, keepdims=True) + EPS)
    return center * inverse, inverse


def norm_back(scaled, inverse, gain, upstream):
    through = upstream * gain
    return inverse * (
        through
        - jnp.mean(through, axis=0, keepdims=True)
        - scaled * jnp.mean(through * scaled, axis=0, keepdims=True)
    )


def fold(values):
    total = values[:, :128]
    for start in range(128, values.shape[1], 128):
        total = total + values[:, start : start + 128]
    return total


def gelu_pair(x):
    size = jnp.abs(x)
    t = 1.0 / (1.0 + (0.3275911 / math.sqrt(2.0)) * size)
    bell = jnp.exp2((-0.5 * LOG2E) * (x * x))
    series = t * (
        0.127414796 + t * (-0.142248368 + t * (0.7107068705 + t * (-0.7265760135 + t * 0.5307027145)))
    )
    tail = series * bell
    phi = jnp.where(x >= 0.0, 1.0 - tail, tail)
    return x * phi, phi + x * bell * (1.0 / math.sqrt(2.0 * math.pi))


def owner_of(spot, m, d, depth):
    z = lax.rem(spot[1] + d, depth)
    return (z * 2 + jnp.bitwise_xor(spot[2], m // 2)) * 2 + jnp.bitwise_xor(spot[3], m % 2)


def unpack(packs, spot, first, rows, plain):
    for m, pack in enumerate(packs):
        depth = pack.shape[0]
        for d in range(depth):
            at = pl.ds(pl.multiple_of(owner_of(spot, m, d, depth) * rows, rows), rows)
            plain[at, :] = pack[d, first : first + rows, :]


def send_grad(outs, spot, first, rows, acc, masks=(0, 1, 2, 3)):
    depth = outs[0].shape[0]
    for out, m in zip(outs, masks):
        for d in range(depth):
            at = pl.ds(pl.multiple_of(owner_of(spot, m, d, depth) * rows, rows), rows)
            out[d, first : first + rows, :] = acc[at, :].astype(BF16)


def attend(count, exact, keys, values, off, query, probs, mixed, inverse, bias):
    head_count = query.shape[0] // HD

    def scores(hs, j):
        part = dot(keys[hs, pl.ds(off + j * BLK, BLK)], query[hs, :], TN)
        if bias is not None:
            part = part + bias[j * BLK : (j + 1) * BLK, :]
        return part

    def first(h, hs):
        total = None
        if exact:
            parts = [scores(hs, j) for j in range(count)]
            top = jnp.max(parts[0], axis=0, keepdims=True)
            for part in parts[1:]:
                top = jnp.maximum(top, jnp.max(part, axis=0, keepdims=True))
        for j in range(count):
            terms = jnp.exp2(parts[j] - top if exact else scores(hs, j))
            partial = jnp.sum(terms.reshape(BLK // 8, 8, BLK), axis=0)
            total = partial if total is None else total + partial
            probs[h, j * BLK : (j + 1) * BLK, :] = terms.astype(BF16)
        return total

    def second(h, hs, total):
        sums = dot(values[hs, pl.ds(off, count * BLK)], probs[h, : count * BLK, :])
        scale = 1.0 / jnp.sum(total, axis=0, keepdims=True)
        mixed[hs, :] = (sums * scale).astype(BF16)
        inverse[pl.ds(h, 1), :] = scale

    if exact:

        def one(h, carry):
            hs = pl.ds(pl.multiple_of(h * HD, HD), HD)
            second(h, hs, first(h, hs))
            return carry

        lax.fori_loop(0, head_count, one, 0)
        return
    waiting = None
    for h in range(head_count):
        total = first(h, slice(h * HD, (h + 1) * HD))
        if h > 0:
            second(h - 1, slice((h - 1) * HD, h * HD), waiting)
        waiting = total
    second(head_count - 1, slice((head_count - 1) * HD, head_count * HD), waiting)


def attend_back(
    count, keys, values, off, query, grad, inner, probs, kept, query_grad, key_grad, value_grad
):
    head_count = query.shape[0] // HD

    def first(h):
        hs = slice(h * HD, (h + 1) * HD)
        for j in range(count):
            us = slice(j * BLK, (j + 1) * BLK)
            prob_grad = dot(values[hs, pl.ds(off + j * BLK, BLK)], grad[hs, :], TN)
            kept[h, us, :] = (probs[h, us, :].astype(F32) * (prob_grad - inner[h : h + 1, :])).astype(BF16)

    def second(h):
        hs = slice(h * HD, (h + 1) * HD)
        us = slice(0, count * BLK)
        window = pl.ds(off, count * BLK)
        query_grad[hs, :] = (dot(keys[hs, window], kept[h, us, :]) * (1.0 / math.sqrt(HD))).astype(BF16)
        key_grad[hs, window] += dot(query[hs, :], kept[h, us, :], NT)
        value_grad[hs, window] += dot(grad[hs, :], probs[h, us, :], NT)

    first(0)
    for h in range(1, head_count):
        first(h)
        second(h - 1)
    second(head_count - 1)


def scale_grad(mixed_grad, mixed, inverse, grad, inner):
    for h in range(mixed.shape[0] // HD):
        hs = slice(h * HD, (h + 1) * HD)
        scaled = mixed_grad[hs, :] * inverse[h : h + 1, :]
        grad[hs, :] = scaled.astype(BF16)
        inner[h : h + 1, :] = jnp.sum(scaled * mixed[hs, :].astype(F32), axis=0, keepdims=True)


def head_norms(rows, head_count):
    found = []
    for h in range(head_count):
        part = rows[h * HD : (h + 1) * HD, :].astype(F32)
        found.append(jnp.max(jnp.sum(part * part, axis=0, keepdims=True), axis=1, keepdims=True))
    return found


def safe_scores(query, key_norms):
    head_count = query.shape[0] // HD
    worst = None
    for h, found in enumerate(head_norms(query[...], head_count)):
        product = found * key_norms[h : h + 1, 0:1]
        worst = product if worst is None else jnp.maximum(worst, product)
    return jnp.max(worst) < SAFE * SAFE


def store_key_norms(key_norms, keys):
    head_count = keys.shape[0] // HD
    for h, found in enumerate(head_norms(keys[...], head_count)):
        key_norms[h : h + 1, :] = jnp.broadcast_to(found, (1, key_norms.shape[1]))


def doc_span(docs, seq, block, block_count):
    mine = docs[seq, block]
    low = jnp.int32(0)
    count = jnp.int32(0)
    for b in range(block_count):
        low = low + jnp.where(docs[seq, b] < mine, 1, 0).astype(jnp.int32)
        count = count + jnp.where(docs[seq, b] == mine, 1, 0).astype(jnp.int32)
    return low, count


def self_forward_kernel(
    shard, docs, spot, hidden, own_tokens, far_tokens, order, reach, pack0, pack1, pack2, pack3,
    keys, values, query, mixed, probs, inverse,
    plain, q_turned, k_turned, v_turned, bias, key_norms,
):
    seq, step = pl.program_id(0), pl.program_id(1)
    steps = pl.num_programs(1)
    rows = shard
    local = own_tokens.shape[1]
    far = far_tokens.shape[2]
    parts = far_tokens.shape[0] + 1
    block_count = order.shape[1]
    me = spot[0]

    @pl.when((seq == 0) & (step == 0))
    def _():
        for which, turned in enumerate((q_turned, k_turned, v_turned)):
            unpack((pack0, pack1, pack2, pack3), spot, which * rows, rows, plain.at[which])
            turned[...] = plain[which].T

    @pl.when(step == 0)
    def _():
        if far != local:
            keys[...] = jnp.zeros_like(keys)
        for part in range(parts):
            tokens = own_tokens[0] if part == 0 else far_tokens[part - 1, 0]
            at = token_window(me, part, parts, local, far)
            turned = tokens.T
            keys[0, :, at] = dot(k_turned[...], turned).astype(BF16)
            values[0, :, at] = dot(v_turned[...], turned).astype(BF16)
        store_key_norms(key_norms, keys.at[0])

    block = me * steps + step
    low, count = doc_span(docs, seq, block, block_count)
    query[0] = (dot(q_turned[...], hidden[0].T) * (LOG2E / math.sqrt(HD))).astype(BF16)

    order_turned = order[0].astype(F32).T
    lanes = lax.broadcasted_iota(jnp.int32, order_turned.shape, 1)
    reach_row = reach[0, pl.ds(block, 1), :].astype(F32)
    differ = lax.broadcasted_iota(jnp.int32, (BLK, BLK), 0) != lax.broadcasted_iota(
        jnp.int32, (BLK, BLK), 1
    )
    for j in range(WINDOW):
        at = low + j
        column = jnp.sum(jnp.where(lanes == at, order_turned, 0.0), axis=1, keepdims=True)
        seen = (column < reach_row) & (differ | (at != block))
        bias[j * BLK : (j + 1) * BLK, :] = jnp.where(seen, 0.0, MASKED)

    safe = safe_scores(query.at[0], key_norms)
    off = pl.multiple_of(low * BLK, BLK)
    for size in range(1, WINDOW + 1):
        for exact in (False, True):

            @pl.when((count == size) & (safe != exact))
            def _(size=size, exact=exact):
                attend(
                    size, exact, keys.at[0], values.at[0], off, query.at[0], probs.at[0, 0],
                    mixed.at[0], inverse.at[0, 0], bias,
                )


def token_window(me, part, parts, local, far):
    owner = lax.rem(me + part, parts)
    if part == 0 or far == local:
        return pl.ds(pl.multiple_of(owner * local, BLK), local)
    return pl.ds(pl.multiple_of(owner * local + jnp.where(owner == 0, local - far, 0), BLK), far)


def cross_forward_kernel(
    shard, bias_rows, spot, hidden, self_mixed, own_enc, far_enc, pack0, pack1, pack2, pack3,
    keys, values, query, mixed, probs, inverse, scaled1, scaled2, inverses, cols, bias_col,
    plain, spread_rows, so_turned, q_turned, k_turned, v_turned, o_turned, key_norms,
):
    seq, step = pl.program_id(0), pl.program_id(1)
    rows = shard
    local = own_enc.shape[1]
    parts = far_enc.shape[0] + 1
    packs = (pack0, pack1, pack2, pack3)

    @pl.when((seq == 0) & (step == 0))
    def _():
        for which, turned in enumerate((so_turned, q_turned, k_turned, v_turned, o_turned)):
            unpack(packs, spot, which * rows, rows, plain.at[which])
            turned[...] = plain[which].T
        depth = pack0.shape[0]
        for m, pack in enumerate(packs):
            for d in range(depth):
                row = pack[d, 5 * rows : 5 * rows + 16, :].astype(F32)[0:1, :]
                spread_rows[pl.ds(owner_of(spot, m, d, depth), 1), :] = row
        spread = spread_rows[...].T
        count = 4 * depth
        bias_col[...] = jnp.concatenate([spread[:bias_rows, f : f + 1] for f in range(count)], axis=0)
        for v in range(7):
            at = slice(bias_rows + v * rows, bias_rows + (v + 1) * rows)
            cols[:, v : v + 1] = jnp.concatenate([spread[at, f : f + 1] for f in range(count)], axis=0)

    @pl.when(step == 0)
    def _():
        for part in range(parts):
            turned = (own_enc[0] if part == 0 else far_enc[part - 1, 0]).T
            at = slice(part * local, (part + 1) * local)
            keys[0, :, at] = dot(k_turned[...], turned).astype(BF16)
            values[0, :, at] = dot(v_turned[...], turned).astype(BF16)
        store_key_norms(key_norms, keys.at[0])

    center, inverse1 = norm(hidden[0].T.astype(F32) + dot(so_turned[...], self_mixed[0]))
    scaled1[0] = center
    normed = center * cols[:, 0:1] + cols[:, 1:2]
    query[0] = (dot(q_turned[...], normed.astype(BF16)) * (LOG2E / math.sqrt(HD))).astype(BF16)
    safe = safe_scores(query.at[0], key_norms)
    for exact in (False, True):

        @pl.when(safe != exact)
        def _(exact=exact):
            attend(
                parts * local // BLK, exact, keys.at[0], values.at[0], 0, query.at[0], probs.at[0, 0],
                mixed.at[0], inverse.at[0, 0], None,
            )

    normed = scaled1[0] * cols[:, 0:1] + cols[:, 1:2]
    center, inverse2 = norm(normed + dot(o_turned[...], mixed[0]))
    scaled2[0] = center
    inverses[0, 0, 0:1, :] = inverse1
    inverses[0, 0, 1:2, :] = inverse2


def feed_forward_kernel(
    shard, outer_rows, spot, scaled2_in, inverses, out_grad, pack0, pack1, pack2, pack3, cols, inner_bias,
    second_grad, layer_out, out0, out1, out2, out3, late,
    inner, inner_turned, outer, outer_turned, inner_acc, outer_acc, sums, bias_sum, slope, sheet,
):
    seq, step = pl.program_id(0), pl.program_id(1)
    rows = shard
    first_step = (seq == 0) & (step == 0)
    last_step = (seq == pl.num_programs(0) - 1) & (step == pl.num_programs(1) - 1)
    width = inner.shape[0]
    chunks = inner.shape[1] // width
    packs = (pack0, pack1, pack2, pack3)

    @pl.when(first_step)
    def _():
        for c in range(chunks):
            cs = slice(c * width, (c + 1) * width)
            unpack(packs, spot, c * rows, rows, inner.at[:, cs])
            inner_turned[cs, :] = inner[:, cs].T
        unpack(packs, spot, chunks * rows, outer_rows, outer)
        for c in range(chunks):
            cs = slice(c * width, (c + 1) * width)
            outer_turned[:, cs] = outer[cs, :].T
        inner_acc[...] = jnp.zeros_like(inner_acc)
        outer_acc[...] = jnp.zeros_like(outer_acc)
        sums[...] = jnp.zeros_like(sums)
        bias_sum[...] = jnp.zeros_like(bias_sum)

    scaled2 = scaled2_in[0]
    gain2 = cols[:, 2:3]
    middle = scaled2 * gain2 + cols[:, 3:4]
    middle_low = middle.astype(BF16)
    pre = dot(inner_turned[...], middle_low) + inner_bias[...]
    active, pull = gelu_pair(pre)
    active = active.astype(BF16)
    slope[...] = pull.astype(BF16)
    third_sum = middle + dot(outer_turned[...], active) + cols[:, 6:7]
    scaled3, inverse3 = norm(third_sum)
    gain3 = cols[:, 4:5]
    layer_out[0] = (scaled3 * gain3 + cols[:, 5:6]).T
    upstream = out_grad[0].T.astype(F32)
    third_grad = norm_back(scaled3, inverse3, gain3, upstream)
    sums[2] += fold(upstream * scaled3)
    sums[3] += fold(upstream)
    outer_low = third_grad.astype(BF16)
    sums[4] += fold(outer_low.astype(F32))
    outer_acc[...] += dot(active, outer_low, NT)
    inner_low = (dot(outer[...], outer_low) * slope[...].astype(F32)).astype(BF16)
    bias_sum[...] += fold(inner_low.astype(F32))
    inner_acc[...] += dot(middle_low, inner_low, NT)
    middle_grad = third_grad + dot(inner[...], inner_low)
    sums[0] += fold(middle_grad * scaled2)
    sums[1] += fold(middle_grad)
    second_grad[0] = norm_back(scaled2, inverses[0, 0, 1:2, :], gain2, middle_grad)

    @pl.when(last_step)
    def _():
        outs = (out0, out1, out2, out3)
        for c in range(chunks):
            send_grad(outs, spot, c * rows, rows, inner_acc.at[:, c * width : (c + 1) * width])
        send_grad(outs, spot, chunks * rows, outer_rows, outer_acc)
        sheet[...] = jnp.zeros_like(sheet)
        for which in range(5):
            sheet[:, which : which + 1] = jnp.sum(sums[which], axis=1, keepdims=True)
        for c in range(chunks):
            part = bias_sum[c * width : (c + 1) * width, :]
            sheet[:, 8 + c : 9 + c] = jnp.sum(part, axis=1, keepdims=True)
        late[...] = sheet[...].T[0:16, :]


def cross_back_kernel(
    shard, spot, second_grad, scaled1, inverses, own_enc, far_enc, keys, values, query, mixed, probs, inverse,
    self_mixed, pack0, pack1, pack2, pack3, cols, late,
    first_grad, self_mixed_grad, own_part, far_part, out0, out1,
    so_plain, q_plain, k_plain, v_plain, o_plain, accs, sums, sheet,
    key_acc, value_acc, kept, grad, inner, query_grad,
):
    seq, step = pl.program_id(0), pl.program_id(1)
    rows = shard
    first_step = (seq == 0) & (step == 0)
    last_step = (seq == pl.num_programs(0) - 1) & (step == pl.num_programs(1) - 1)
    local = own_enc.shape[1]
    parts = far_enc.shape[0] + 1

    @pl.when(first_step)
    def _():
        for which, plain in enumerate((so_plain, q_plain, k_plain, v_plain, o_plain)):
            unpack((pack0, pack1, pack2, pack3), spot, which * rows, rows, plain)
        accs[...] = jnp.zeros_like(accs)
        sums[...] = jnp.zeros_like(sums)

    @pl.when(step == 0)
    def _():
        key_acc[...] = jnp.zeros_like(key_acc)
        value_acc[...] = jnp.zeros_like(value_acc)

    cross_low = second_grad[0].astype(BF16)
    scale_grad(dot(o_plain[...], cross_low), mixed.at[0], inverse.at[0, 0], grad, inner)
    accs[4] += dot(mixed[0], cross_low, NT)
    attend_back(
        parts * local // BLK, keys.at[0], values.at[0], 0, query.at[0], grad, inner, probs.at[0, 0],
        kept, query_grad, key_acc, value_acc,
    )
    scaled = scaled1[0]
    gain = cols[:, 0:1]
    normed_low = (scaled * gain + cols[:, 1:2]).astype(BF16)
    accs[1] += dot(normed_low, query_grad[...], NT)
    normed_grad = second_grad[0] + dot(q_plain[...], query_grad[...])
    sums[0] += fold(normed_grad * scaled)
    sums[1] += fold(normed_grad)
    through = norm_back(scaled, inverses[0, 0, 0:1, :], gain, normed_grad)
    first_grad[0] = through
    self_low = through.astype(BF16)
    accs[0] += dot(self_mixed[0], self_low, NT)
    self_mixed_grad[0] = dot(so_plain[...], self_low).astype(BF16)

    @pl.when(step == pl.num_programs(1) - 1)
    def _():
        for part in range(parts):
            at = slice(part * local, (part + 1) * local)
            key_low = (key_acc[:, at] * LN2).astype(BF16)
            value_low = value_acc[:, at].astype(BF16)
            turned = (own_enc[0] if part == 0 else far_enc[part - 1, 0]).T
            accs[2] += dot(turned, key_low, NT)
            accs[3] += dot(turned, value_low, NT)
            whole = (dot(k_plain[...], key_low) + dot(v_plain[...], value_low)).T
            if part == 0:
                own_part[0] = whole
            else:
                far_part[part - 1, 0] = whole.astype(BF16)

    @pl.when(last_step)
    def _():
        for y in range(2):
            outs = (out0.at[y], out1.at[y])
            for which in range(5):
                send_grad(outs, spot, which * rows, rows, accs.at[which], (2 * y, 2 * y + 1))
        sheet[...] = jnp.zeros_like(sheet)
        for which in range(2):
            sheet[:, 5 + which : 6 + which] = jnp.sum(sums[which], axis=1, keepdims=True)
        tray = (sheet[...].T[0:16, :] + late[...]).astype(BF16)
        for out in (out0, out1):
            for y in range(2):
                for d in range(out.shape[1]):
                    out[y, d, 5 * rows : 5 * rows + 16, :] = tray


def self_back_kernel(
    shard, docs, spot, hidden, first_grad, own_tokens, far_tokens, keys, values, query, mixed, probs, inverse,
    mixed_grad, pack0, pack1, pack2, pack3,
    hidden_grad, own_part, far_part, out0, out1,
    accs, q_plain, k_plain, v_plain, key_acc, value_acc, kept, grad, inner, query_grad,
):
    seq, step = pl.program_id(0), pl.program_id(1)
    steps = pl.num_programs(1)
    rows = shard
    local = own_tokens.shape[1]
    far = far_tokens.shape[2]
    parts = far_tokens.shape[0] + 1
    me = spot[0]
    block_count = parts * steps

    @pl.when((seq == 0) & (step == 0))
    def _():
        for which, plain in enumerate((q_plain, k_plain, v_plain)):
            unpack((pack0, pack1, pack2, pack3), spot, which * rows, rows, plain)
        accs[...] = jnp.zeros_like(accs)

    @pl.when(step == 0)
    def _():
        key_acc[...] = jnp.zeros_like(key_acc)
        value_acc[...] = jnp.zeros_like(value_acc)

    low, count = doc_span(docs, seq, me * steps + step, block_count)
    off = pl.multiple_of(low * BLK, BLK)
    scale_grad(mixed_grad[0].astype(F32), mixed.at[0], inverse.at[0, 0], grad, inner)
    for size in range(1, WINDOW + 1):

        @pl.when(count == size)
        def _(size=size):
            attend_back(
                size, keys.at[0], values.at[0], off, query.at[0], grad, inner, probs.at[0, 0],
                kept, query_grad, key_acc, value_acc,
            )

    accs[0] += dot(hidden[0].T, query_grad[...], NT)
    hidden_grad[0] = (first_grad[0] + dot(q_plain[...], query_grad[...])).T

    @pl.when(step == steps - 1)
    def _():
        for part in range(parts):
            at = token_window(me, part, parts, local, far)
            key_low = (key_acc[:, at] * LN2).astype(BF16)
            value_low = value_acc[:, at].astype(BF16)
            turned = (own_tokens[0] if part == 0 else far_tokens[part - 1, 0]).T
            accs[1] += dot(turned, key_low, NT)
            accs[2] += dot(turned, value_low, NT)
            whole = (dot(k_plain[...], key_low) + dot(v_plain[...], value_low)).T
            if part == 0:
                own_part[0] = whole
            else:
                far_part[part - 1, 0] = whole.astype(BF16)

    @pl.when((seq == pl.num_programs(0) - 1) & (step == steps - 1))
    def _():
        for y in range(2):
            outs = (out0.at[y], out1.at[y])
            for which in range(3):
                send_grad(outs, spot, which * rows, rows, accs.at[which], (2 * y, 2 * y + 1))


def settle_kernel(spot, own, far, out):
    out[...] = own[...] + far[...].astype(F32)


def whole_spec():
    return pl.BlockSpec(memory_space=pltpu.VMEM)


def call(body, grid, scalars, in_specs, out_specs, out_shape, scratch, micros, args, aliases={}):
    return pl.pallas_call(
        body,
        grid_spec=pltpu.PrefetchScalarGridSpec(
            num_scalar_prefetch=scalars,
            grid=grid,
            in_specs=in_specs,
            out_specs=out_specs,
            scratch_shapes=scratch,
        ),
        out_shape=[jax.ShapeDtypeStruct(shape, kind) for shape, kind in out_shape],
        input_output_aliases=aliases,
        compiler_params=pltpu.CompilerParams(vmem_limit_bytes=VMEM_LIMIT),
        cost_estimate=pl.CostEstimate(flops=int(micros * 1e9), bytes_accessed=2**24, transcendentals=0),
    )(*args)


def shift(array, axis, by, size):
    return lax.ppermute(array, axis, [((i + by) % size, i) for i in range(size)])


def z_shift(array, by, depth):
    pairs = [(((z + by) % depth) * 4 + w, z * 4 + w) for z in range(depth) for w in range(4)]
    return lax.ppermute(array, "fsdp", pairs)


def w_flip(array, mask, depth):
    return lax.ppermute(array, "fsdp", [(z * 4 + (w ^ mask), z * 4 + w) for z in range(depth) for w in range(4)])


def together(*arrays):
    return lax.optimization_barrier(arrays)


def after(array, *earlier):
    return lax.optimization_barrier((array,) + earlier)[0]


def gather_stack(packed, got):
    return jnp.stack([packed] + got)


def gather_z(packed, depth):
    return gather_stack(packed, [z_shift(packed, d, depth) for d in range(1, depth)])


def gather_w(pieces, depth):
    across = w_flip(pieces, 2, depth)
    return [pieces, w_flip(pieces, 1, depth), across, w_flip(across, 1, depth)]


def swap_w(outs, depth):
    return [w_flip(outs[m], m, depth) for m in (1, 2, 3)]


def swap_z(pieces, depth):
    return [z_shift(pieces[d].astype(BF16), -d, depth) for d in range(1, depth)]


def add_w(own, got, depth):
    return [sum(piece[d].astype(F32) for piece in [own] + got) for d in range(depth)]


def swap_sp(total, sp):
    mine = total.astype(BF16)
    return [shift(mine, "sp", r, sp) for r in range(1, sp)]


def add_all(total, got):
    return sum((piece.astype(F32) for piece in got), total)


def on_device(sp, fsdp, *arrays):
    (
        hidden_in, token_stream, encoder_out, out_grad, doc_ids, key_order, context_size,
        self_query, self_key, self_value, self_output, cross_query, cross_key, cross_value, cross_output,
        inner_weight, inner_bias, outer_weight, outer_bias, first_gain, first_shift, second_gain,
        second_shift, third_gain, third_shift,
    ) = arrays
    seqs, local, width = hidden_in.shape
    enc_local = encoder_out.shape[1]
    shard, hidden_width = inner_weight.shape
    outer_rows = outer_weight.shape[0]
    bias_rows = inner_bias.shape[0]
    chunks = hidden_width // width
    steps = local // BLK
    heads = width // HD
    length = local * sp
    enc_len = enc_local * sp
    block_count = key_order.shape[1]
    depth = fsdp // 4
    tray = 16
    far = min(local, (WINDOW - 1) * BLK) if sp == 2 else local

    me, mine = lax.axis_index("sp"), lax.axis_index("fsdp")
    spot = jnp.stack([me, mine // 4, mine // 2 % 2, mine % 2]).astype(jnp.int32)

    pack_a = jnp.concatenate([self_query, self_key, self_value], axis=0)
    sent = token_stream
    if far != local:
        start = jnp.where(me == 0, local - far, 0)
        sent = lax.dynamic_slice(token_stream, (0, start, 0), (seqs, far, width))
    far_tokens = jnp.stack([shift(sent, "sp", r, sp) for r in range(1, sp)])
    vectors = (inner_bias, first_gain, first_shift, second_gain, second_shift, third_gain, third_shift, outer_bias)
    flat = jnp.concatenate(vectors)
    flat = jnp.pad(flat, (0, tray * width - flat.shape[0])).reshape(tray, width)
    pack_b = jnp.concatenate([self_output, cross_query, cross_key, cross_value, cross_output, flat], axis=0)
    pack_c = jnp.concatenate(jnp.split(inner_weight, chunks, axis=1) + [outer_weight], axis=0)

    pieces_a = gather_z(pack_a, depth)
    pieces_b = gather_z(after(pack_b, pieces_a), depth)
    packs_a = gather_w(pieces_a, depth)
    hidden_early, pieces_b = together(hidden_in, pieces_b)
    core_b = w_flip(pieces_b, 1, depth)
    hidden_early, core_b = together(hidden_early, core_b)
    swap_b = w_flip(pieces_b, 2, depth)
    swap_c = [z_shift(after(pack_c, pieces_b), d, depth) for d in range(1, depth)]
    sent = after(encoder_out, far_tokens)
    far_enc = jnp.stack([shift(sent, "sp", r, sp) for r in range(1, sp)])

    whole = whole_spec()
    anywhere = pl.BlockSpec(memory_space=pl.ANY)
    turned_spec = lambda b=0: pl.BlockSpec((1, width, BLK), lambda s, i, *_: (s + b, 0, i))
    plain_spec = lambda b=0: pl.BlockSpec((1, BLK, width), lambda s, i, *_: (s + b, i, 0))
    per_seq = lambda shape, b=0: pl.BlockSpec((1,) + shape, lambda s, i, *_: (s + b, 0, 0))
    far_seq = lambda rows: pl.BlockSpec((sp - 1, 1, rows, width), lambda s, i, *_: (0, s, 0, 0))
    rows_spec = lambda b=0: pl.BlockSpec((1, 1, 8, BLK), lambda s, i, *_: (s + b, i, 0, 0))
    probs_spec = lambda keys, b=0: pl.BlockSpec(
        (1, 1, heads, keys, BLK), lambda s, i, *_: (s + b, i, 0, 0, 0)
    )
    turned_shape = (seqs, width, local)
    rows_shape = (seqs, steps, 8, BLK)
    big = lambda a, b, kind: pltpu.VMEM((a, b), kind)
    square = big(width, width, BF16)
    window = WINDOW * BLK

    keys, values, query, mixed, probs, inverse = call(
        functools.partial(self_forward_kernel, shard),
        (seqs, steps), 2,
        [
            plain_spec(), per_seq((local, width)), far_seq(far), per_seq((block_count, BLK)),
            per_seq((block_count, BLK)),
        ] + [whole] * 4,
        [
            per_seq((width, length)), per_seq((width, length)), turned_spec(), turned_spec(),
            probs_spec(window), rows_spec(),
        ],
        [
            ((seqs, width, length), BF16), ((seqs, width, length), BF16), (turned_shape, BF16),
            (turned_shape, BF16), ((seqs, steps, heads, window, BLK), BF16), (rows_shape, F32),
        ],
        [pltpu.VMEM((3, width, width), BF16)] + [square] * 3 + [big(window, BLK, F32), big(heads, 128, F32)],
        32000.0,
        (doc_ids, spot, hidden_early, token_stream, far_tokens, key_order, context_size, *packs_a),
    )
    keys, values, query, mixed, probs, inverse, pieces_b, far_enc, swap_b, *swap_c = together(
        keys, values, query, mixed, probs, inverse, pieces_b, far_enc, swap_b, *swap_c
    )
    packs_b = [pieces_b, core_b, swap_b, w_flip(swap_b, 1, depth)]
    pieces_c = jnp.stack([pack_c] + swap_c)
    mixed, pieces_c = together(mixed, pieces_c)
    swap_c = w_flip(pieces_c, 2, depth)

    (
        cross_keys, cross_values, cross_q, cross_mixed, cross_probs, cross_inverse, scaled1, scaled2, inverses,
        cols, inner_bias_col,
    ) = call(
        functools.partial(cross_forward_kernel, shard, bias_rows),
        (seqs, steps), 1,
        [plain_spec(), turned_spec(), per_seq((enc_local, width)), far_seq(enc_local)] + [whole] * 4,
        [
            per_seq((width, enc_len)), per_seq((width, enc_len)), turned_spec(), turned_spec(), probs_spec(enc_len),
            rows_spec(), turned_spec(), turned_spec(), rows_spec(), whole, whole,
        ],
        [
            ((seqs, width, enc_len), BF16), ((seqs, width, enc_len), BF16), (turned_shape, BF16),
            (turned_shape, BF16), ((seqs, steps, heads, enc_len, BLK), BF16), (rows_shape, F32),
            (turned_shape, F32), (turned_shape, F32), (rows_shape, F32), ((width, 8), F32),
            ((hidden_width, 1), F32),
        ],
        [pltpu.VMEM((5, width, width), BF16), big(fsdp, width, F32)] + [square] * 5 + [big(heads, 128, F32)],
        32000.0,
        (spot, hidden_in, mixed, encoder_out, far_enc, *packs_b),
    )

    (
        cross_keys, cross_values, cross_q, cross_mixed, cross_probs, cross_inverse, scaled1, scaled2, inverses,
        cols, inner_bias_col, pieces_c, swap_c,
    ) = together(
        cross_keys, cross_values, cross_q, cross_mixed, cross_probs, cross_inverse, scaled1, scaled2, inverses,
        cols, inner_bias_col, pieces_c, swap_c,
    )
    packs_c = [pieces_c, w_flip(pieces_c, 1, depth), swap_c, w_flip(swap_c, 1, depth)]

    grads_shape = lambda rows: [((depth, rows, width), BF16)] * 4
    ff_rows = chunks * shard + outer_rows
    second_grad, layer_out, *ff_outs, late = call(
        functools.partial(feed_forward_kernel, shard, outer_rows),
        (seqs, steps), 1,
        [turned_spec(), rows_spec(), plain_spec()] + [whole] * 6,
        [turned_spec(), plain_spec()] + [whole] * 5,
        [(turned_shape, F32), ((seqs, local, width), F32)] + grads_shape(ff_rows) + [((16, width), F32)],
        [
            big(width, hidden_width, BF16), big(hidden_width, width, BF16), big(hidden_width, width, BF16),
            big(width, hidden_width, BF16), big(width, hidden_width, F32), big(hidden_width, width, F32),
            pltpu.VMEM((5, width, 128), F32), big(hidden_width, 128, F32), big(hidden_width, BLK, BF16),
            big(width, 128, F32),
        ],
        70000.0,
        (spot, scaled2, inverses, out_grad, *packs_c, cols, inner_bias_col),
    )

    ff_swap = swap_w(ff_outs, depth)
    attention_scratch = lambda keys_len, kept_len: [
        big(width, keys_len, F32), big(width, keys_len, F32), pltpu.VMEM((heads, kept_len, BLK), BF16),
        big(width, BLK, BF16), big(heads, BLK, F32), big(width, BLK, BF16),
    ]
    first_grad, mixed_grad, own_enc_part, far_enc_part, *cross_outs = call(
        functools.partial(cross_back_kernel, shard),
        (seqs, steps), 1,
        [
            turned_spec(), turned_spec(), rows_spec(), per_seq((enc_local, width)), far_seq(enc_local),
            per_seq((width, enc_len)), per_seq((width, enc_len)), turned_spec(), turned_spec(),
            probs_spec(enc_len), rows_spec(), turned_spec(),
        ] + [whole] * 6,
        [
            turned_spec(), turned_spec(), per_seq((enc_local, width)), far_seq(enc_local),
        ] + [whole] * 2,
        [
            (turned_shape, F32), (turned_shape, BF16), ((seqs, enc_local, width), F32),
            ((sp - 1, seqs, enc_local, width), BF16),
        ] + [((2, depth, 5 * shard + tray, width), BF16)] * 2,
        [square] * 5
        + [pltpu.VMEM((5, width, width), F32), pltpu.VMEM((2, width, 128), F32), big(width, 128, F32)]
        + attention_scratch(enc_len, enc_len),
        56000.0,
        (
            spot, second_grad, scaled1, inverses, encoder_out, far_enc, cross_keys, cross_values, cross_q,
            cross_mixed, cross_probs, cross_inverse, mixed, *packs_b, cols, late,
        ),
    )

    first_grad, mixed_grad, own_enc_part, far_enc_part, *got = together(
        first_grad, mixed_grad, own_enc_part, far_enc_part, *cross_outs, *ff_swap
    )
    cross_outs, ff_swap = got[:2], got[2:]
    cross_core = w_flip(cross_outs[1], 1, depth)
    ff_pieces = add_w(ff_outs[0], ff_swap, depth)
    cross_half = [cross_outs[0][y].astype(F32) + cross_core[y].astype(F32) for y in range(2)]
    mixed_grad, *got = together(mixed_grad, *cross_half, *ff_pieces)
    cross_half, ff_pieces = got[:2], got[2:]
    ff_swap = swap_z(ff_pieces, depth)
    enc_swap = [shift(far_enc_part[r - 1], "sp", -r, sp) for r in range(1, sp)]
    cross_swap = w_flip(cross_half[1].astype(BF16), 2, depth)
    hidden_grad, token_grad, far_part, *self_outs = call(
        functools.partial(self_back_kernel, shard),
        (seqs, steps), 2,
        [
            plain_spec(), turned_spec(), per_seq((local, width)), far_seq(far),
            per_seq((width, length)), per_seq((width, length)), turned_spec(), turned_spec(),
            probs_spec(window), rows_spec(), turned_spec(),
        ] + [whole] * 4,
        [plain_spec(), per_seq((local, width)), far_seq(far)] + [whole] * 2,
        [((seqs, local, width), F32), ((seqs, local, width), F32), ((sp - 1, seqs, far, width), BF16)]
        + [((2, depth, 3 * shard, width), BF16)] * 2,
        [pltpu.VMEM((3, width, width), F32)] + [square] * 3 + attention_scratch(length, window),
        50000.0,
        (
            doc_ids, spot, hidden_in, first_grad, token_stream, far_tokens, keys, values, query, mixed,
            probs, inverse, mixed_grad, *packs_a,
        ),
    )

    count = len(ff_swap)
    hidden_grad, token_grad, far_part, own_half, far_half, *got = together(
        hidden_grad, token_grad, far_part, *self_outs, *ff_swap, cross_swap, *enc_swap
    )
    ff_got, cross_swap, enc_swap = got[:count], got[count], got[count + 1 :]
    self_got = w_flip(far_half, 1, depth)
    ff_sum = add_all(ff_pieces[0], ff_got)
    ff_sp = swap_sp(ff_sum, sp)
    cross_pieces = [cross_half[0][d] + cross_swap[d].astype(F32) for d in range(depth)]
    cross_got = swap_z(cross_pieces, depth)
    self_half = [own_half[y].astype(F32) + self_got[y].astype(F32) for y in range(2)]
    self_swap = w_flip(self_half[1].astype(BF16), 2, depth)
    self_pieces = [self_half[0][d] + self_swap[d].astype(F32) for d in range(depth)]
    cross_sum = add_all(cross_pieces[0], [after(piece, self_swap) for piece in cross_got])
    self_more = swap_z(self_pieces, depth)
    cross_sp = swap_sp(cross_sum, sp)
    self_sum = add_all(self_pieces[0], self_more)
    self_sp = swap_sp(self_sum, sp)

    shift_back = (local - far) // BLK
    for r in range(1, sp):
        got = shift(far_part[r - 1], "sp", -r, sp)
        spec = pl.BlockSpec(
            (1, BLK, width), lambda s, i, spot: (s, i + jnp.where(spot[0] == 0, shift_back, 0), 0)
        )
        (token_grad,) = call(
            settle_kernel, (seqs, far // BLK), 1,
            [spec, pl.BlockSpec((1, BLK, width), lambda s, i, spot: (s, i, 0))],
            [spec], [((seqs, local, width), F32)], [], 2000.0, (spot, token_grad, got), {1: 0},
        )
    encoder_grad = own_enc_part
    for r in range(1, sp):
        encoder_grad = encoder_grad + enc_swap[r - 1].astype(F32)

    ff_total = add_all(ff_sum, ff_sp)
    cross_total = add_all(cross_sum, cross_sp)
    self_total = add_all(self_sum, self_sp)
    inner_total = jnp.concatenate([ff_total[c * shard : (c + 1) * shard] for c in range(chunks)], axis=1)
    outer_total = ff_total[chunks * shard :]
    small = cross_total[5 * shard :]
    cut = lambda total, k: total[k * shard : (k + 1) * shard]
    vec = lambda k: lax.dynamic_slice(small, (k, mine * shard), (1, shard))[0]
    bias_total = lax.dynamic_slice(small[8 : 8 + chunks].reshape(-1), (mine * bias_rows,), (bias_rows,))
    return (
        layer_out, hidden_grad, token_grad, encoder_grad,
        cut(self_total, 0), cut(self_total, 1), cut(self_total, 2), cut(cross_total, 0),
        cut(cross_total, 1), cut(cross_total, 2), cut(cross_total, 3), cut(cross_total, 4),
        inner_total, bias_total, outer_total, vec(4), vec(5), vec(6), vec(0), vec(1), vec(2), vec(3),
    )


def solution(mesh):
    tokens, table, vector = P("fsdp", "sp", None), P("fsdp", None), P("fsdp")
    order = P("fsdp", None, None)
    return jax.shard_map(
        functools.partial(on_device, mesh.shape["sp"], mesh.shape["fsdp"]),
        mesh=mesh,
        in_specs=(tokens,) * 4
        + (table, order, order)
        + (table,) * 9
        + (vector, table)
        + (vector,) * 7,
        out_specs=(tokens,) * 4 + (table,) * 9 + (vector, table) + (vector,) * 7,
        check_vma=False,
    )
```

```python
import functools
import math

import jax
import jax.numpy as jnp
from jax import lax
from jax.experimental import pallas as pl
from jax.experimental.pallas import tpu as pltpu
from jax.sharding import PartitionSpec as P

HD = 64
BLK = 256
WINDOW = 4
EPS = 1e-05
MASKED = -1e30
LOG2E = 1.4426950408889634
LN2 = 0.6931471805599453
SAFE = 60.0
F32 = jnp.float32
BF16 = jnp.bfloat16
NN = (((1,), (0,)), ((), ()))
NT = (((1,), (1,)), ((), ()))
TN = (((0,), (0,)), ((), ()))
VMEM_LIMIT = 62 * 2**20


def dot(left, right, form=NN):
    return lax.dot_general(left, right, form, preferred_element_type=F32)


def norm(rows):
    center = rows - jnp.mean(rows, axis=0, keepdims=True)
    inverse = lax.rsqrt(jnp.mean(center * center, axis=0, keepdims=True) + EPS)
    return center * inverse, inverse


def norm_back(scaled, inverse, gain, upstream):
    through = upstream * gain
    return inverse * (
        through
        - jnp.mean(through, axis=0, keepdims=True)
        - scaled * jnp.mean(through * scaled, axis=0, keepdims=True)
    )


def fold(values):
    total = values[:, :128]
    for start in range(128, values.shape[1], 128):
        total = total + values[:, start : start + 128]
    return total


def gelu_pair(x):
    phi = 0.5 + 0.5 * lax.erf(x * math.sqrt(0.5))
    bell = jnp.exp2((-0.5 * LOG2E) * (x * x))
    return x * phi, phi + x * bell * (1.0 / math.sqrt(2.0 * math.pi))


def owner_of(spot, m, d, depth):
    z = lax.rem(spot[1] + d, depth)
    return (z * 2 + jnp.bitwise_xor(spot[2], m // 2)) * 2 + jnp.bitwise_xor(spot[3], m % 2)


def unpack(packs, spot, first, rows, plain):
    for m, pack in enumerate(packs):
        depth = pack.shape[0]
        for d in range(depth):
            at = pl.ds(pl.multiple_of(owner_of(spot, m, d, depth) * rows, rows), rows)
            plain[at, :] = pack[d, first : first + rows, :]


def send_grad(outs, spot, first, rows, acc, masks=(0, 1, 2, 3)):
    depth = outs[0].shape[0]
    for out, m in zip(outs, masks):
        for d in range(depth):
            at = pl.ds(pl.multiple_of(owner_of(spot, m, d, depth) * rows, rows), rows)
            out[d, first : first + rows, :] = acc[at, :].astype(BF16)


def attend(count, exact, keys, values, off, query, probs, mixed, inverse, bias):
    head_count, span = query.shape[0] // HD, query.shape[1]

    def scores(hs, j):
        part = dot(keys[hs, pl.ds(off + j * BLK, BLK)], query[hs, :], TN)
        if bias is not None:
            part = part + bias[j * BLK : (j + 1) * BLK, :]
        return part

    def first(h, hs):
        total = None
        if exact:
            parts = [scores(hs, j) for j in range(count)]
            top = jnp.max(parts[0], axis=0, keepdims=True)
            for part in parts[1:]:
                top = jnp.maximum(top, jnp.max(part, axis=0, keepdims=True))
        for j in range(count):
            terms = jnp.exp2(parts[j] - top if exact else scores(hs, j))
            partial = jnp.sum(terms.reshape(BLK // 8, 8, span), axis=0)
            total = partial if total is None else total + partial
            probs[h, j * BLK : (j + 1) * BLK, :] = terms.astype(BF16)
        return total

    def second(h, hs, total):
        sums = dot(values[hs, pl.ds(off, count * BLK)], probs[h, : count * BLK, :])
        scale = 1.0 / jnp.sum(total, axis=0, keepdims=True)
        mixed[hs, :] = (sums * scale).astype(BF16)
        inverse[pl.ds(h, 1), :] = scale

    if exact:

        def one(h, carry):
            hs = pl.ds(pl.multiple_of(h * HD, HD), HD)
            second(h, hs, first(h, hs))
            return carry

        lax.fori_loop(0, head_count, one, 0)
        return
    waiting = None
    for h in range(head_count):
        total = first(h, slice(h * HD, (h + 1) * HD))
        if h > 0:
            second(h - 1, slice((h - 1) * HD, h * HD), waiting)
        waiting = total
    second(head_count - 1, slice((head_count - 1) * HD, head_count * HD), waiting)


def attend_back(
    count, keys, values, off, query, grad, inner, probs, kept, query_grad, key_grad, value_grad
):
    head_count = query.shape[0] // HD

    def first(h):
        hs = slice(h * HD, (h + 1) * HD)
        for j in range(count):
            us = slice(j * BLK, (j + 1) * BLK)
            prob_grad = dot(values[hs, pl.ds(off + j * BLK, BLK)], grad[hs, :], TN)
            change = probs[h, us, :].astype(F32) * (prob_grad - inner[h : h + 1, :])
            kept[h, us, :] = change.astype(BF16)

    def second(h):
        hs = slice(h * HD, (h + 1) * HD)
        us = slice(0, count * BLK)
        window = pl.ds(off, count * BLK)
        query_grad[hs, :] = (dot(keys[hs, window], kept[h, us, :]) * (1.0 / math.sqrt(HD))).astype(BF16)
        key_grad[hs, window] += dot(query[hs, :], kept[h, us, :], NT)
        value_grad[hs, window] += dot(grad[hs, :], probs[h, us, :], NT)

    first(0)
    for h in range(1, head_count):
        first(h)
        second(h - 1)
    second(head_count - 1)


def scale_grad(mixed_grad, mixed, inverse, grad, inner):
    for h in range(mixed.shape[0] // HD):
        hs = slice(h * HD, (h + 1) * HD)
        scaled = mixed_grad[hs, :] * inverse[h : h + 1, :]
        grad[hs, :] = scaled.astype(BF16)
        inner[h : h + 1, :] = jnp.sum(scaled * mixed[hs, :].astype(F32), axis=0, keepdims=True)


def head_norms(rows, head_count):
    found = []
    for h in range(head_count):
        part = rows[h * HD : (h + 1) * HD, :].astype(F32)
        found.append(jnp.max(jnp.sum(part * part, axis=0, keepdims=True), axis=1, keepdims=True))
    return found


def safe_scores(query, key_norms):
    head_count = query.shape[0] // HD
    worst = None
    for h, found in enumerate(head_norms(query[...], head_count)):
        product = found * key_norms[h : h + 1, 0:1]
        worst = product if worst is None else jnp.maximum(worst, product)
    return jnp.max(worst) < SAFE * SAFE


def store_key_norms(key_norms, keys):
    head_count = keys.shape[0] // HD
    for h, found in enumerate(head_norms(keys[...], head_count)):
        key_norms[h : h + 1, :] = jnp.broadcast_to(found, (1, key_norms.shape[1]))


def doc_span(docs, seq, block, block_count):
    mine = docs[seq, block]
    low = jnp.int32(0)
    count = jnp.int32(0)
    for b in range(block_count):
        low = low + jnp.where(docs[seq, b] < mine, 1, 0).astype(jnp.int32)
        count = count + jnp.where(docs[seq, b] == mine, 1, 0).astype(jnp.int32)
    return low, count


def self_forward_kernel(
    shard, docs, spot, hidden, own_tokens, far_tokens, order, reach, pack0, pack1, pack2, pack3,
    keys, values, query, mixed, probs, inverse,
    plain, q_turned, k_turned, v_turned, bias, key_norms,
):
    seq, step = pl.program_id(0), pl.program_id(1)
    steps = pl.num_programs(1)
    rows = shard
    local = own_tokens.shape[1]
    far = far_tokens.shape[2]
    parts = far_tokens.shape[0] + 1
    block_count = order.shape[1]
    me = spot[0]

    @pl.when((seq == 0) & (step == 0))
    def _():
        for which, turned in enumerate((q_turned, k_turned, v_turned)):
            unpack((pack0, pack1, pack2, pack3), spot, which * rows, rows, plain.at[which])
            turned[...] = plain[which].T

    @pl.when(step == 0)
    def _():
        if far != local:
            keys[...] = jnp.zeros_like(keys)
        for part in range(parts):
            tokens = own_tokens[0] if part == 0 else far_tokens[part - 1, 0]
            at = token_window(me, part, parts, local, far)
            turned = tokens.T
            keys[0, :, at] = dot(k_turned[...], turned).astype(BF16)
            values[0, :, at] = dot(v_turned[...], turned).astype(BF16)
        store_key_norms(key_norms, keys.at[0])

    query[0] = (dot(q_turned[...], hidden[0].T) * (LOG2E / math.sqrt(HD))).astype(BF16)
    safe = safe_scores(query.at[0], key_norms)
    order_turned = order[0].astype(F32).T
    lanes = lax.broadcasted_iota(jnp.int32, order_turned.shape, 1)
    differ = lax.broadcasted_iota(jnp.int32, (BLK, BLK), 0) != lax.broadcasted_iota(
        jnp.int32, (BLK, BLK), 1
    )
    subs = hidden.shape[1] // BLK
    for part in range(subs):
        block = (me * steps + step) * subs + part
        low, count = doc_span(docs, seq, block, block_count)
        reach_row = reach[0, pl.ds(block, 1), :].astype(F32)
        for j in range(WINDOW):
            at = low + j
            column = jnp.sum(jnp.where(lanes == at, order_turned, 0.0), axis=1, keepdims=True)
            seen = (column < reach_row) & (differ | (at != block))
            bias[part, j * BLK : (j + 1) * BLK, :] = jnp.where(seen, 0.0, MASKED)
        off = pl.multiple_of(low * BLK, BLK)
        ts = slice(part * BLK, (part + 1) * BLK)
        for size in range(1, WINDOW + 1):
            for exact in (False, True):

                @pl.when((count == size) & (safe != exact))
                def _(size=size, exact=exact, part=part, off=off, ts=ts):
                    attend(
                        size, exact, keys.at[0], values.at[0], off, query.at[0, :, ts], probs.at[0, part],
                        mixed.at[0, :, ts], inverse.at[0, part], bias.at[part],
                    )


def token_window(me, part, parts, local, far):
    owner = lax.rem(me + part, parts)
    if part == 0 or far == local:
        return pl.ds(pl.multiple_of(owner * local, BLK), local)
    return pl.ds(pl.multiple_of(owner * local + jnp.where(owner == 0, local - far, 0), BLK), far)


def cross_forward_kernel(
    shard, bias_rows, spot, hidden, self_mixed, own_enc, far_enc, pack0, pack1, pack2, pack3,
    keys, values, query, mixed, probs, inverse, scaled1, scaled2, inverses, cols, bias_col,
    plain, spread_rows, so_turned, q_turned, k_turned, v_turned, o_turned, key_norms,
):
    seq, step = pl.program_id(0), pl.program_id(1)
    rows = shard
    local = own_enc.shape[1]
    parts = far_enc.shape[0] + 1
    packs = (pack0, pack1, pack2, pack3)

    @pl.when((seq == 0) & (step == 0))
    def _():
        for which, turned in enumerate((so_turned, q_turned, k_turned, v_turned, o_turned)):
            unpack(packs, spot, which * rows, rows, plain.at[which])
            turned[...] = plain[which].T
        depth = pack0.shape[0]
        for m, pack in enumerate(packs):
            for d in range(depth):
                row = pack[d, 5 * rows : 5 * rows + 16, :].astype(F32)[0:1, :]
                spread_rows[pl.ds(owner_of(spot, m, d, depth), 1), :] = row
        spread = spread_rows[...].T
        count = 4 * depth
        bias_col[...] = jnp.concatenate([spread[:bias_rows, f : f + 1] for f in range(count)], axis=0)
        for v in range(7):
            at = slice(bias_rows + v * rows, bias_rows + (v + 1) * rows)
            cols[:, v : v + 1] = jnp.concatenate([spread[at, f : f + 1] for f in range(count)], axis=0)

    @pl.when(step == 0)
    def _():
        for part in range(parts):
            turned = (own_enc[0] if part == 0 else far_enc[part - 1, 0]).T
            at = slice(part * local, (part + 1) * local)
            keys[0, :, at] = dot(k_turned[...], turned).astype(BF16)
            values[0, :, at] = dot(v_turned[...], turned).astype(BF16)
        store_key_norms(key_norms, keys.at[0])

    center, inverse1 = norm(hidden[0].T.astype(F32) + dot(so_turned[...], self_mixed[0]))
    scaled1[0] = center
    normed = center * cols[:, 0:1] + cols[:, 1:2]
    query[0] = (dot(q_turned[...], normed.astype(BF16)) * (LOG2E / math.sqrt(HD))).astype(BF16)
    safe = safe_scores(query.at[0], key_norms)
    for exact in (False, True):

        @pl.when(safe != exact)
        def _(exact=exact):
            attend(
                parts * local // BLK, exact, keys.at[0], values.at[0], 0, query.at[0], probs.at[0, 0],
                mixed.at[0], inverse.at[0, 0], None,
            )

    normed = scaled1[0] * cols[:, 0:1] + cols[:, 1:2]
    center, inverse2 = norm(normed + dot(o_turned[...], mixed[0]))
    scaled2[0] = center
    inverses[0, 0, 0:1, :] = inverse1
    inverses[0, 0, 1:2, :] = inverse2


def feed_forward_kernel(
    shard, outer_rows, spot, scaled2_in, inverses, out_grad, pack0, pack1, pack2, pack3, cols, inner_bias,
    second_grad, layer_out, out0, out1, out2, out3, late,
    inner, inner_turned, outer, outer_turned, inner_acc, outer_acc, sums, bias_sum, slope, sheet,
):
    seq, step = pl.program_id(0), pl.program_id(1)
    rows = shard
    first_step = (seq == 0) & (step == 0)
    last_step = (seq == pl.num_programs(0) - 1) & (step == pl.num_programs(1) - 1)
    width = inner.shape[0]
    chunks = inner.shape[1] // width
    packs = (pack0, pack1, pack2, pack3)

    @pl.when(first_step)
    def _():
        for c in range(chunks):
            cs = slice(c * width, (c + 1) * width)
            unpack(packs, spot, c * rows, rows, inner.at[:, cs])
            inner_turned[cs, :] = inner[:, cs].T
        unpack(packs, spot, chunks * rows, outer_rows, outer)
        for c in range(chunks):
            cs = slice(c * width, (c + 1) * width)
            outer_turned[:, cs] = outer[cs, :].T
        inner_acc[...] = jnp.zeros_like(inner_acc)
        outer_acc[...] = jnp.zeros_like(outer_acc)
        sums[...] = jnp.zeros_like(sums)
        bias_sum[...] = jnp.zeros_like(bias_sum)

    scaled2 = scaled2_in[0]
    gain2 = cols[:, 2:3]
    middle = scaled2 * gain2 + cols[:, 3:4]
    middle_low = middle.astype(BF16)
    pre = dot(inner_turned[...], middle_low) + inner_bias[...]
    active, pull = gelu_pair(pre)
    active = active.astype(BF16)
    slope[...] = pull.astype(BF16)
    third_sum = middle + dot(outer_turned[...], active) + cols[:, 6:7]
    scaled3, inverse3 = norm(third_sum)
    gain3 = cols[:, 4:5]
    layer_out[0] = (scaled3 * gain3 + cols[:, 5:6]).T
    upstream = out_grad[0].T.astype(F32)
    third_grad = norm_back(scaled3, inverse3, gain3, upstream)
    sums[2] += fold(upstream * scaled3)
    sums[3] += fold(upstream)
    outer_low = third_grad.astype(BF16)
    sums[4] += fold(outer_low.astype(F32))
    outer_acc[...] += dot(active, outer_low, NT)
    inner_low = (dot(outer[...], outer_low) * slope[...].astype(F32)).astype(BF16)
    bias_sum[...] += fold(inner_low.astype(F32))
    inner_acc[...] += dot(middle_low, inner_low, NT)
    middle_grad = third_grad + dot(inner[...], inner_low)
    sums[0] += fold(middle_grad * scaled2)
    sums[1] += fold(middle_grad)
    second_grad[0] = norm_back(scaled2, inverses[0, 0, 1:2, :], gain2, middle_grad)

    @pl.when(last_step)
    def _():
        outs = (out0, out1, out2, out3)
        for c in range(chunks):
            send_grad(outs, spot, c * rows, rows, inner_acc.at[:, c * width : (c + 1) * width])
        send_grad(outs, spot, chunks * rows, outer_rows, outer_acc)
        sheet[...] = jnp.zeros_like(sheet)
        for which in range(5):
            sheet[:, which : which + 1] = jnp.sum(sums[which], axis=1, keepdims=True)
        for c in range(chunks):
            part = bias_sum[c * width : (c + 1) * width, :]
            sheet[:, 8 + c : 9 + c] = jnp.sum(part, axis=1, keepdims=True)
        late[...] = sheet[...].T[0:16, :]


def cross_back_kernel(
    shard, spot, second_grad, scaled1, inverses, own_enc, far_enc, keys, values, query, mixed, probs, inverse,
    self_mixed, pack0, pack1, pack2, pack3, cols, late,
    first_grad, self_mixed_grad, own_part, far_part, out0, out1,
    so_plain, q_plain, k_plain, v_plain, o_plain, accs, sums, sheet,
    key_acc, value_acc, kept, grad, inner, query_grad,
):
    seq, step = pl.program_id(0), pl.program_id(1)
    rows = shard
    first_step = (seq == 0) & (step == 0)
    last_step = (seq == pl.num_programs(0) - 1) & (step == pl.num_programs(1) - 1)
    local = own_enc.shape[1]
    parts = far_enc.shape[0] + 1

    @pl.when(first_step)
    def _():
        for which, plain in enumerate((so_plain, q_plain, k_plain, v_plain, o_plain)):
            unpack((pack0, pack1, pack2, pack3), spot, which * rows, rows, plain)
        accs[...] = jnp.zeros_like(accs)
        sums[...] = jnp.zeros_like(sums)

    @pl.when(step == 0)
    def _():
        key_acc[...] = jnp.zeros_like(key_acc)
        value_acc[...] = jnp.zeros_like(value_acc)

    cross_low = second_grad[0].astype(BF16)
    scale_grad(dot(o_plain[...], cross_low), mixed.at[0], inverse.at[0, 0], grad, inner)
    accs[4] += dot(mixed[0], cross_low, NT)
    attend_back(
        parts * local // BLK, keys.at[0], values.at[0], 0, query.at[0], grad, inner, probs.at[0, 0],
        kept, query_grad, key_acc, value_acc,
    )
    scaled = scaled1[0]
    gain = cols[:, 0:1]
    normed_low = (scaled * gain + cols[:, 1:2]).astype(BF16)
    accs[1] += dot(normed_low, query_grad[...], NT)
    normed_grad = second_grad[0] + dot(q_plain[...], query_grad[...])
    sums[0] += fold(normed_grad * scaled)
    sums[1] += fold(normed_grad)
    through = norm_back(scaled, inverses[0, 0, 0:1, :], gain, normed_grad)
    first_grad[0] = through
    self_low = through.astype(BF16)
    accs[0] += dot(self_mixed[0], self_low, NT)
    self_mixed_grad[0] = dot(so_plain[...], self_low).astype(BF16)

    @pl.when(step == pl.num_programs(1) - 1)
    def _():
        for part in range(parts):
            at = slice(part * local, (part + 1) * local)
            key_low = (key_acc[:, at] * LN2).astype(BF16)
            value_low = value_acc[:, at].astype(BF16)
            turned = (own_enc[0] if part == 0 else far_enc[part - 1, 0]).T
            accs[2] += dot(turned, key_low, NT)
            accs[3] += dot(turned, value_low, NT)
            whole = (dot(k_plain[...], key_low) + dot(v_plain[...], value_low)).T
            if part == 0:
                own_part[0] = whole
            else:
                far_part[part - 1, 0] = whole.astype(BF16)

    @pl.when(last_step)
    def _():
        for y in range(2):
            outs = (out0.at[y], out1.at[y])
            for which in range(5):
                send_grad(outs, spot, which * rows, rows, accs.at[which], (2 * y, 2 * y + 1))
        sheet[...] = jnp.zeros_like(sheet)
        for which in range(2):
            sheet[:, 5 + which : 6 + which] = jnp.sum(sums[which], axis=1, keepdims=True)
        tray = (sheet[...].T[0:16, :] + late[...]).astype(BF16)
        for out in (out0, out1):
            for y in range(2):
                for d in range(out.shape[1]):
                    out[y, d, 5 * rows : 5 * rows + 16, :] = tray


def self_back_kernel(
    shard, seqs, docs, spot, hidden, first_grad, own_tokens, far_tokens, keys, values, query, mixed, probs,
    inverse, mixed_grad, pack0, pack1, pack2, pack3, hidden_grad, own_part, *refs,
):
    far_parts, refs = refs[:seqs], refs[seqs:]
    out0, out1, accs, q_plain, k_plain, v_plain, key_acc, value_acc, kept, grad, inner, query_grad = refs
    seq, step = pl.program_id(0), pl.program_id(1)
    steps = pl.num_programs(1)
    rows = shard
    local = own_tokens.shape[1]
    far = far_tokens.shape[2]
    parts = far_tokens.shape[0] + 1
    me = spot[0]
    block_count = parts * steps * (hidden.shape[1] // BLK)

    @pl.when((seq == 0) & (step == 0))
    def _():
        for which, plain in enumerate((q_plain, k_plain, v_plain)):
            unpack((pack0, pack1, pack2, pack3), spot, which * rows, rows, plain)
        accs[...] = jnp.zeros_like(accs)

    @pl.when(step == 0)
    def _():
        key_acc[...] = jnp.zeros_like(key_acc)
        value_acc[...] = jnp.zeros_like(value_acc)

    subs = hidden.shape[1] // BLK
    for part in range(subs):
        ts = slice(part * BLK, (part + 1) * BLK)
        scale_grad(
            mixed_grad[0, :, ts].astype(F32), mixed.at[0, :, ts], inverse.at[0, part], grad.at[:, ts],
            inner.at[:, ts],
        )
    for part in range(subs):
        ts = slice(part * BLK, (part + 1) * BLK)
        low, count = doc_span(docs, seq, (me * steps + step) * subs + part, block_count)
        off = pl.multiple_of(low * BLK, BLK)
        for size in range(1, WINDOW + 1):

            @pl.when(count == size)
            def _(size=size, part=part, ts=ts, off=off):
                attend_back(
                    size, keys.at[0], values.at[0], off, query.at[0, :, ts], grad.at[:, ts], inner.at[:, ts],
                    probs.at[0, part], kept, query_grad.at[:, ts], key_acc, value_acc,
                )

    accs[0] += dot(hidden[0].T, query_grad[...], NT)
    hidden_grad[0] = (first_grad[0] + dot(q_plain[...], query_grad[...])).T

    @pl.when(step == steps - 1)
    def _():
        for part in range(parts):
            at = token_window(me, part, parts, local, far)
            key_low = (key_acc[:, at] * LN2).astype(BF16)
            value_low = value_acc[:, at].astype(BF16)
            turned = (own_tokens[0] if part == 0 else far_tokens[part - 1, 0]).T
            accs[1] += dot(turned, key_low, NT)
            accs[2] += dot(turned, value_low, NT)
            whole = (dot(k_plain[...], key_low) + dot(v_plain[...], value_low)).T
            if part == 0:
                own_part[0] = whole
            else:
                whole = whole.astype(BF16)
                for s in range(seqs):

                    @pl.when(seq == s)
                    def _(s=s, whole=whole, part=part):
                        far_parts[s][part - 1] = whole

    @pl.when((seq == pl.num_programs(0) - 1) & (step == steps - 1))
    def _():
        for y in range(2):
            outs = (out0.at[y], out1.at[y])
            for which in range(3):
                send_grad(outs, spot, which * rows, rows, accs.at[which], (2 * y, 2 * y + 1))


def settle_kernel(spot, own, far, out):
    out[...] = own[...] + far[...].astype(F32)


def sum_kernel(*refs):
    for d, out in enumerate(refs[4:]):
        total = refs[0][d].astype(F32)
        for ref in refs[1:4]:
            total = total + ref[d].astype(F32)
        out[...] = total.astype(out.dtype)


def whole_spec():
    return pl.BlockSpec(memory_space=pltpu.VMEM)


def call(body, grid, scalars, in_specs, out_specs, out_shape, scratch, micros, args, aliases={}):
    return pl.pallas_call(
        body,
        grid_spec=pltpu.PrefetchScalarGridSpec(
            num_scalar_prefetch=scalars,
            grid=grid,
            in_specs=in_specs,
            out_specs=out_specs,
            scratch_shapes=scratch,
        ),
        out_shape=[jax.ShapeDtypeStruct(shape, kind) for shape, kind in out_shape],
        input_output_aliases=aliases,
        compiler_params=pltpu.CompilerParams(vmem_limit_bytes=VMEM_LIMIT),
        cost_estimate=pl.CostEstimate(flops=int(micros * 1e9), bytes_accessed=2**24, transcendentals=0),
    )(*args)


def shift(array, axis, by, size):
    return lax.ppermute(array, axis, [((i + by) % size, i) for i in range(size)])


def z_shift(array, by, depth):
    pairs = [(((z + by) % depth) * 4 + w, z * 4 + w) for z in range(depth) for w in range(4)]
    return lax.ppermute(array, "fsdp", pairs)


def w_flip(array, mask, depth):
    return lax.ppermute(array, "fsdp", [(z * 4 + (w ^ mask), z * 4 + w) for z in range(depth) for w in range(4)])


def together(*arrays):
    return lax.optimization_barrier(arrays)


def after(array, *earlier):
    return lax.optimization_barrier((array,) + earlier)[0]


def gather_stack(packed, got):
    return jnp.stack([packed] + got)


def gather_z(packed, depth):
    return gather_stack(packed, [z_shift(packed, d, depth) for d in range(1, depth)])


def gather_w(pieces, depth):
    across = w_flip(pieces, 2, depth)
    return [pieces, w_flip(pieces, 1, depth), across, w_flip(across, 1, depth)]


def swap_w(outs, depth):
    return [w_flip(outs[m], m, depth) for m in (1, 2, 3)]


def swap_z(pieces, depth):
    return [z_shift(pieces[d].astype(BF16), -d, depth) for d in range(1, depth)]


def add_w(own, got, depth):
    return [sum(piece[d].astype(F32) for piece in [own] + got) for d in range(depth)]


def swap_sp(total, sp):
    mine = total.astype(BF16)
    return [shift(mine, "sp", r, sp) for r in range(1, sp)]


def add_all(total, got):
    return sum((piece.astype(F32) for piece in got), total)


def on_device(sp, fsdp, *arrays):
    (
        hidden_in, token_stream, encoder_out, out_grad, doc_ids, key_order, context_size,
        self_query, self_key, self_value, self_output, cross_query, cross_key, cross_value, cross_output,
        inner_weight, inner_bias, outer_weight, outer_bias, first_gain, first_shift, second_gain,
        second_shift, third_gain, third_shift,
    ) = arrays
    seqs, local, width = hidden_in.shape
    enc_local = encoder_out.shape[1]
    shard, hidden_width = inner_weight.shape
    outer_rows = outer_weight.shape[0]
    bias_rows = inner_bias.shape[0]
    chunks = hidden_width // width
    span = min(local, 2 * BLK)
    subs = span // BLK
    steps = local // span
    heads = width // HD
    length = local * sp
    enc_len = enc_local * sp
    block_count = key_order.shape[1]
    depth = fsdp // 4
    tray = 16
    far = min(local, (WINDOW - 1) * BLK) if sp == 2 else local

    me, mine = lax.axis_index("sp"), lax.axis_index("fsdp")
    spot = jnp.stack([me, mine // 4, mine // 2 % 2, mine % 2]).astype(jnp.int32)

    pack_a = jnp.concatenate([self_query, self_key, self_value], axis=0)
    sent = token_stream
    if far != local:
        start = jnp.where(me == 0, local - far, 0)
        sent = lax.dynamic_slice(token_stream, (0, start, 0), (seqs, far, width))
    far_tokens = jnp.stack([shift(sent, "sp", r, sp) for r in range(1, sp)])
    vectors = (inner_bias, first_gain, first_shift, second_gain, second_shift, third_gain, third_shift, outer_bias)
    flat = jnp.concatenate(vectors)
    flat = jnp.pad(flat, (0, tray * width - flat.shape[0])).reshape(tray, width)
    pack_b = jnp.concatenate([self_output, cross_query, cross_key, cross_value, cross_output, flat], axis=0)
    pack_c = jnp.concatenate(jnp.split(inner_weight, chunks, axis=1) + [outer_weight], axis=0)

    pieces_a = gather_z(after(pack_a, sent), depth)
    pieces_b = gather_z(after(pack_b, pieces_a), depth)
    packs_a = gather_w(pieces_a, depth)
    hidden_early, pieces_b = together(hidden_in, pieces_b)
    core_b = w_flip(pieces_b, 1, depth)
    hidden_early, core_b = together(hidden_early, core_b)
    swap_b = w_flip(pieces_b, 2, depth)
    pack_c = after(pack_c, pieces_b, core_b, *packs_a)
    swap_c = [z_shift(pack_c, d, depth) for d in range(1, depth)]
    sent = after(encoder_out, far_tokens)
    far_enc = jnp.stack([shift(sent, "sp", r, sp) for r in range(1, sp)])

    whole = whole_spec()
    anywhere = pl.BlockSpec(memory_space=pl.ANY)
    turned_spec = lambda wide=span: pl.BlockSpec((1, width, wide), lambda s, i, *_: (s, 0, i))
    plain_spec = lambda wide=span: pl.BlockSpec((1, wide, width), lambda s, i, *_: (s, i, 0))
    per_seq = lambda shape: pl.BlockSpec((1,) + shape, lambda s, i, *_: (s, 0, 0))
    far_seq = lambda rows: pl.BlockSpec((sp - 1, 1, rows, width), lambda s, i, *_: (0, s, 0, 0))
    rows_spec = lambda count, wide: pl.BlockSpec((1, count, 8, wide), lambda s, i, *_: (s, i, 0, 0))
    probs_spec = lambda count, keys, wide: pl.BlockSpec(
        (1, count, heads, keys, wide), lambda s, i, *_: (s, i, 0, 0, 0)
    )
    half_rows = pl.BlockSpec((1, 1, 8, BLK), lambda s, i, *_: (s, i // subs, 0, i % subs))
    half_probs = pl.BlockSpec(
        (1, 1, heads, enc_len, BLK), lambda s, i, *_: (s, i // subs, 0, 0, i % subs)
    )
    turned_shape = (seqs, width, local)
    rows_shape = (seqs, steps, 8, span)
    self_rows_shape = (seqs, steps * subs, 8, BLK)
    big = lambda a, b, kind: pltpu.VMEM((a, b), kind)
    square = big(width, width, BF16)
    window = WINDOW * BLK

    keys, values, query, mixed, probs, inverse = call(
        functools.partial(self_forward_kernel, shard),
        (seqs, steps), 2,
        [
            plain_spec(), per_seq((local, width)), far_seq(far), per_seq((block_count, BLK)),
            per_seq((block_count, BLK)),
        ] + [whole] * 4,
        [
            per_seq((width, length)), per_seq((width, length)), turned_spec(), turned_spec(),
            probs_spec(subs, window, BLK), rows_spec(subs, BLK),
        ],
        [
            ((seqs, width, length), BF16), ((seqs, width, length), BF16), (turned_shape, BF16),
            (turned_shape, BF16), ((seqs, steps * subs, heads, window, BLK), BF16), (self_rows_shape, F32),
        ],
        [pltpu.VMEM((3, width, width), BF16)] + [square] * 3 + [pltpu.VMEM((subs, window, BLK), F32), big(heads, 128, F32)],
        32000.0,
        (doc_ids, spot, hidden_early, token_stream, far_tokens, key_order, context_size, *packs_a),
    )
    keys, values, query, mixed, probs, inverse, pieces_b, far_enc, swap_b, *swap_c = together(
        keys, values, query, mixed, probs, inverse, pieces_b, far_enc, swap_b, *swap_c
    )
    packs_b = [pieces_b, core_b, swap_b, w_flip(swap_b, 1, depth)]
    pieces_c = jnp.stack([pack_c] + swap_c)
    mixed, pieces_c = together(mixed, pieces_c)
    swap_c, core_c = w_flip(pieces_c, 2, depth), w_flip(pieces_c, 1, depth)

    (
        cross_keys, cross_values, cross_q, cross_mixed, cross_probs, cross_inverse, scaled1, scaled2, inverses,
        cols, inner_bias_col,
    ) = call(
        functools.partial(cross_forward_kernel, shard, bias_rows),
        (seqs, steps), 1,
        [plain_spec(), turned_spec(), per_seq((enc_local, width)), far_seq(enc_local)] + [whole] * 4,
        [
            per_seq((width, enc_len)), per_seq((width, enc_len)), turned_spec(), turned_spec(),
            probs_spec(1, enc_len, span), rows_spec(1, span), turned_spec(), turned_spec(), rows_spec(1, span),
            whole, whole,
        ],
        [
            ((seqs, width, enc_len), BF16), ((seqs, width, enc_len), BF16), (turned_shape, BF16),
            (turned_shape, BF16), ((seqs, steps, heads, enc_len, span), BF16), (rows_shape, F32),
            (turned_shape, F32), (turned_shape, F32), (rows_shape, F32), ((width, 8), F32),
            ((hidden_width, 1), F32),
        ],
        [pltpu.VMEM((5, width, width), BF16), big(fsdp, width, F32)] + [square] * 5 + [big(heads, 128, F32)],
        32000.0,
        (spot, hidden_in, mixed, encoder_out, far_enc, *packs_b),
    )

    (
        cross_keys, cross_values, cross_q, cross_mixed, cross_probs, cross_inverse, scaled1, scaled2, inverses,
        cols, inner_bias_col, pieces_c, swap_c, core_c,
    ) = together(
        cross_keys, cross_values, cross_q, cross_mixed, cross_probs, cross_inverse, scaled1, scaled2, inverses,
        cols, inner_bias_col, pieces_c, swap_c, core_c,
    )
    packs_c = [pieces_c, core_c, swap_c, w_flip(swap_c, 1, depth)]

    grads_shape = lambda rows: [((depth, rows, width), BF16)] * 4
    ff_rows = chunks * shard + outer_rows
    second_grad, layer_out, *ff_outs, late = call(
        functools.partial(feed_forward_kernel, shard, outer_rows),
        (seqs, steps), 1,
        [turned_spec(), rows_spec(1, span), plain_spec()] + [whole] * 6,
        [turned_spec(), plain_spec()] + [whole] * 5,
        [(turned_shape, F32), ((seqs, local, width), F32)] + grads_shape(ff_rows) + [((16, width), F32)],
        [
            big(width, hidden_width, BF16), big(hidden_width, width, BF16), big(hidden_width, width, BF16),
            big(width, hidden_width, BF16), big(width, hidden_width, F32), big(hidden_width, width, F32),
            pltpu.VMEM((5, width, 128), F32), big(hidden_width, 128, F32), big(hidden_width, span, BF16),
            big(width, 128, F32),
        ],
        70000.0,
        (spot, scaled2, inverses, out_grad, *packs_c, cols, inner_bias_col),
    )

    ff_swap = swap_w(ff_outs, depth)
    attention_scratch = lambda keys_len, kept_len: [
        big(width, keys_len, F32), big(width, keys_len, F32), pltpu.VMEM((heads, kept_len, BLK), BF16),
        big(width, BLK, BF16), big(heads, BLK, F32), big(width, BLK, BF16),
    ]
    first_grad, mixed_grad, own_enc_part, far_enc_part, *cross_outs = call(
        functools.partial(cross_back_kernel, shard),
        (seqs, steps * subs), 1,
        [
            turned_spec(BLK), turned_spec(BLK), half_rows, per_seq((enc_local, width)), far_seq(enc_local),
            per_seq((width, enc_len)), per_seq((width, enc_len)), turned_spec(BLK), turned_spec(BLK),
            half_probs, half_rows, turned_spec(BLK),
        ] + [whole] * 6,
        [
            turned_spec(BLK), turned_spec(BLK), per_seq((enc_local, width)), far_seq(enc_local),
        ] + [whole] * 2,
        [
            (turned_shape, F32), (turned_shape, BF16), ((seqs, enc_local, width), F32),
            ((sp - 1, seqs, enc_local, width), BF16),
        ] + [((2, depth, 5 * shard + tray, width), BF16)] * 2,
        [square] * 5
        + [pltpu.VMEM((5, width, width), F32), pltpu.VMEM((2, width, 128), F32), big(width, 128, F32)]
        + attention_scratch(enc_len, enc_len),
        56000.0,
        (
            spot, second_grad, scaled1, inverses, encoder_out, far_enc, cross_keys, cross_values, cross_q,
            cross_mixed, cross_probs, cross_inverse, mixed, *packs_b, cols, late,
        ),
    )

    first_grad, mixed_grad, own_enc_part, far_enc_part, *got = together(
        first_grad, mixed_grad, own_enc_part, far_enc_part, *cross_outs, *ff_swap
    )
    cross_outs, ff_swap = got[:2], got[2:]
    cross_core = w_flip(cross_outs[1], 1, depth)
    cut_rows = ff_rows // 4
    ff_pieces = call(
        sum_kernel, (4,), 0,
        [pl.BlockSpec((depth, cut_rows, width), lambda i: (0, i, 0))] * 4,
        [pl.BlockSpec((cut_rows, width), lambda i: (i, 0))] * depth,
        [((ff_rows, width), F32)] + [((ff_rows, width), BF16)] * (depth - 1), [], 2000.0, (ff_outs[0], *ff_swap),
    )
    cross_half = [cross_outs[0][y].astype(F32) + cross_core[y].astype(F32) for y in range(2)]
    mixed_grad, *got = together(mixed_grad, *cross_half, *ff_pieces)
    cross_half, ff_pieces = got[:2], got[2:]
    ff_swap = swap_z(ff_pieces, depth)
    enc_swap = [shift(far_enc_part[r - 1], "sp", -r, sp) for r in range(1, sp)]
    cross_swap = w_flip(cross_half[1].astype(BF16), 2, depth)
    hidden_grad, token_grad, *rest = call(
        functools.partial(self_back_kernel, shard, seqs),
        (seqs, steps * subs), 2,
        [
            plain_spec(BLK), turned_spec(BLK), per_seq((local, width)), far_seq(far),
            per_seq((width, length)), per_seq((width, length)), turned_spec(BLK), turned_spec(BLK),
            probs_spec(1, window, BLK), rows_spec(1, BLK), turned_spec(BLK),
        ] + [whole] * 4,
        [plain_spec(BLK), per_seq((local, width))] + [whole] * (seqs + 2),
        [((seqs, local, width), F32)] * 2 + [((sp - 1, far, width), BF16)] * seqs
        + [((2, depth, 3 * shard, width), BF16)] * 2,
        [pltpu.VMEM((3, width, width), F32)] + [square] * 3 + attention_scratch(length, window),
        50000.0,
        (
            doc_ids, spot, hidden_in, first_grad, token_stream, far_tokens, keys, values, query, mixed,
            probs, inverse, mixed_grad, *packs_a,
        ),
    )
    far_parts, self_outs = rest[:seqs], rest[seqs:]
    count = len(ff_swap)
    hidden_grad, token_grad, own_half, far_half, cross_swap, *got = together(
        hidden_grad, token_grad, *self_outs, cross_swap, *far_parts, *ff_swap, *enc_swap
    )
    far_parts, ff_got, enc_swap = got[:seqs], got[seqs : seqs + count], got[seqs + count :]
    send_back = lambda parts: [shift(parts[r - 1], "sp", -r, sp) for r in range(1, sp)]
    token_swap = [send_back(far_parts[0])]
    self_got = w_flip(far_half, 1, depth)
    self_half = [own_half[y].astype(F32) + self_got[y].astype(F32) for y in range(2)]
    self_swap = w_flip(self_half[1].astype(BF16), 2, depth)
    cross_half[0], cross_swap, ff_first, enc_first, *_ = together(
        cross_half[0], cross_swap, ff_pieces[0], own_enc_part, *self_half
    )
    cross_pieces = [cross_half[0][d] + cross_swap[d].astype(F32) for d in range(depth)]
    cross_got = swap_z(cross_pieces, depth)
    ff_sum = add_all(ff_first, ff_got)
    count = len(cross_got)
    self_swap, *got = together(self_swap, *cross_got, *token_swap[0])
    cross_got, token_swap[0] = got[:count], got[count:]
    self_pieces = [self_half[0][d] + self_swap[d].astype(F32) for d in range(depth)]
    for s in range(1, seqs):
        token_swap.append(send_back([after(far_parts[s], *token_swap[-1])[r] for r in range(sp - 1)]))
    self_more = swap_z(self_pieces, depth)
    ff_sp = swap_sp(after(ff_sum, self_swap), sp)
    cross_first = after(cross_pieces[0], *self_more)
    self_sum = add_all(self_pieces[0], self_more)
    self_sp = swap_sp(self_sum, sp)
    cross_sum = add_all(cross_first, cross_got)
    cross_sp = swap_sp(cross_sum, sp)

    shift_back = (local - far) // BLK
    for s in range(seqs):
        for piece in token_swap[s]:
            spec = pl.BlockSpec(
                (1, BLK, width), lambda i, spot, s=s: (s, i + jnp.where(spot[0] == 0, shift_back, 0), 0)
            )
            (token_grad,) = call(
                settle_kernel, (far // BLK,), 1,
                [spec, pl.BlockSpec((1, BLK, width), lambda i, spot: (0, i, 0))],
                [spec], [((seqs, local, width), F32)], [], 3000.0, (spot, token_grad, piece[None]), {1: 0},
            )
    encoder_grad = enc_first
    for r in range(1, sp):
        encoder_grad = encoder_grad + enc_swap[r - 1].astype(F32)

    ff_total = add_all(ff_sum, ff_sp)
    cross_total = add_all(cross_sum, cross_sp)
    self_total = add_all(self_sum, self_sp)
    inner_total = jnp.concatenate([ff_total[c * shard : (c + 1) * shard] for c in range(chunks)], axis=1)
    outer_total = ff_total[chunks * shard :]
    small = cross_total[5 * shard :]
    cut = lambda total, k: total[k * shard : (k + 1) * shard]
    vec = lambda k: lax.dynamic_slice(small, (k, mine * shard), (1, shard))[0]
    bias_total = lax.dynamic_slice(small[8 : 8 + chunks].reshape(-1), (mine * bias_rows,), (bias_rows,))
    return (
        layer_out, hidden_grad, token_grad, encoder_grad,
        cut(self_total, 0), cut(self_total, 1), cut(self_total, 2), cut(cross_total, 0),
        cut(cross_total, 1), cut(cross_total, 2), cut(cross_total, 3), cut(cross_total, 4),
        inner_total, bias_total, outer_total, vec(4), vec(5), vec(6), vec(0), vec(1), vec(2), vec(3),
    )


def solution(mesh):
    tokens, table, vector = P("fsdp", "sp", None), P("fsdp", None), P("fsdp")
    order = P("fsdp", None, None)
    return jax.shard_map(
        functools.partial(on_device, mesh.shape["sp"], mesh.shape["fsdp"]),
        mesh=mesh,
        in_specs=(tokens,) * 4
        + (table, order, order)
        + (table,) * 9
        + (vector, table)
        + (vector,) * 7,
        out_specs=(tokens,) * 4 + (table,) * 9 + (vector, table) + (vector,) * 7,
        check_vma=False,
    )
```

```python
import functools
import math

import jax
import jax.numpy as jnp
from jax import lax
from jax.experimental import pallas as pl
from jax.experimental.pallas import tpu as pltpu
from jax.sharding import PartitionSpec as P

HD = 64
BLK = 256
WINDOW = 4
EPS = 1e-05
MASKED = -1e30
LOG2E = 1.4426950408889634
LN2 = 0.6931471805599453
SAFE = 60.0
F32 = jnp.float32
BF16 = jnp.bfloat16
NN = (((1,), (0,)), ((), ()))
NT = (((1,), (1,)), ((), ()))
TN = (((0,), (0,)), ((), ()))
VMEM_LIMIT = 62 * 2**20


def dot(left, right, form=NN):
    return lax.dot_general(left, right, form, preferred_element_type=F32)


def norm(rows):
    center = rows - jnp.mean(rows, axis=0, keepdims=True)
    inverse = lax.rsqrt(jnp.mean(center * center, axis=0, keepdims=True) + EPS)
    return center * inverse, inverse


def norm_back(scaled, inverse, gain, upstream):
    through = upstream * gain
    return inverse * (
        through
        - jnp.mean(through, axis=0, keepdims=True)
        - scaled * jnp.mean(through * scaled, axis=0, keepdims=True)
    )


def fold(values):
    total = values[:, :128]
    for start in range(128, values.shape[1], 128):
        total = total + values[:, start : start + 128]
    return total


def gelu_pair(x):
    phi = 0.5 + 0.5 * lax.erf(x * math.sqrt(0.5))
    bell = jnp.exp2((-0.5 * LOG2E) * (x * x))
    return x * phi, phi + x * bell * (1.0 / math.sqrt(2.0 * math.pi))


def owner_of(spot, m, d, depth):
    z = lax.rem(spot[1] + d, depth)
    return (z * 2 + jnp.bitwise_xor(spot[2], m // 2)) * 2 + jnp.bitwise_xor(spot[3], m % 2)


def unpack(packs, spot, first, rows, plain):
    for m, pack in enumerate(packs):
        depth = pack.shape[0]
        for d in range(depth):
            at = pl.ds(pl.multiple_of(owner_of(spot, m, d, depth) * rows, rows), rows)
            plain[at, :] = pack[d, first : first + rows, :]


def send_grad(outs, spot, first, rows, acc, masks=(0, 1, 2, 3)):
    depth = outs[0].shape[0]
    for out, m in zip(outs, masks):
        for d in range(depth):
            at = pl.ds(pl.multiple_of(owner_of(spot, m, d, depth) * rows, rows), rows)
            out[d, first : first + rows, :] = acc[at, :].astype(BF16)


def attend(count, exact, keys, values, off, query, probs, mixed, inverse, bias):
    head_count, span = query.shape[0] // HD, query.shape[1]

    def scores(hs, j):
        part = dot(keys[hs, pl.ds(off + j * BLK, BLK)], query[hs, :], TN)
        if bias is not None:
            part = part + bias[j * BLK : (j + 1) * BLK, :]
        return part

    def first(h, hs):
        total = None
        if exact:
            parts = [scores(hs, j) for j in range(count)]
            top = jnp.max(parts[0], axis=0, keepdims=True)
            for part in parts[1:]:
                top = jnp.maximum(top, jnp.max(part, axis=0, keepdims=True))
        for j in range(count):
            terms = jnp.exp2(parts[j] - top if exact else scores(hs, j))
            partial = jnp.sum(terms.reshape(BLK // 8, 8, span), axis=0)
            total = partial if total is None else total + partial
            probs[h, j * BLK : (j + 1) * BLK, :] = terms.astype(BF16)
        return total

    def second(h, hs, total):
        sums = dot(values[hs, pl.ds(off, count * BLK)], probs[h, : count * BLK, :])
        scale = 1.0 / jnp.sum(total, axis=0, keepdims=True)
        mixed[hs, :] = (sums * scale).astype(BF16)
        inverse[pl.ds(h, 1), :] = scale

    if exact:

        def one(h, carry):
            hs = pl.ds(pl.multiple_of(h * HD, HD), HD)
            second(h, hs, first(h, hs))
            return carry

        lax.fori_loop(0, head_count, one, 0)
        return
    waiting = None
    for h in range(head_count):
        total = first(h, slice(h * HD, (h + 1) * HD))
        if h > 0:
            second(h - 1, slice((h - 1) * HD, h * HD), waiting)
        waiting = total
    second(head_count - 1, slice((head_count - 1) * HD, head_count * HD), waiting)


def attend_back(
    count, keys, values, off, query, grad, inner, probs, kept, query_grad, key_grad, value_grad
):
    head_count = query.shape[0] // HD

    def first(h):
        hs = slice(h * HD, (h + 1) * HD)
        for j in range(count):
            us = slice(j * BLK, (j + 1) * BLK)
            prob_grad = dot(values[hs, pl.ds(off + j * BLK, BLK)], grad[hs, :], TN)
            change = probs[h, us, :].astype(F32) * (prob_grad - inner[h : h + 1, :])
            kept[h, us, :] = change.astype(BF16)

    def second(h):
        hs = slice(h * HD, (h + 1) * HD)
        us = slice(0, count * BLK)
        window = pl.ds(off, count * BLK)
        query_grad[hs, :] = (dot(keys[hs, window], kept[h, us, :]) * (1.0 / math.sqrt(HD))).astype(BF16)
        key_grad[hs, window] += dot(query[hs, :], kept[h, us, :], NT)
        value_grad[hs, window] += dot(grad[hs, :], probs[h, us, :], NT)

    first(0)
    for h in range(1, head_count):
        first(h)
        second(h - 1)
    second(head_count - 1)


def scale_grad(mixed_grad, mixed, inverse, grad, inner):
    for h in range(mixed.shape[0] // HD):
        hs = slice(h * HD, (h + 1) * HD)
        scaled = mixed_grad[hs, :] * inverse[h : h + 1, :]
        grad[hs, :] = scaled.astype(BF16)
        inner[h : h + 1, :] = jnp.sum(scaled * mixed[hs, :].astype(F32), axis=0, keepdims=True)


def head_norms(rows, head_count):
    found = []
    for h in range(head_count):
        part = rows[h * HD : (h + 1) * HD, :].astype(F32)
        found.append(jnp.max(jnp.sum(part * part, axis=0, keepdims=True), axis=1, keepdims=True))
    return found


def safe_scores(query, key_norms):
    head_count = query.shape[0] // HD
    worst = None
    for h, found in enumerate(head_norms(query[...], head_count)):
        product = found * key_norms[h : h + 1, 0:1]
        worst = product if worst is None else jnp.maximum(worst, product)
    return jnp.max(worst) < SAFE * SAFE


def store_key_norms(key_norms, keys):
    head_count = keys.shape[0] // HD
    for h, found in enumerate(head_norms(keys[...], head_count)):
        key_norms[h : h + 1, :] = jnp.broadcast_to(found, (1, key_norms.shape[1]))


def doc_span(docs, seq, block, block_count):
    mine = docs[seq, block]
    low = jnp.int32(0)
    count = jnp.int32(0)
    for b in range(block_count):
        low = low + jnp.where(docs[seq, b] < mine, 1, 0).astype(jnp.int32)
        count = count + jnp.where(docs[seq, b] == mine, 1, 0).astype(jnp.int32)
    return low, count


def self_forward_kernel(
    shard, docs, spot, hidden, own_tokens, far_tokens, order, reach, pack0, pack1, pack2, pack3,
    keys, values, query, mixed, probs, inverse,
    plain, q_turned, k_turned, v_turned, bias, key_norms,
):
    seq, step = pl.program_id(0), pl.program_id(1)
    steps = pl.num_programs(1)
    rows = shard
    local = own_tokens.shape[1]
    far = far_tokens.shape[2]
    parts = far_tokens.shape[0] + 1
    block_count = order.shape[1]
    me = spot[0]

    @pl.when((seq == 0) & (step == 0))
    def _():
        for which, turned in enumerate((q_turned, k_turned, v_turned)):
            unpack((pack0, pack1, pack2, pack3), spot, which * rows, rows, plain.at[which])
            turned[...] = plain[which].T

    @pl.when(step == 0)
    def _():
        if far != local:
            keys[...] = jnp.zeros_like(keys)
        for part in range(parts):
            tokens = own_tokens[0] if part == 0 else far_tokens[part - 1, 0]
            at = token_window(me, part, parts, local, far)
            turned = tokens.T
            keys[0, :, at] = dot(k_turned[...], turned).astype(BF16)
            values[0, :, at] = dot(v_turned[...], turned).astype(BF16)
        store_key_norms(key_norms, keys.at[0])

    query[0] = (dot(q_turned[...], hidden[0].T) * (LOG2E / math.sqrt(HD))).astype(BF16)
    safe = safe_scores(query.at[0], key_norms)
    order_turned = order[0].astype(F32).T
    lanes = lax.broadcasted_iota(jnp.int32, order_turned.shape, 1)
    differ = lax.broadcasted_iota(jnp.int32, (BLK, BLK), 0) != lax.broadcasted_iota(
        jnp.int32, (BLK, BLK), 1
    )
    subs = hidden.shape[1] // BLK
    for part in range(subs):
        block = (me * steps + step) * subs + part
        low, count = doc_span(docs, seq, block, block_count)
        reach_row = reach[0, pl.ds(block, 1), :].astype(F32)
        for j in range(WINDOW):
            at = low + j
            column = jnp.sum(jnp.where(lanes == at, order_turned, 0.0), axis=1, keepdims=True)
            seen = (column < reach_row) & (differ | (at != block))
            bias[part, j * BLK : (j + 1) * BLK, :] = jnp.where(seen, 0.0, MASKED)
        off = pl.multiple_of(low * BLK, BLK)
        ts = slice(part * BLK, (part + 1) * BLK)
        for size in range(1, WINDOW + 1):
            for exact in (False, True):

                @pl.when((count == size) & (safe != exact))
                def _(size=size, exact=exact, part=part, off=off, ts=ts):
                    attend(
                        size, exact, keys.at[0], values.at[0], off, query.at[0, :, ts], probs.at[0, part],
                        mixed.at[0, :, ts], inverse.at[0, part], bias.at[part],
                    )


def token_window(me, part, parts, local, far):
    owner = lax.rem(me + part, parts)
    if part == 0 or far == local:
        return pl.ds(pl.multiple_of(owner * local, BLK), local)
    return pl.ds(pl.multiple_of(owner * local + jnp.where(owner == 0, local - far, 0), BLK), far)


def cross_forward_kernel(
    shard, bias_rows, spot, hidden, self_mixed, own_enc, far_enc, pack0, pack1, pack2, pack3,
    keys, values, query, mixed, probs, inverse, scaled1, scaled2, inverses, cols, bias_col,
    plain, spread_rows, so_turned, q_turned, k_turned, v_turned, o_turned, key_norms,
):
    seq, step = pl.program_id(0), pl.program_id(1)
    rows = shard
    local = own_enc.shape[1]
    parts = far_enc.shape[0] + 1
    packs = (pack0, pack1, pack2, pack3)

    @pl.when((seq == 0) & (step == 0))
    def _():
        for which, turned in enumerate((so_turned, q_turned, k_turned, v_turned, o_turned)):
            unpack(packs, spot, which * rows, rows, plain.at[which])
            turned[...] = plain[which].T
        depth = pack0.shape[0]
        for m, pack in enumerate(packs):
            for d in range(depth):
                row = pack[d, 5 * rows : 5 * rows + 16, :].astype(F32)[0:1, :]
                spread_rows[pl.ds(owner_of(spot, m, d, depth), 1), :] = row
        spread = spread_rows[...].T
        count = 4 * depth
        bias_col[...] = jnp.concatenate([spread[:bias_rows, f : f + 1] for f in range(count)], axis=0)
        for v in range(7):
            at = slice(bias_rows + v * rows, bias_rows + (v + 1) * rows)
            cols[:, v : v + 1] = jnp.concatenate([spread[at, f : f + 1] for f in range(count)], axis=0)

    @pl.when(step == 0)
    def _():
        for part in range(parts):
            turned = (own_enc[0] if part == 0 else far_enc[part - 1, 0]).T
            at = slice(part * local, (part + 1) * local)
            keys[0, :, at] = dot(k_turned[...], turned).astype(BF16)
            values[0, :, at] = dot(v_turned[...], turned).astype(BF16)
        store_key_norms(key_norms, keys.at[0])

    center, inverse1 = norm(hidden[0].T.astype(F32) + dot(so_turned[...], self_mixed[0]))
    scaled1[0] = center
    normed = center * cols[:, 0:1] + cols[:, 1:2]
    query[0] = (dot(q_turned[...], normed.astype(BF16)) * (LOG2E / math.sqrt(HD))).astype(BF16)
    safe = safe_scores(query.at[0], key_norms)
    for exact in (False, True):

        @pl.when(safe != exact)
        def _(exact=exact):
            attend(
                parts * local // BLK, exact, keys.at[0], values.at[0], 0, query.at[0], probs.at[0, 0],
                mixed.at[0], inverse.at[0, 0], None,
            )

    normed = scaled1[0] * cols[:, 0:1] + cols[:, 1:2]
    center, inverse2 = norm(normed + dot(o_turned[...], mixed[0]))
    scaled2[0] = center
    inverses[0, 0, 0:1, :] = inverse1
    inverses[0, 0, 1:2, :] = inverse2


def feed_forward_kernel(
    shard, outer_rows, spot, scaled2_in, inverses, out_grad, pack0, pack1, pack2, pack3, cols, inner_bias,
    second_grad, layer_out, out0, out1, out2, out3, late,
    inner, inner_turned, outer, outer_turned, inner_acc, outer_acc, sums, bias_sum, slope, sheet,
):
    seq, step = pl.program_id(0), pl.program_id(1)
    rows = shard
    first_step = (seq == 0) & (step == 0)
    last_step = (seq == pl.num_programs(0) - 1) & (step == pl.num_programs(1) - 1)
    width = inner.shape[0]
    chunks = inner.shape[1] // width
    packs = (pack0, pack1, pack2, pack3)

    @pl.when(first_step)
    def _():
        for c in range(chunks):
            cs = slice(c * width, (c + 1) * width)
            unpack(packs, spot, c * rows, rows, inner.at[:, cs])
            inner_turned[cs, :] = inner[:, cs].T
        unpack(packs, spot, chunks * rows, outer_rows, outer)
        for c in range(chunks):
            cs = slice(c * width, (c + 1) * width)
            outer_turned[:, cs] = outer[cs, :].T
        inner_acc[...] = jnp.zeros_like(inner_acc)
        outer_acc[...] = jnp.zeros_like(outer_acc)
        sums[...] = jnp.zeros_like(sums)
        bias_sum[...] = jnp.zeros_like(bias_sum)

    scaled2 = scaled2_in[0]
    gain2 = cols[:, 2:3]
    middle = scaled2 * gain2 + cols[:, 3:4]
    middle_low = middle.astype(BF16)
    pre = dot(inner_turned[...], middle_low) + inner_bias[...]
    active, pull = gelu_pair(pre)
    active = active.astype(BF16)
    slope[...] = pull.astype(BF16)
    third_sum = middle + dot(outer_turned[...], active) + cols[:, 6:7]
    scaled3, inverse3 = norm(third_sum)
    gain3 = cols[:, 4:5]
    layer_out[0] = (scaled3 * gain3 + cols[:, 5:6]).T
    upstream = out_grad[0].T.astype(F32)
    third_grad = norm_back(scaled3, inverse3, gain3, upstream)
    sums[2] += fold(upstream * scaled3)
    sums[3] += fold(upstream)
    outer_low = third_grad.astype(BF16)
    sums[4] += fold(outer_low.astype(F32))
    outer_acc[...] += dot(active, outer_low, NT)
    inner_low = (dot(outer[...], outer_low) * slope[...].astype(F32)).astype(BF16)
    bias_sum[...] += fold(inner_low.astype(F32))
    inner_acc[...] += dot(middle_low, inner_low, NT)
    middle_grad = third_grad + dot(inner[...], inner_low)
    sums[0] += fold(middle_grad * scaled2)
    sums[1] += fold(middle_grad)
    second_grad[0] = norm_back(scaled2, inverses[0, 0, 1:2, :], gain2, middle_grad)

    @pl.when(last_step)
    def _():
        outs = (out0, out1, out2, out3)
        for c in range(chunks):
            send_grad(outs, spot, c * rows, rows, inner_acc.at[:, c * width : (c + 1) * width])
        send_grad(outs, spot, chunks * rows, outer_rows, outer_acc)
        sheet[...] = jnp.zeros_like(sheet)
        for which in range(5):
            sheet[:, which : which + 1] = jnp.sum(sums[which], axis=1, keepdims=True)
        for c in range(chunks):
            part = bias_sum[c * width : (c + 1) * width, :]
            sheet[:, 8 + c : 9 + c] = jnp.sum(part, axis=1, keepdims=True)
        late[...] = sheet[...].T[0:16, :]


def cross_back_kernel(
    shard, spot, second_grad, scaled1, inverses, own_enc, far_enc, keys, values, query, mixed, probs, inverse,
    self_mixed, pack0, pack1, pack2, pack3, cols, late,
    first_grad, self_mixed_grad, own_part, far_part, out0, out1,
    so_plain, q_plain, k_plain, v_plain, o_plain, accs, sums, sheet,
    key_acc, value_acc, kept, grad, inner, query_grad,
):
    seq, step = pl.program_id(0), pl.program_id(1)
    rows = shard
    first_step = (seq == 0) & (step == 0)
    last_step = (seq == pl.num_programs(0) - 1) & (step == pl.num_programs(1) - 1)
    local = own_enc.shape[1]
    parts = far_enc.shape[0] + 1

    @pl.when(first_step)
    def _():
        for which, plain in enumerate((so_plain, q_plain, k_plain, v_plain, o_plain)):
            unpack((pack0, pack1, pack2, pack3), spot, which * rows, rows, plain)
        accs[...] = jnp.zeros_like(accs)
        sums[...] = jnp.zeros_like(sums)

    @pl.when(step == 0)
    def _():
        key_acc[...] = jnp.zeros_like(key_acc)
        value_acc[...] = jnp.zeros_like(value_acc)

    cross_low = second_grad[0].astype(BF16)
    scale_grad(dot(o_plain[...], cross_low), mixed.at[0], inverse.at[0, 0], grad, inner)
    accs[4] += dot(mixed[0], cross_low, NT)
    attend_back(
        parts * local // BLK, keys.at[0], values.at[0], 0, query.at[0], grad, inner, probs.at[0, 0],
        kept, query_grad, key_acc, value_acc,
    )
    scaled = scaled1[0]
    gain = cols[:, 0:1]
    normed_low = (scaled * gain + cols[:, 1:2]).astype(BF16)
    accs[1] += dot(normed_low, query_grad[...], NT)
    normed_grad = second_grad[0] + dot(q_plain[...], query_grad[...])
    sums[0] += fold(normed_grad * scaled)
    sums[1] += fold(normed_grad)
    through = norm_back(scaled, inverses[0, 0, 0:1, :], gain, normed_grad)
    first_grad[0] = through
    self_low = through.astype(BF16)
    accs[0] += dot(self_mixed[0], self_low, NT)
    self_mixed_grad[0] = dot(so_plain[...], self_low).astype(BF16)

    @pl.when(step == pl.num_programs(1) - 1)
    def _():
        for part in range(parts):
            at = slice(part * local, (part + 1) * local)
            key_low = (key_acc[:, at] * LN2).astype(BF16)
            value_low = value_acc[:, at].astype(BF16)
            turned = (own_enc[0] if part == 0 else far_enc[part - 1, 0]).T
            accs[2] += dot(turned, key_low, NT)
            accs[3] += dot(turned, value_low, NT)
            whole = (dot(k_plain[...], key_low) + dot(v_plain[...], value_low)).T
            if part == 0:
                own_part[0] = whole
            else:
                far_part[part - 1, 0] = whole.astype(BF16)

    @pl.when(last_step)
    def _():
        for c in range(2):
            outs = (out0.at[c], out1.at[c])
            for which in range(5):
                send_grad(outs, spot, which * rows, rows, accs.at[which], (c, 2 + c))
        sheet[...] = jnp.zeros_like(sheet)
        for which in range(2):
            sheet[:, 5 + which : 6 + which] = jnp.sum(sums[which], axis=1, keepdims=True)
        tray = (sheet[...].T[0:16, :] + late[...]).astype(BF16)
        for out in (out0, out1):
            for c in range(2):
                for d in range(out.shape[1]):
                    out[c, d, 5 * rows : 5 * rows + 16, :] = tray


def self_back_kernel(
    shard, docs, spot, hidden, first_grad, own_tokens, far_tokens, keys, values, query, mixed, probs,
    inverse, mixed_grad, pack0, pack1, pack2, pack3, hidden_grad, own_part, far_part, out0, out1,
    accs, q_plain, k_plain, v_plain, key_acc, value_acc, kept, grad, inner, query_grad,
):
    seq, step = pl.program_id(0), pl.program_id(1)
    steps = pl.num_programs(1)
    rows = shard
    local = own_tokens.shape[1]
    far = far_tokens.shape[2]
    parts = far_tokens.shape[0] + 1
    me = spot[0]
    block_count = parts * steps * (hidden.shape[1] // BLK)

    @pl.when((seq == 0) & (step == 0))
    def _():
        for which, plain in enumerate((q_plain, k_plain, v_plain)):
            unpack((pack0, pack1, pack2, pack3), spot, which * rows, rows, plain)
        accs[...] = jnp.zeros_like(accs)

    @pl.when(step == 0)
    def _():
        key_acc[...] = jnp.zeros_like(key_acc)
        value_acc[...] = jnp.zeros_like(value_acc)

    subs = hidden.shape[1] // BLK
    for part in range(subs):
        ts = slice(part * BLK, (part + 1) * BLK)
        scale_grad(
            mixed_grad[0, :, ts].astype(F32), mixed.at[0, :, ts], inverse.at[0, part], grad.at[:, ts],
            inner.at[:, ts],
        )
    for part in range(subs):
        ts = slice(part * BLK, (part + 1) * BLK)
        low, count = doc_span(docs, seq, (me * steps + step) * subs + part, block_count)
        off = pl.multiple_of(low * BLK, BLK)
        for size in range(1, WINDOW + 1):

            @pl.when(count == size)
            def _(size=size, part=part, ts=ts, off=off):
                attend_back(
                    size, keys.at[0], values.at[0], off, query.at[0, :, ts], grad.at[:, ts], inner.at[:, ts],
                    probs.at[0, part], kept, query_grad.at[:, ts], key_acc, value_acc,
                )

    accs[0] += dot(hidden[0].T, query_grad[...], NT)
    hidden_grad[0] = (first_grad[0] + dot(q_plain[...], query_grad[...])).T

    @pl.when(step == steps - 1)
    def _():
        for part in range(parts):
            at = token_window(me, part, parts, local, far)
            key_low = (key_acc[:, at] * LN2).astype(BF16)
            value_low = value_acc[:, at].astype(BF16)
            turned = (own_tokens[0] if part == 0 else far_tokens[part - 1, 0]).T
            accs[1] += dot(turned, key_low, NT)
            accs[2] += dot(turned, value_low, NT)
            whole = (dot(k_plain[...], key_low) + dot(v_plain[...], value_low)).T
            if part == 0:
                own_part[0] = whole
            else:
                far_part[part - 1, 0] = whole.astype(BF16)

    @pl.when((seq == pl.num_programs(0) - 1) & (step == steps - 1))
    def _():
        for y in range(2):
            outs = (out0.at[y], out1.at[y])
            for which in range(3):
                send_grad(outs, spot, which * rows, rows, accs.at[which], (2 * y, 2 * y + 1))


def settle_kernel(spot, own, far, out):
    out[...] = own[...] + far[...].astype(F32)


def sum_kernel(*refs):
    for d, out in enumerate(refs[4:]):
        total = refs[0][d].astype(F32)
        for ref in refs[1:4]:
            total = total + ref[d].astype(F32)
        out[...] = total.astype(out.dtype)


def whole_spec():
    return pl.BlockSpec(memory_space=pltpu.VMEM)


def call(body, grid, scalars, in_specs, out_specs, out_shape, scratch, micros, args, aliases={}):
    return pl.pallas_call(
        body,
        grid_spec=pltpu.PrefetchScalarGridSpec(
            num_scalar_prefetch=scalars,
            grid=grid,
            in_specs=in_specs,
            out_specs=out_specs,
            scratch_shapes=scratch,
        ),
        out_shape=[jax.ShapeDtypeStruct(shape, kind) for shape, kind in out_shape],
        input_output_aliases=aliases,
        compiler_params=pltpu.CompilerParams(vmem_limit_bytes=VMEM_LIMIT),
        cost_estimate=pl.CostEstimate(flops=int(micros * 1e9), bytes_accessed=2**24, transcendentals=0),
    )(*args)


def shift(array, axis, by, size):
    return lax.ppermute(array, axis, [((i + by) % size, i) for i in range(size)])


def z_shift(array, by, depth):
    pairs = [(((z + by) % depth) * 4 + w, z * 4 + w) for z in range(depth) for w in range(4)]
    return lax.ppermute(array, "fsdp", pairs)


def w_flip(array, mask, depth):
    return lax.ppermute(array, "fsdp", [(z * 4 + (w ^ mask), z * 4 + w) for z in range(depth) for w in range(4)])


def together(*arrays):
    return lax.optimization_barrier(arrays)


def after(array, *earlier):
    return lax.optimization_barrier((array,) + earlier)[0]


def gather_stack(packed, got):
    return jnp.stack([packed] + got)


def gather_z(packed, depth):
    return gather_stack(packed, [z_shift(packed, d, depth) for d in range(1, depth)])


def gather_w(pieces, depth):
    across = w_flip(pieces, 2, depth)
    return [pieces, w_flip(pieces, 1, depth), across, w_flip(across, 1, depth)]


def swap_w(outs, depth):
    return [w_flip(outs[m], m, depth) for m in (1, 2, 3)]


def swap_z(pieces, depth):
    return [z_shift(pieces[d].astype(BF16), -d, depth) for d in range(1, depth)]


def add_w(own, got, depth):
    return [sum(piece[d].astype(F32) for piece in [own] + got) for d in range(depth)]


def swap_sp(total, sp):
    mine = total.astype(BF16)
    return [shift(mine, "sp", r, sp) for r in range(1, sp)]


def add_all(total, got):
    return sum((piece.astype(F32) for piece in got), total)


def on_device(sp, fsdp, *arrays):
    (
        hidden_in, token_stream, encoder_out, out_grad, doc_ids, key_order, context_size,
        self_query, self_key, self_value, self_output, cross_query, cross_key, cross_value, cross_output,
        inner_weight, inner_bias, outer_weight, outer_bias, first_gain, first_shift, second_gain,
        second_shift, third_gain, third_shift,
    ) = arrays
    seqs, local, width = hidden_in.shape
    enc_local = encoder_out.shape[1]
    shard, hidden_width = inner_weight.shape
    outer_rows = outer_weight.shape[0]
    bias_rows = inner_bias.shape[0]
    chunks = hidden_width // width
    span = min(local, 2 * BLK)
    subs = span // BLK
    steps = local // span
    heads = width // HD
    length = local * sp
    enc_len = enc_local * sp
    block_count = key_order.shape[1]
    depth = fsdp // 4
    tray = 16
    far = min(local, (WINDOW - 1) * BLK) if sp == 2 else local

    me, mine = lax.axis_index("sp"), lax.axis_index("fsdp")
    spot = jnp.stack([me, mine // 4, mine // 2 % 2, mine % 2]).astype(jnp.int32)

    pack_a = jnp.concatenate([self_query, self_key, self_value], axis=0)
    sent = token_stream
    if far != local:
        start = jnp.where(me == 0, local - far, 0)
        sent = lax.dynamic_slice(token_stream, (0, start, 0), (seqs, far, width))
    far_tokens = jnp.stack([shift(sent, "sp", r, sp) for r in range(1, sp)])
    vectors = (inner_bias, first_gain, first_shift, second_gain, second_shift, third_gain, third_shift, outer_bias)
    flat = jnp.concatenate(vectors)
    flat = jnp.pad(flat, (0, tray * width - flat.shape[0])).reshape(tray, width)
    pack_b = jnp.concatenate([self_output, cross_query, cross_key, cross_value, cross_output, flat], axis=0)
    pack_c = jnp.concatenate(jnp.split(inner_weight, chunks, axis=1) + [outer_weight], axis=0)

    pieces_a = gather_z(after(pack_a, sent), depth)
    pieces_b = gather_z(after(pack_b, pieces_a), depth)
    packs_a = gather_w(pieces_a, depth)
    hidden_early, pieces_b = together(hidden_in, pieces_b)
    core_b = w_flip(pieces_b, 1, depth)
    hidden_early, core_b = together(hidden_early, core_b)
    swap_b = w_flip(pieces_b, 2, depth)
    pack_c = after(pack_c, pieces_b, core_b, *packs_a)
    swap_c = [z_shift(pack_c, d, depth) for d in range(1, depth)]
    sent = after(encoder_out, far_tokens)
    far_enc = jnp.stack([shift(sent, "sp", r, sp) for r in range(1, sp)])

    whole = whole_spec()
    anywhere = pl.BlockSpec(memory_space=pl.ANY)
    turned_spec = lambda wide=span: pl.BlockSpec((1, width, wide), lambda s, i, *_: (s, 0, i))
    plain_spec = lambda wide=span: pl.BlockSpec((1, wide, width), lambda s, i, *_: (s, i, 0))
    per_seq = lambda shape: pl.BlockSpec((1,) + shape, lambda s, i, *_: (s, 0, 0))
    far_seq = lambda rows: pl.BlockSpec((sp - 1, 1, rows, width), lambda s, i, *_: (0, s, 0, 0))
    rows_spec = lambda count, wide: pl.BlockSpec((1, count, 8, wide), lambda s, i, *_: (s, i, 0, 0))
    probs_spec = lambda count, keys, wide: pl.BlockSpec(
        (1, count, heads, keys, wide), lambda s, i, *_: (s, i, 0, 0, 0)
    )
    half_rows = pl.BlockSpec((1, 1, 8, BLK), lambda s, i, *_: (s, i // subs, 0, i % subs))
    half_probs = pl.BlockSpec(
        (1, 1, heads, enc_len, BLK), lambda s, i, *_: (s, i // subs, 0, 0, i % subs)
    )
    turned_shape = (seqs, width, local)
    rows_shape = (seqs, steps, 8, span)
    self_rows_shape = (seqs, steps * subs, 8, BLK)
    big = lambda a, b, kind: pltpu.VMEM((a, b), kind)
    square = big(width, width, BF16)
    window = WINDOW * BLK

    keys, values, query, mixed, probs, inverse = call(
        functools.partial(self_forward_kernel, shard),
        (seqs, steps), 2,
        [
            plain_spec(), per_seq((local, width)), far_seq(far), per_seq((block_count, BLK)),
            per_seq((block_count, BLK)),
        ] + [whole] * 4,
        [
            per_seq((width, length)), per_seq((width, length)), turned_spec(), turned_spec(),
            probs_spec(subs, window, BLK), rows_spec(subs, BLK),
        ],
        [
            ((seqs, width, length), BF16), ((seqs, width, length), BF16), (turned_shape, BF16),
            (turned_shape, BF16), ((seqs, steps * subs, heads, window, BLK), BF16), (self_rows_shape, F32),
        ],
        [pltpu.VMEM((3, width, width), BF16)] + [square] * 3 + [pltpu.VMEM((subs, window, BLK), F32), big(heads, 128, F32)],
        32000.0,
        (doc_ids, spot, hidden_early, token_stream, far_tokens, key_order, context_size, *packs_a),
    )
    keys, values, query, mixed, probs, inverse, pieces_b, far_enc, swap_b, *swap_c = together(
        keys, values, query, mixed, probs, inverse, pieces_b, far_enc, swap_b, *swap_c
    )
    packs_b = [pieces_b, core_b, swap_b, w_flip(swap_b, 1, depth)]
    pieces_c = jnp.stack([pack_c] + swap_c)
    mixed, pieces_c = together(mixed, pieces_c)
    swap_c, core_c = w_flip(pieces_c, 2, depth), w_flip(pieces_c, 1, depth)

    (
        cross_keys, cross_values, cross_q, cross_mixed, cross_probs, cross_inverse, scaled1, scaled2, inverses,
        cols, inner_bias_col,
    ) = call(
        functools.partial(cross_forward_kernel, shard, bias_rows),
        (seqs, steps), 1,
        [plain_spec(), turned_spec(), per_seq((enc_local, width)), far_seq(enc_local)] + [whole] * 4,
        [
            per_seq((width, enc_len)), per_seq((width, enc_len)), turned_spec(), turned_spec(),
            probs_spec(1, enc_len, span), rows_spec(1, span), turned_spec(), turned_spec(), rows_spec(1, span),
            whole, whole,
        ],
        [
            ((seqs, width, enc_len), BF16), ((seqs, width, enc_len), BF16), (turned_shape, BF16),
            (turned_shape, BF16), ((seqs, steps, heads, enc_len, span), BF16), (rows_shape, F32),
            (turned_shape, F32), (turned_shape, F32), (rows_shape, F32), ((width, 8), F32),
            ((hidden_width, 1), F32),
        ],
        [pltpu.VMEM((5, width, width), BF16), big(fsdp, width, F32)] + [square] * 5 + [big(heads, 128, F32)],
        32000.0,
        (spot, hidden_in, mixed, encoder_out, far_enc, *packs_b),
    )

    (
        cross_keys, cross_values, cross_q, cross_mixed, cross_probs, cross_inverse, scaled1, scaled2, inverses,
        cols, inner_bias_col, pieces_c, swap_c, core_c,
    ) = together(
        cross_keys, cross_values, cross_q, cross_mixed, cross_probs, cross_inverse, scaled1, scaled2, inverses,
        cols, inner_bias_col, pieces_c, swap_c, core_c,
    )
    packs_c = [pieces_c, core_c, swap_c, w_flip(swap_c, 1, depth)]

    grads_shape = lambda rows: [((depth, rows, width), BF16)] * 4
    ff_rows = chunks * shard + outer_rows
    second_grad, layer_out, *ff_outs, late = call(
        functools.partial(feed_forward_kernel, shard, outer_rows),
        (seqs, steps), 1,
        [turned_spec(), rows_spec(1, span), plain_spec()] + [whole] * 6,
        [turned_spec(), plain_spec()] + [whole] * 5,
        [(turned_shape, F32), ((seqs, local, width), F32)] + grads_shape(ff_rows) + [((16, width), F32)],
        [
            big(width, hidden_width, BF16), big(hidden_width, width, BF16), big(hidden_width, width, BF16),
            big(width, hidden_width, BF16), big(width, hidden_width, F32), big(hidden_width, width, F32),
            pltpu.VMEM((5, width, 128), F32), big(hidden_width, 128, F32), big(hidden_width, span, BF16),
            big(width, 128, F32),
        ],
        70000.0,
        (spot, scaled2, inverses, out_grad, *packs_c, cols, inner_bias_col),
    )

    ff_swap = swap_w(ff_outs, depth)
    attention_scratch = lambda keys_len, kept_len: [
        big(width, keys_len, F32), big(width, keys_len, F32), pltpu.VMEM((heads, kept_len, BLK), BF16),
        big(width, BLK, BF16), big(heads, BLK, F32), big(width, BLK, BF16),
    ]
    first_grad, mixed_grad, own_enc_part, far_enc_part, *cross_outs = call(
        functools.partial(cross_back_kernel, shard),
        (seqs, steps * subs), 1,
        [
            turned_spec(BLK), turned_spec(BLK), half_rows, per_seq((enc_local, width)), far_seq(enc_local),
            per_seq((width, enc_len)), per_seq((width, enc_len)), turned_spec(BLK), turned_spec(BLK),
            half_probs, half_rows, turned_spec(BLK),
        ] + [whole] * 6,
        [
            turned_spec(BLK), turned_spec(BLK), per_seq((enc_local, width)), far_seq(enc_local),
        ] + [whole] * 2,
        [
            (turned_shape, F32), (turned_shape, BF16), ((seqs, enc_local, width), F32),
            ((sp - 1, seqs, enc_local, width), BF16),
        ] + [((2, depth, 5 * shard + tray, width), BF16)] * 2,
        [square] * 5
        + [pltpu.VMEM((5, width, width), F32), pltpu.VMEM((2, width, 128), F32), big(width, 128, F32)]
        + attention_scratch(enc_len, enc_len),
        56000.0,
        (
            spot, second_grad, scaled1, inverses, encoder_out, far_enc, cross_keys, cross_values, cross_q,
            cross_mixed, cross_probs, cross_inverse, mixed, *packs_b, cols, late,
        ),
    )

    first_grad, mixed_grad, own_enc_part, far_enc_part, *got = together(
        first_grad, mixed_grad, own_enc_part, far_enc_part, *cross_outs, *ff_swap
    )
    cross_outs, ff_swap = got[:2], got[2:]
    cross_swap = w_flip(cross_outs[1], 2, depth)
    cut_rows = ff_rows // 4
    ff_pieces = call(
        sum_kernel, (4,), 0,
        [pl.BlockSpec((depth, cut_rows, width), lambda i: (0, i, 0))] * 4,
        [pl.BlockSpec((cut_rows, width), lambda i: (i, 0))] * depth,
        [((ff_rows, width), F32)] + [((ff_rows, width), BF16)] * (depth - 1), [], 2000.0, (ff_outs[0], *ff_swap),
    )
    mixed_grad, *ff_pieces = together(mixed_grad, *ff_pieces)
    ff_swap = swap_z(ff_pieces, depth)
    enc_swap = [shift(far_enc_part[r - 1], "sp", -r, sp) for r in range(1, sp)]
    hidden_grad, token_grad, far_part, *self_outs = call(
        functools.partial(self_back_kernel, shard),
        (seqs, steps * subs), 2,
        [
            plain_spec(BLK), turned_spec(BLK), per_seq((local, width)), far_seq(far),
            per_seq((width, length)), per_seq((width, length)), turned_spec(BLK), turned_spec(BLK),
            probs_spec(1, window, BLK), rows_spec(1, BLK), turned_spec(BLK),
        ] + [whole] * 4,
        [plain_spec(BLK), per_seq((local, width)), far_seq(far)] + [whole] * 2,
        [((seqs, local, width), F32)] * 2 + [((sp - 1, seqs, far, width), BF16)]
        + [((2, depth, 3 * shard, width), BF16)] * 2,
        [pltpu.VMEM((3, width, width), F32)] + [square] * 3 + attention_scratch(length, window),
        50000.0,
        (
            doc_ids, spot, hidden_in, first_grad, token_stream, far_tokens, keys, values, query, mixed,
            probs, inverse, mixed_grad, *packs_a,
        ),
    )
    count = len(ff_swap)
    hidden_grad, token_grad, far_part, own_half, far_half, cross_own, cross_swap, *got = together(
        hidden_grad, token_grad, far_part, *self_outs, cross_outs[0], cross_swap, *ff_swap, *enc_swap
    )
    ff_got, enc_swap = got[:count], got[count:]
    token_swap = [shift(far_part[r - 1], "sp", -r, sp) for r in range(1, sp)]
    self_got = w_flip(far_half, 1, depth)
    self_got, ff_first, enc_first, ff_got[-1] = together(self_got, ff_pieces[0], own_enc_part, ff_got[-1])
    self_half = [own_half[y].astype(F32) + self_got[y].astype(F32) for y in range(2)]
    self_swap = w_flip(self_half[1].astype(BF16), 2, depth)
    cross_half = [cross_own[c].astype(F32) + cross_swap[c].astype(F32) for c in range(2)]
    cross_core = w_flip(cross_half[1].astype(BF16), 1, depth)
    cross_pieces = [cross_half[0][d] + cross_core[d].astype(F32) for d in range(depth)]
    cross_got = swap_z(cross_pieces, depth)
    ff_sum = add_all(ff_first, ff_got)
    self_swap, cross_first, *cross_got = together(self_swap, cross_pieces[0], *cross_got)
    self_pieces = [self_half[0][d] + self_swap[d].astype(F32) for d in range(depth)]
    self_more = swap_z(self_pieces, depth)
    self_sum = add_all(self_pieces[0], self_more)
    self_sp = swap_sp(self_sum, sp)
    cross_sum = add_all(cross_first, cross_got)
    ff_sum, cross_sum, *token_swap = together(ff_sum, cross_sum, *token_swap)
    ff_sp, cross_sp = swap_sp(ff_sum, sp), swap_sp(cross_sum, sp)

    shift_back = (local - far) // BLK
    for piece in token_swap:
        spec = pl.BlockSpec(
            (1, BLK, width), lambda s, i, spot: (s, i + jnp.where(spot[0] == 0, shift_back, 0), 0)
        )
        (token_grad,) = call(
            settle_kernel, (seqs, far // BLK), 1,
            [spec, pl.BlockSpec((1, BLK, width), lambda s, i, spot: (s, i, 0))],
            [spec], [((seqs, local, width), F32)], [], 5000.0, (spot, token_grad, piece), {1: 0},
        )
    encoder_grad = enc_first
    for r in range(1, sp):
        encoder_grad = encoder_grad + enc_swap[r - 1].astype(F32)

    ff_total = add_all(ff_sum, ff_sp)
    cross_total = add_all(cross_sum, cross_sp)
    self_total = add_all(self_sum, self_sp)
    inner_total = jnp.concatenate([ff_total[c * shard : (c + 1) * shard] for c in range(chunks)], axis=1)
    outer_total = ff_total[chunks * shard :]
    small = cross_total[5 * shard :]
    cut = lambda total, k: total[k * shard : (k + 1) * shard]
    vec = lambda k: lax.dynamic_slice(small, (k, mine * shard), (1, shard))[0]
    bias_total = lax.dynamic_slice(small[8 : 8 + chunks].reshape(-1), (mine * bias_rows,), (bias_rows,))
    return (
        layer_out, hidden_grad, token_grad, encoder_grad,
        cut(self_total, 0), cut(self_total, 1), cut(self_total, 2), cut(cross_total, 0),
        cut(cross_total, 1), cut(cross_total, 2), cut(cross_total, 3), cut(cross_total, 4),
        inner_total, bias_total, outer_total, vec(4), vec(5), vec(6), vec(0), vec(1), vec(2), vec(3),
    )


def solution(mesh):
    tokens, table, vector = P("fsdp", "sp", None), P("fsdp", None), P("fsdp")
    order = P("fsdp", None, None)
    return jax.shard_map(
        functools.partial(on_device, mesh.shape["sp"], mesh.shape["fsdp"]),
        mesh=mesh,
        in_specs=(tokens,) * 4
        + (table, order, order)
        + (table,) * 9
        + (vector, table)
        + (vector,) * 7,
        out_specs=(tokens,) * 4 + (table,) * 9 + (vector, table) + (vector,) * 7,
        check_vma=False,
    )
```

```python
import functools
import math

import jax
import jax.numpy as jnp
from jax import lax
from jax.experimental import pallas as pl
from jax.experimental.pallas import tpu as pltpu
from jax.sharding import PartitionSpec as P

HD = 64
BLK = 256
WINDOW = 4
EPS = 1e-05
MASKED = -1e30
LOG2E = 1.4426950408889634
LN2 = 0.6931471805599453
SAFE = 60.0
F32 = jnp.float32
BF16 = jnp.bfloat16
NN = (((1,), (0,)), ((), ()))
NT = (((1,), (1,)), ((), ()))
TN = (((0,), (0,)), ((), ()))
VMEM_LIMIT = 62 * 2**20


def dot(left, right, form=NN):
    return lax.dot_general(left, right, form, preferred_element_type=F32)


def norm(rows):
    center = rows - jnp.mean(rows, axis=0, keepdims=True)
    inverse = lax.rsqrt(jnp.mean(center * center, axis=0, keepdims=True) + EPS)
    return center * inverse, inverse


def norm_back(scaled, inverse, gain, upstream):
    through = upstream * gain
    return inverse * (
        through
        - jnp.mean(through, axis=0, keepdims=True)
        - scaled * jnp.mean(through * scaled, axis=0, keepdims=True)
    )


def fold(values):
    total = values[:, :128]
    for start in range(128, values.shape[1], 128):
        total = total + values[:, start : start + 128]
    return total


def gelu_pair(x):
    phi = 0.5 + 0.5 * lax.erf(x * math.sqrt(0.5))
    bell = jnp.exp2((-0.5 * LOG2E) * (x * x))
    return x * phi, phi + x * bell * (1.0 / math.sqrt(2.0 * math.pi))


def owner_of(spot, m, d, depth):
    z = lax.rem(spot[1] + d, depth)
    return (z * 2 + jnp.bitwise_xor(spot[2], m // 2)) * 2 + jnp.bitwise_xor(spot[3], m % 2)


def unpack(packs, spot, first, rows, plain):
    for m, pack in enumerate(packs):
        depth = pack.shape[0]
        for d in range(depth):
            at = pl.ds(pl.multiple_of(owner_of(spot, m, d, depth) * rows, rows), rows)
            plain[at, :] = pack[d, first : first + rows, :]


def send_grad(outs, spot, first, rows, acc, masks=(0, 1, 2, 3)):
    depth = outs[0].shape[0]
    for out, m in zip(outs, masks):
        for d in range(depth):
            at = pl.ds(pl.multiple_of(owner_of(spot, m, d, depth) * rows, rows), rows)
            out[d, first : first + rows, :] = acc[at, :].astype(BF16)


def attend(count, exact, keys, values, off, query, probs, mixed, inverse, bias):
    head_count, span = query.shape[0] // HD, query.shape[1]

    def scores(hs, j):
        part = dot(keys[hs, pl.ds(off + j * BLK, BLK)], query[hs, :], TN)
        if bias is not None:
            part = part + bias[j * BLK : (j + 1) * BLK, :]
        return part

    def first(h, hs):
        total = None
        if exact:
            parts = [scores(hs, j) for j in range(count)]
            top = jnp.max(parts[0], axis=0, keepdims=True)
            for part in parts[1:]:
                top = jnp.maximum(top, jnp.max(part, axis=0, keepdims=True))
        for j in range(count):
            terms = jnp.exp2(parts[j] - top if exact else scores(hs, j))
            partial = jnp.sum(terms.reshape(BLK // 8, 8, span), axis=0)
            total = partial if total is None else total + partial
            probs[h, j * BLK : (j + 1) * BLK, :] = terms.astype(BF16)
        return total

    def second(h, hs, total):
        sums = dot(values[hs, pl.ds(off, count * BLK)], probs[h, : count * BLK, :])
        scale = 1.0 / jnp.sum(total, axis=0, keepdims=True)
        mixed[hs, :] = (sums * scale).astype(BF16)
        inverse[pl.ds(h, 1), :] = scale

    if exact:

        def one(h, carry):
            hs = pl.ds(pl.multiple_of(h * HD, HD), HD)
            second(h, hs, first(h, hs))
            return carry

        lax.fori_loop(0, head_count, one, 0)
        return
    waiting = None
    for h in range(head_count):
        total = first(h, slice(h * HD, (h + 1) * HD))
        if h > 0:
            second(h - 1, slice((h - 1) * HD, h * HD), waiting)
        waiting = total
    second(head_count - 1, slice((head_count - 1) * HD, head_count * HD), waiting)


def attend_back(
    count, keys, values, off, query, grad, inner, probs, kept, query_grad, key_grad, value_grad
):
    head_count = query.shape[0] // HD

    def first(h):
        hs = slice(h * HD, (h + 1) * HD)
        for j in range(count):
            us = slice(j * BLK, (j + 1) * BLK)
            prob_grad = dot(values[hs, pl.ds(off + j * BLK, BLK)], grad[hs, :], TN)
            change = probs[h, us, :].astype(F32) * (prob_grad - inner[h : h + 1, :])
            kept[h, us, :] = change.astype(BF16)

    def second(h):
        hs = slice(h * HD, (h + 1) * HD)
        us = slice(0, count * BLK)
        window = pl.ds(off, count * BLK)
        query_grad[hs, :] = (dot(keys[hs, window], kept[h, us, :]) * (1.0 / math.sqrt(HD))).astype(BF16)
        key_grad[hs, window] += dot(query[hs, :], kept[h, us, :], NT)
        value_grad[hs, window] += dot(grad[hs, :], probs[h, us, :], NT)

    first(0)
    for h in range(1, head_count):
        first(h)
        second(h - 1)
    second(head_count - 1)


def scale_grad(mixed_grad, mixed, inverse, grad, inner):
    for h in range(mixed.shape[0] // HD):
        hs = slice(h * HD, (h + 1) * HD)
        scaled = mixed_grad[hs, :] * inverse[h : h + 1, :]
        grad[hs, :] = scaled.astype(BF16)
        inner[h : h + 1, :] = jnp.sum(scaled * mixed[hs, :].astype(F32), axis=0, keepdims=True)


def head_norms(rows, head_count):
    found = []
    for h in range(head_count):
        part = rows[h * HD : (h + 1) * HD, :].astype(F32)
        found.append(jnp.max(jnp.sum(part * part, axis=0, keepdims=True), axis=1, keepdims=True))
    return found


def safe_scores(query, key_norms):
    head_count = query.shape[0] // HD
    worst = None
    for h, found in enumerate(head_norms(query[...], head_count)):
        product = found * key_norms[h : h + 1, 0:1]
        worst = product if worst is None else jnp.maximum(worst, product)
    return jnp.max(worst) < SAFE * SAFE


def store_key_norms(key_norms, keys):
    head_count = keys.shape[0] // HD
    for h, found in enumerate(head_norms(keys[...], head_count)):
        key_norms[h : h + 1, :] = jnp.broadcast_to(found, (1, key_norms.shape[1]))


def doc_span(docs, seq, block, block_count):
    mine = docs[seq, block]
    low = jnp.int32(0)
    count = jnp.int32(0)
    for b in range(block_count):
        low = low + jnp.where(docs[seq, b] < mine, 1, 0).astype(jnp.int32)
        count = count + jnp.where(docs[seq, b] == mine, 1, 0).astype(jnp.int32)
    return low, count


def self_forward_kernel(
    shard, docs, spot, hidden, own_tokens, far_tokens, order, reach, pack0, pack1, pack2, pack3,
    keys, values, query, mixed, probs, inverse,
    plain, q_turned, k_turned, v_turned, bias, key_norms,
):
    seq, step = pl.program_id(0), pl.program_id(1)
    steps = pl.num_programs(1)
    rows = shard
    local = own_tokens.shape[1]
    far = far_tokens.shape[2]
    parts = far_tokens.shape[0] + 1
    block_count = order.shape[1]
    me = spot[0]

    @pl.when((seq == 0) & (step == 0))
    def _():
        for which, turned in enumerate((q_turned, k_turned, v_turned)):
            unpack((pack0, pack1, pack2, pack3), spot, which * rows, rows, plain.at[which])
            turned[...] = plain[which].T

    @pl.when(step == 0)
    def _():
        if far != local:
            keys[...] = jnp.zeros_like(keys)
        for part in range(parts):
            tokens = own_tokens[0] if part == 0 else far_tokens[part - 1, 0]
            at = token_window(me, part, parts, local, far)
            turned = tokens.T
            keys[0, :, at] = dot(k_turned[...], turned).astype(BF16)
            values[0, :, at] = dot(v_turned[...], turned).astype(BF16)
        store_key_norms(key_norms, keys.at[0])

    query[0] = (dot(q_turned[...], hidden[0].T) * (LOG2E / math.sqrt(HD))).astype(BF16)
    safe = safe_scores(query.at[0], key_norms)
    order_turned = order[0].astype(F32).T
    lanes = lax.broadcasted_iota(jnp.int32, order_turned.shape, 1)
    differ = lax.broadcasted_iota(jnp.int32, (BLK, BLK), 0) != lax.broadcasted_iota(
        jnp.int32, (BLK, BLK), 1
    )
    subs = hidden.shape[1] // BLK
    for part in range(subs):
        block = (me * steps + step) * subs + part
        low, count = doc_span(docs, seq, block, block_count)
        reach_row = reach[0, pl.ds(block, 1), :].astype(F32)
        for j in range(WINDOW):
            at = low + j
            column = jnp.sum(jnp.where(lanes == at, order_turned, 0.0), axis=1, keepdims=True)
            seen = (column < reach_row) & (differ | (at != block))
            bias[part, j * BLK : (j + 1) * BLK, :] = jnp.where(seen, 0.0, MASKED)
        off = pl.multiple_of(low * BLK, BLK)
        ts = slice(part * BLK, (part + 1) * BLK)
        for size in range(1, WINDOW + 1):
            for exact in (False, True):

                @pl.when((count == size) & (safe != exact))
                def _(size=size, exact=exact, part=part, off=off, ts=ts):
                    attend(
                        size, exact, keys.at[0], values.at[0], off, query.at[0, :, ts], probs.at[0, part],
                        mixed.at[0, :, ts], inverse.at[0, part], bias.at[part],
                    )


def token_window(me, part, parts, local, far):
    owner = lax.rem(me + part, parts)
    if part == 0 or far == local:
        return pl.ds(pl.multiple_of(owner * local, BLK), local)
    return pl.ds(pl.multiple_of(owner * local + jnp.where(owner == 0, local - far, 0), BLK), far)


def cross_forward_kernel(
    shard, bias_rows, spot, hidden, self_mixed, own_enc, far_enc, pack0, pack1, pack2, pack3,
    keys, values, query, mixed, probs, inverse, scaled1, scaled2, inverses, cols, bias_col,
    plain, spread_rows, so_turned, q_turned, k_turned, v_turned, o_turned, key_norms,
):
    seq, step = pl.program_id(0), pl.program_id(1)
    rows = shard
    local = own_enc.shape[1]
    parts = far_enc.shape[0] + 1
    packs = (pack0, pack1, pack2, pack3)

    @pl.when((seq == 0) & (step == 0))
    def _():
        for which, turned in enumerate((so_turned, q_turned, k_turned, v_turned, o_turned)):
            unpack(packs, spot, which * rows, rows, plain.at[which])
            turned[...] = plain[which].T
        depth = pack0.shape[0]
        for m, pack in enumerate(packs):
            for d in range(depth):
                row = pack[d, 5 * rows : 5 * rows + 16, :].astype(F32)[0:1, :]
                spread_rows[pl.ds(owner_of(spot, m, d, depth), 1), :] = row
        spread = spread_rows[...].T
        count = 4 * depth
        bias_col[...] = jnp.concatenate([spread[:bias_rows, f : f + 1] for f in range(count)], axis=0)
        for v in range(7):
            at = slice(bias_rows + v * rows, bias_rows + (v + 1) * rows)
            cols[:, v : v + 1] = jnp.concatenate([spread[at, f : f + 1] for f in range(count)], axis=0)

    @pl.when(step == 0)
    def _():
        for part in range(parts):
            turned = (own_enc[0] if part == 0 else far_enc[part - 1, 0]).T
            at = slice(part * local, (part + 1) * local)
            keys[0, :, at] = dot(k_turned[...], turned).astype(BF16)
            values[0, :, at] = dot(v_turned[...], turned).astype(BF16)
        store_key_norms(key_norms, keys.at[0])

    center, inverse1 = norm(hidden[0].T.astype(F32) + dot(so_turned[...], self_mixed[0]))
    scaled1[0] = center
    normed = center * cols[:, 0:1] + cols[:, 1:2]
    query[0] = (dot(q_turned[...], normed.astype(BF16)) * (LOG2E / math.sqrt(HD))).astype(BF16)
    safe = safe_scores(query.at[0], key_norms)
    for exact in (False, True):

        @pl.when(safe != exact)
        def _(exact=exact):
            attend(
                parts * local // BLK, exact, keys.at[0], values.at[0], 0, query.at[0], probs.at[0, 0],
                mixed.at[0], inverse.at[0, 0], None,
            )

    normed = scaled1[0] * cols[:, 0:1] + cols[:, 1:2]
    center, inverse2 = norm(normed + dot(o_turned[...], mixed[0]))
    scaled2[0] = center
    inverses[0, 0, 0:1, :] = inverse1
    inverses[0, 0, 1:2, :] = inverse2


def feed_forward_kernel(
    shard, outer_rows, spot, scaled2_in, inverses, out_grad, pack0, pack1, pack2, pack3, cols, inner_bias,
    second_grad, layer_out, out0, out1, out2, out3, late,
    inner, inner_turned, outer, outer_turned, inner_acc, outer_acc, sums, bias_sum, slope, sheet,
):
    seq, step = pl.program_id(0), pl.program_id(1)
    rows = shard
    first_step = (seq == 0) & (step == 0)
    last_step = (seq == pl.num_programs(0) - 1) & (step == pl.num_programs(1) - 1)
    width = inner.shape[0]
    chunks = inner.shape[1] // width
    packs = (pack0, pack1, pack2, pack3)

    @pl.when(first_step)
    def _():
        for c in range(chunks):
            cs = slice(c * width, (c + 1) * width)
            unpack(packs, spot, c * rows, rows, inner.at[:, cs])
            inner_turned[cs, :] = inner[:, cs].T
        unpack(packs, spot, chunks * rows, outer_rows, outer)
        for c in range(chunks):
            cs = slice(c * width, (c + 1) * width)
            outer_turned[:, cs] = outer[cs, :].T
        inner_acc[...] = jnp.zeros_like(inner_acc)
        outer_acc[...] = jnp.zeros_like(outer_acc)
        sums[...] = jnp.zeros_like(sums)
        bias_sum[...] = jnp.zeros_like(bias_sum)

    scaled2 = scaled2_in[0]
    gain2 = cols[:, 2:3]
    middle = scaled2 * gain2 + cols[:, 3:4]
    middle_low = middle.astype(BF16)
    pre = dot(inner_turned[...], middle_low) + inner_bias[...]
    active, pull = gelu_pair(pre)
    active = active.astype(BF16)
    slope[...] = pull.astype(BF16)
    third_sum = middle + dot(outer_turned[...], active) + cols[:, 6:7]
    scaled3, inverse3 = norm(third_sum)
    gain3 = cols[:, 4:5]
    layer_out[0] = (scaled3 * gain3 + cols[:, 5:6]).T
    upstream = out_grad[0].T.astype(F32)
    third_grad = norm_back(scaled3, inverse3, gain3, upstream)
    sums[2] += fold(upstream * scaled3)
    sums[3] += fold(upstream)
    outer_low = third_grad.astype(BF16)
    sums[4] += fold(outer_low.astype(F32))
    outer_acc[...] += dot(active, outer_low, NT)
    inner_low = (dot(outer[...], outer_low) * slope[...].astype(F32)).astype(BF16)
    bias_sum[...] += fold(inner_low.astype(F32))
    inner_acc[...] += dot(middle_low, inner_low, NT)
    middle_grad = third_grad + dot(inner[...], inner_low)
    sums[0] += fold(middle_grad * scaled2)
    sums[1] += fold(middle_grad)
    second_grad[0] = norm_back(scaled2, inverses[0, 0, 1:2, :], gain2, middle_grad)

    @pl.when(last_step)
    def _():
        outs = (out0, out1, out2, out3)
        for c in range(chunks):
            send_grad(outs, spot, c * rows, rows, inner_acc.at[:, c * width : (c + 1) * width])
        send_grad(outs, spot, chunks * rows, outer_rows, outer_acc)
        sheet[...] = jnp.zeros_like(sheet)
        for which in range(5):
            sheet[:, which : which + 1] = jnp.sum(sums[which], axis=1, keepdims=True)
        for c in range(chunks):
            part = bias_sum[c * width : (c + 1) * width, :]
            sheet[:, 8 + c : 9 + c] = jnp.sum(part, axis=1, keepdims=True)
        late[...] = sheet[...].T[0:16, :]


def cross_back_kernel(
    shard, spot, second_grad, scaled1, inverses, own_enc, far_enc, keys, values, query, mixed, probs, inverse,
    self_mixed, pack0, pack1, pack2, pack3, cols, late,
    first_grad, self_mixed_grad, own_part, far_part, out0, out1,
    so_plain, q_plain, k_plain, v_plain, o_plain, accs, sums, sheet,
    key_acc, value_acc, kept, grad, inner, query_grad,
):
    seq, step = pl.program_id(0), pl.program_id(1)
    rows = shard
    first_step = (seq == 0) & (step == 0)
    last_step = (seq == pl.num_programs(0) - 1) & (step == pl.num_programs(1) - 1)
    local = own_enc.shape[1]
    parts = far_enc.shape[0] + 1

    @pl.when(first_step)
    def _():
        for which, plain in enumerate((so_plain, q_plain, k_plain, v_plain, o_plain)):
            unpack((pack0, pack1, pack2, pack3), spot, which * rows, rows, plain)
        accs[...] = jnp.zeros_like(accs)
        sums[...] = jnp.zeros_like(sums)

    @pl.when(step == 0)
    def _():
        key_acc[...] = jnp.zeros_like(key_acc)
        value_acc[...] = jnp.zeros_like(value_acc)

    cross_low = second_grad[0].astype(BF16)
    scale_grad(dot(o_plain[...], cross_low), mixed.at[0], inverse.at[0, 0], grad, inner)
    accs[4] += dot(mixed[0], cross_low, NT)
    attend_back(
        parts * local // BLK, keys.at[0], values.at[0], 0, query.at[0], grad, inner, probs.at[0, 0],
        kept, query_grad, key_acc, value_acc,
    )
    scaled = scaled1[0]
    gain = cols[:, 0:1]
    normed_low = (scaled * gain + cols[:, 1:2]).astype(BF16)
    accs[1] += dot(normed_low, query_grad[...], NT)
    normed_grad = second_grad[0] + dot(q_plain[...], query_grad[...])
    sums[0] += fold(normed_grad * scaled)
    sums[1] += fold(normed_grad)
    through = norm_back(scaled, inverses[0, 0, 0:1, :], gain, normed_grad)
    first_grad[0] = through
    self_low = through.astype(BF16)
    accs[0] += dot(self_mixed[0], self_low, NT)
    self_mixed_grad[0] = dot(so_plain[...], self_low).astype(BF16)

    @pl.when(step == pl.num_programs(1) - 1)
    def _():
        for part in range(parts):
            at = slice(part * local, (part + 1) * local)
            key_low = (key_acc[:, at] * LN2).astype(BF16)
            value_low = value_acc[:, at].astype(BF16)
            turned = (own_enc[0] if part == 0 else far_enc[part - 1, 0]).T
            accs[2] += dot(turned, key_low, NT)
            accs[3] += dot(turned, value_low, NT)
            whole = (dot(k_plain[...], key_low) + dot(v_plain[...], value_low)).T
            if part == 0:
                own_part[0] = whole
            else:
                far_part[part - 1, 0] = whole.astype(BF16)

    @pl.when(last_step)
    def _():
        for c in range(2):
            outs = (out0.at[c], out1.at[c])
            for which in range(5):
                send_grad(outs, spot, which * rows, rows, accs.at[which], (c, 2 + c))
        sheet[...] = jnp.zeros_like(sheet)
        for which in range(2):
            sheet[:, 5 + which : 6 + which] = jnp.sum(sums[which], axis=1, keepdims=True)
        tray = (sheet[...].T[0:16, :] + late[...]).astype(BF16)
        for out in (out0, out1):
            for c in range(2):
                for d in range(out.shape[1]):
                    out[c, d, 5 * rows : 5 * rows + 16, :] = tray


def self_back_kernel(
    shard, docs, spot, hidden, first_grad, own_tokens, far_tokens, keys, values, query, mixed, probs,
    inverse, mixed_grad, pack0, pack1, pack2, pack3, hidden_grad, own_part, far_part, out0, out1,
    accs, q_plain, k_plain, v_plain, key_acc, value_acc, kept, grad, inner, query_grad,
):
    seq, step = pl.program_id(0), pl.program_id(1)
    steps = pl.num_programs(1)
    rows = shard
    local = own_tokens.shape[1]
    far = far_tokens.shape[2]
    parts = far_tokens.shape[0] + 1
    me = spot[0]
    block_count = parts * steps * (hidden.shape[1] // BLK)

    @pl.when((seq == 0) & (step == 0))
    def _():
        for which, plain in enumerate((q_plain, k_plain, v_plain)):
            unpack((pack0, pack1, pack2, pack3), spot, which * rows, rows, plain)
        accs[...] = jnp.zeros_like(accs)

    @pl.when(step == 0)
    def _():
        key_acc[...] = jnp.zeros_like(key_acc)
        value_acc[...] = jnp.zeros_like(value_acc)

    subs = hidden.shape[1] // BLK
    for part in range(subs):
        ts = slice(part * BLK, (part + 1) * BLK)
        scale_grad(
            mixed_grad[0, :, ts].astype(F32), mixed.at[0, :, ts], inverse.at[0, part], grad.at[:, ts],
            inner.at[:, ts],
        )
    for part in range(subs):
        ts = slice(part * BLK, (part + 1) * BLK)
        low, count = doc_span(docs, seq, (me * steps + step) * subs + part, block_count)
        off = pl.multiple_of(low * BLK, BLK)
        for size in range(1, WINDOW + 1):

            @pl.when(count == size)
            def _(size=size, part=part, ts=ts, off=off):
                attend_back(
                    size, keys.at[0], values.at[0], off, query.at[0, :, ts], grad.at[:, ts], inner.at[:, ts],
                    probs.at[0, part], kept, query_grad.at[:, ts], key_acc, value_acc,
                )

    accs[0] += dot(hidden[0].T, query_grad[...], NT)
    hidden_grad[0] = (first_grad[0] + dot(q_plain[...], query_grad[...])).T

    @pl.when(step == steps - 1)
    def _():
        for part in range(parts):
            at = token_window(me, part, parts, local, far)
            key_low = (key_acc[:, at] * LN2).astype(BF16)
            value_low = value_acc[:, at].astype(BF16)
            turned = (own_tokens[0] if part == 0 else far_tokens[part - 1, 0]).T
            accs[1] += dot(turned, key_low, NT)
            accs[2] += dot(turned, value_low, NT)
            whole = (dot(k_plain[...], key_low) + dot(v_plain[...], value_low)).T
            if part == 0:
                own_part[0] = whole
            else:
                far_part[part - 1, 0] = whole.astype(BF16)

    @pl.when((seq == pl.num_programs(0) - 1) & (step == steps - 1))
    def _():
        for y in range(2):
            outs = (out0.at[y], out1.at[y])
            for which in range(3):
                send_grad(outs, spot, which * rows, rows, accs.at[which], (2 * y, 2 * y + 1))


def settle_kernel(spot, own, far, out):
    out[...] = own[...] + far[...].astype(F32)


def sum_kernel(*refs):
    for d, out in enumerate(refs[4:]):
        total = refs[0][d].astype(F32)
        for ref in refs[1:4]:
            total = total + ref[d].astype(F32)
        out[...] = total.astype(out.dtype)


def whole_spec():
    return pl.BlockSpec(memory_space=pltpu.VMEM)


def call(body, grid, scalars, in_specs, out_specs, out_shape, scratch, micros, args, aliases={}):
    return pl.pallas_call(
        body,
        grid_spec=pltpu.PrefetchScalarGridSpec(
            num_scalar_prefetch=scalars,
            grid=grid,
            in_specs=in_specs,
            out_specs=out_specs,
            scratch_shapes=scratch,
        ),
        out_shape=[jax.ShapeDtypeStruct(shape, kind) for shape, kind in out_shape],
        input_output_aliases=aliases,
        compiler_params=pltpu.CompilerParams(vmem_limit_bytes=VMEM_LIMIT),
        cost_estimate=pl.CostEstimate(flops=int(micros * 1e9), bytes_accessed=2**24, transcendentals=0),
    )(*args)


def shift(array, axis, by, size):
    return lax.ppermute(array, axis, [((i + by) % size, i) for i in range(size)])


def z_shift(array, by, depth):
    pairs = [(((z + by) % depth) * 4 + w, z * 4 + w) for z in range(depth) for w in range(4)]
    return lax.ppermute(array, "fsdp", pairs)


def w_flip(array, mask, depth):
    return lax.ppermute(array, "fsdp", [(z * 4 + (w ^ mask), z * 4 + w) for z in range(depth) for w in range(4)])


def together(*arrays):
    return lax.optimization_barrier(arrays)


def after(array, *earlier):
    return lax.optimization_barrier((array,) + earlier)[0]


def gather_stack(packed, got):
    return jnp.stack([packed] + got)


def gather_z(packed, depth):
    return gather_stack(packed, [z_shift(packed, d, depth) for d in range(1, depth)])


def gather_w(pieces, depth):
    across = w_flip(pieces, 2, depth)
    return [pieces, w_flip(pieces, 1, depth), across, w_flip(across, 1, depth)]


def swap_w(outs, depth):
    return [w_flip(outs[m], m, depth) for m in (1, 2, 3)]


def swap_z(pieces, depth):
    return [z_shift(pieces[d].astype(BF16), -d, depth) for d in range(1, depth)]


def add_w(own, got, depth):
    return [sum(piece[d].astype(F32) for piece in [own] + got) for d in range(depth)]


def swap_sp(total, sp):
    mine = total.astype(BF16)
    return [shift(mine, "sp", r, sp) for r in range(1, sp)]


def add_all(total, got):
    return sum((piece.astype(F32) for piece in got), total)


def on_device(sp, fsdp, *arrays):
    (
        hidden_in, token_stream, encoder_out, out_grad, doc_ids, key_order, context_size,
        self_query, self_key, self_value, self_output, cross_query, cross_key, cross_value, cross_output,
        inner_weight, inner_bias, outer_weight, outer_bias, first_gain, first_shift, second_gain,
        second_shift, third_gain, third_shift,
    ) = arrays
    seqs, local, width = hidden_in.shape
    enc_local = encoder_out.shape[1]
    shard, hidden_width = inner_weight.shape
    outer_rows = outer_weight.shape[0]
    bias_rows = inner_bias.shape[0]
    chunks = hidden_width // width
    span = min(local, 2 * BLK)
    subs = span // BLK
    steps = local // span
    heads = width // HD
    length = local * sp
    enc_len = enc_local * sp
    block_count = key_order.shape[1]
    depth = fsdp // 4
    tray = 16
    far = min(local, (WINDOW - 1) * BLK) if sp == 2 else local

    me, mine = lax.axis_index("sp"), lax.axis_index("fsdp")
    spot = jnp.stack([me, mine // 4, mine // 2 % 2, mine % 2]).astype(jnp.int32)

    pack_a = jnp.concatenate([self_query, self_key, self_value], axis=0)
    sent = token_stream
    if far != local:
        start = jnp.where(me == 0, local - far, 0)
        sent = lax.dynamic_slice(token_stream, (0, start, 0), (seqs, far, width))
    far_tokens = jnp.stack([shift(sent, "sp", r, sp) for r in range(1, sp)])
    vectors = (inner_bias, first_gain, first_shift, second_gain, second_shift, third_gain, third_shift, outer_bias)
    flat = jnp.concatenate(vectors)
    flat = jnp.pad(flat, (0, tray * width - flat.shape[0])).reshape(tray, width)
    pack_b = jnp.concatenate([self_output, cross_query, cross_key, cross_value, cross_output, flat], axis=0)
    pack_c = jnp.concatenate(jnp.split(inner_weight, chunks, axis=1) + [outer_weight], axis=0)

    pieces_a = gather_z(after(pack_a, sent), depth)
    pieces_b = gather_z(after(pack_b, pieces_a), depth)
    packs_a = gather_w(pieces_a, depth)
    hidden_early, pieces_b = together(hidden_in, pieces_b)
    core_b = w_flip(pieces_b, 1, depth)
    hidden_early, core_b = together(hidden_early, core_b)
    swap_b = w_flip(pieces_b, 2, depth)
    pack_c = after(pack_c, pieces_b, core_b, *packs_a)
    swap_c = [z_shift(pack_c, d, depth) for d in range(1, depth)]
    sent = after(encoder_out, far_tokens)
    far_enc = jnp.stack([shift(sent, "sp", r, sp) for r in range(1, sp)])

    whole = whole_spec()
    anywhere = pl.BlockSpec(memory_space=pl.ANY)
    turned_spec = lambda wide=span: pl.BlockSpec((1, width, wide), lambda s, i, *_: (s, 0, i))
    plain_spec = lambda wide=span: pl.BlockSpec((1, wide, width), lambda s, i, *_: (s, i, 0))
    per_seq = lambda shape: pl.BlockSpec((1,) + shape, lambda s, i, *_: (s, 0, 0))
    far_seq = lambda rows: pl.BlockSpec((sp - 1, 1, rows, width), lambda s, i, *_: (0, s, 0, 0))
    rows_spec = lambda count, wide: pl.BlockSpec((1, count, 8, wide), lambda s, i, *_: (s, i, 0, 0))
    probs_spec = lambda count, keys, wide: pl.BlockSpec(
        (1, count, heads, keys, wide), lambda s, i, *_: (s, i, 0, 0, 0)
    )
    half_rows = pl.BlockSpec((1, 1, 8, BLK), lambda s, i, *_: (s, i // subs, 0, i % subs))
    half_probs = pl.BlockSpec(
        (1, 1, heads, enc_len, BLK), lambda s, i, *_: (s, i // subs, 0, 0, i % subs)
    )
    turned_shape = (seqs, width, local)
    rows_shape = (seqs, steps, 8, span)
    self_rows_shape = (seqs, steps * subs, 8, BLK)
    big = lambda a, b, kind: pltpu.VMEM((a, b), kind)
    square = big(width, width, BF16)
    window = WINDOW * BLK

    keys, values, query, mixed, probs, inverse = call(
        functools.partial(self_forward_kernel, shard),
        (seqs, steps), 2,
        [
            plain_spec(), per_seq((local, width)), far_seq(far), per_seq((block_count, BLK)),
            per_seq((block_count, BLK)),
        ] + [whole] * 4,
        [
            per_seq((width, length)), per_seq((width, length)), turned_spec(), turned_spec(),
            probs_spec(subs, window, BLK), rows_spec(subs, BLK),
        ],
        [
            ((seqs, width, length), BF16), ((seqs, width, length), BF16), (turned_shape, BF16),
            (turned_shape, BF16), ((seqs, steps * subs, heads, window, BLK), BF16), (self_rows_shape, F32),
        ],
        [pltpu.VMEM((3, width, width), BF16)] + [square] * 3 + [pltpu.VMEM((subs, window, BLK), F32), big(heads, 128, F32)],
        32000.0,
        (doc_ids, spot, hidden_early, token_stream, far_tokens, key_order, context_size, *packs_a),
    )
    keys, values, query, mixed, probs, inverse, pieces_b, far_enc, swap_b, *swap_c = together(
        keys, values, query, mixed, probs, inverse, pieces_b, far_enc, swap_b, *swap_c
    )
    packs_b = [pieces_b, core_b, swap_b, w_flip(swap_b, 1, depth)]
    pieces_c = jnp.stack([pack_c] + swap_c)
    mixed, pieces_c = together(mixed, pieces_c)
    swap_c, core_c = w_flip(pieces_c, 2, depth), w_flip(pieces_c, 1, depth)

    (
        cross_keys, cross_values, cross_q, cross_mixed, cross_probs, cross_inverse, scaled1, scaled2, inverses,
        cols, inner_bias_col,
    ) = call(
        functools.partial(cross_forward_kernel, shard, bias_rows),
        (seqs, steps), 1,
        [plain_spec(), turned_spec(), per_seq((enc_local, width)), far_seq(enc_local)] + [whole] * 4,
        [
            per_seq((width, enc_len)), per_seq((width, enc_len)), turned_spec(), turned_spec(),
            probs_spec(1, enc_len, span), rows_spec(1, span), turned_spec(), turned_spec(), rows_spec(1, span),
            whole, whole,
        ],
        [
            ((seqs, width, enc_len), BF16), ((seqs, width, enc_len), BF16), (turned_shape, BF16),
            (turned_shape, BF16), ((seqs, steps, heads, enc_len, span), BF16), (rows_shape, F32),
            (turned_shape, F32), (turned_shape, F32), (rows_shape, F32), ((width, 8), F32),
            ((hidden_width, 1), F32),
        ],
        [pltpu.VMEM((5, width, width), BF16), big(fsdp, width, F32)] + [square] * 5 + [big(heads, 128, F32)],
        32000.0,
        (spot, hidden_in, mixed, encoder_out, far_enc, *packs_b),
    )

    (
        cross_keys, cross_values, cross_q, cross_mixed, cross_probs, cross_inverse, scaled1, scaled2, inverses,
        cols, inner_bias_col, pieces_c, swap_c, core_c,
    ) = together(
        cross_keys, cross_values, cross_q, cross_mixed, cross_probs, cross_inverse, scaled1, scaled2, inverses,
        cols, inner_bias_col, pieces_c, swap_c, core_c,
    )
    packs_c = [pieces_c, core_c, swap_c, w_flip(swap_c, 1, depth)]

    grads_shape = lambda rows: [((depth, rows, width), BF16)] * 4
    ff_rows = chunks * shard + outer_rows
    second_grad, layer_out, *ff_outs, late = call(
        functools.partial(feed_forward_kernel, shard, outer_rows),
        (seqs, steps), 1,
        [turned_spec(), rows_spec(1, span), plain_spec()] + [whole] * 6,
        [turned_spec(), plain_spec()] + [whole] * 5,
        [(turned_shape, F32), ((seqs, local, width), F32)] + grads_shape(ff_rows) + [((16, width), F32)],
        [
            big(width, hidden_width, BF16), big(hidden_width, width, BF16), big(hidden_width, width, BF16),
            big(width, hidden_width, BF16), big(width, hidden_width, F32), big(hidden_width, width, F32),
            pltpu.VMEM((5, width, 128), F32), big(hidden_width, 128, F32), big(hidden_width, span, BF16),
            big(width, 128, F32),
        ],
        70000.0,
        (spot, scaled2, inverses, out_grad, *packs_c, cols, inner_bias_col),
    )

    ff_swap = swap_w(ff_outs, depth)
    attention_scratch = lambda keys_len, kept_len: [
        big(width, keys_len, F32), big(width, keys_len, F32), pltpu.VMEM((heads, kept_len, BLK), BF16),
        big(width, BLK, BF16), big(heads, BLK, F32), big(width, BLK, BF16),
    ]
    first_grad, mixed_grad, own_enc_part, far_enc_part, *cross_outs = call(
        functools.partial(cross_back_kernel, shard),
        (seqs, steps * subs), 1,
        [
            turned_spec(BLK), turned_spec(BLK), half_rows, per_seq((enc_local, width)), far_seq(enc_local),
            per_seq((width, enc_len)), per_seq((width, enc_len)), turned_spec(BLK), turned_spec(BLK),
            half_probs, half_rows, turned_spec(BLK),
        ] + [whole] * 6,
        [
            turned_spec(BLK), turned_spec(BLK), per_seq((enc_local, width)), far_seq(enc_local),
        ] + [whole] * 2,
        [
            (turned_shape, F32), (turned_shape, BF16), ((seqs, enc_local, width), F32),
            ((sp - 1, seqs, enc_local, width), BF16),
        ] + [((2, depth, 5 * shard + tray, width), BF16)] * 2,
        [square] * 5
        + [pltpu.VMEM((5, width, width), F32), pltpu.VMEM((2, width, 128), F32), big(width, 128, F32)]
        + attention_scratch(enc_len, enc_len),
        56000.0,
        (
            spot, second_grad, scaled1, inverses, encoder_out, far_enc, cross_keys, cross_values, cross_q,
            cross_mixed, cross_probs, cross_inverse, mixed, *packs_b, cols, late,
        ),
    )

    first_grad, mixed_grad, own_enc_part, far_enc_part, *got = together(
        first_grad, mixed_grad, own_enc_part, far_enc_part, *cross_outs, *ff_swap
    )
    cross_outs, ff_swap = got[:2], got[2:]
    cross_swap = w_flip(cross_outs[1], 2, depth)
    cut_rows = ff_rows // 2
    ff_pieces = call(
        sum_kernel, (2,), 0,
        [pl.BlockSpec((depth, cut_rows, width), lambda i: (0, i, 0))] * 4,
        [pl.BlockSpec((cut_rows, width), lambda i: (i, 0))] * depth,
        [((ff_rows, width), F32)] + [((ff_rows, width), BF16)] * (depth - 1), [], 2000.0, (ff_outs[0], *ff_swap),
    )
    mixed_grad, *ff_pieces = together(mixed_grad, *ff_pieces)
    ff_swap = swap_z(ff_pieces, depth)
    enc_swap = [shift(far_enc_part[r - 1], "sp", -r, sp) for r in range(1, sp)]
    hidden_grad, token_grad, far_part, *self_outs = call(
        functools.partial(self_back_kernel, shard),
        (seqs, steps * subs), 2,
        [
            plain_spec(BLK), turned_spec(BLK), per_seq((local, width)), far_seq(far),
            per_seq((width, length)), per_seq((width, length)), turned_spec(BLK), turned_spec(BLK),
            probs_spec(1, window, BLK), rows_spec(1, BLK), turned_spec(BLK),
        ] + [whole] * 4,
        [plain_spec(BLK), per_seq((local, width)), far_seq(far)] + [whole] * 2,
        [((seqs, local, width), F32)] * 2 + [((sp - 1, seqs, far, width), BF16)]
        + [((2, depth, 3 * shard, width), BF16)] * 2,
        [pltpu.VMEM((3, width, width), F32)] + [square] * 3 + attention_scratch(length, window),
        50000.0,
        (
            doc_ids, spot, hidden_in, first_grad, token_stream, far_tokens, keys, values, query, mixed,
            probs, inverse, mixed_grad, *packs_a,
        ),
    )
    count = len(ff_swap)
    hidden_grad, token_grad, far_part, own_half, far_half, cross_own, cross_swap, *got = together(
        hidden_grad, token_grad, far_part, *self_outs, cross_outs[0], cross_swap, *ff_swap, *enc_swap
    )
    ff_got, enc_swap = got[:count], got[count:]
    token_swap = [shift(far_part[r - 1], "sp", -r, sp) for r in range(1, sp)]
    self_got = w_flip(far_half, 1, depth)
    self_got, ff_first, enc_first, ff_got[-1] = together(self_got, ff_pieces[0], own_enc_part, ff_got[-1])
    self_half = [own_half[y].astype(F32) + self_got[y].astype(F32) for y in range(2)]
    self_swap = w_flip(self_half[1].astype(BF16), 2, depth)
    cross_half = [cross_own[c].astype(F32) + cross_swap[c].astype(F32) for c in range(2)]
    cross_core = w_flip(cross_half[1].astype(BF16), 1, depth)
    cross_pieces = [cross_half[0][d] + cross_core[d].astype(F32) for d in range(depth)]
    cross_got = swap_z(cross_pieces, depth)
    ff_sum = add_all(ff_first, ff_got)
    self_swap, cross_first, ff_sum, *cross_got = together(self_swap, cross_pieces[0], ff_sum, *cross_got)
    self_pieces = [self_half[0][d] + self_swap[d].astype(F32) for d in range(depth)]
    self_more = swap_z(self_pieces, depth)
    self_sum = add_all(self_pieces[0], self_more)
    self_sp = swap_sp(self_sum, sp)
    cross_sum = add_all(cross_first, cross_got)
    ff_sp, cross_sp = swap_sp(ff_sum, sp), swap_sp(cross_sum, sp)
    ff_total = add_all(ff_sum, ff_sp)
    cross_total = add_all(cross_sum, cross_sp)
    self_total = add_all(self_sum, self_sp)
    inner_total = jnp.concatenate([ff_total[c * shard : (c + 1) * shard] for c in range(chunks)], axis=1)
    outer_total = ff_total[chunks * shard :]
    rest = cross_total[5 * shard :]
    cut = lambda total, k: total[k * shard : (k + 1) * shard]
    vec = lambda k: lax.dynamic_slice(rest, (k, mine * shard), (1, shard))[0]
    bias_total = lax.dynamic_slice(rest[8 : 8 + chunks].reshape(-1), (mine * bias_rows,), (bias_rows,))
    small = (
        cut(self_total, 0), cut(self_total, 1), cut(self_total, 2), cut(cross_total, 0),
        cut(cross_total, 1), cut(cross_total, 2), cut(cross_total, 3), cut(cross_total, 4),
        inner_total, bias_total, outer_total, vec(4), vec(5), vec(6), vec(0), vec(1), vec(2), vec(3),
    )
    count = len(small)
    got = together(*small, *token_swap)
    small, token_swap = got[:count], got[count:]
    shift_back = (local - far) // BLK
    for piece in token_swap:
        spec = pl.BlockSpec(
            (seqs, BLK, width), lambda i, spot: (0, i + jnp.where(spot[0] == 0, shift_back, 0), 0)
        )
        (token_grad,) = call(
            settle_kernel, (far // BLK,), 1,
            [spec, pl.BlockSpec((seqs, BLK, width), lambda i, spot: (0, i, 0))],
            [spec], [((seqs, local, width), F32)], [], 5000.0, (spot, token_grad, piece), {1: 0},
        )
    encoder_grad = enc_first
    for r in range(1, sp):
        encoder_grad = encoder_grad + enc_swap[r - 1].astype(F32)

    return (layer_out, hidden_grad, token_grad, encoder_grad, *small)


def solution(mesh):
    tokens, table, vector = P("fsdp", "sp", None), P("fsdp", None), P("fsdp")
    order = P("fsdp", None, None)
    return jax.shard_map(
        functools.partial(on_device, mesh.shape["sp"], mesh.shape["fsdp"]),
        mesh=mesh,
        in_specs=(tokens,) * 4
        + (table, order, order)
        + (table,) * 9
        + (vector, table)
        + (vector,) * 7,
        out_specs=(tokens,) * 4 + (table,) * 9 + (vector, table) + (vector,) * 7,
        check_vma=False,
    )
```
